32 devices in a mesh: stream: 2 (over x), batch: 16 (over z, y, core).
Axes of the slice: x: 2, y: 2, z: 4, core: 2. Of those that a mesh axis runs over, the one named last changes fastest.
Arguments:
- inputs: float32 [16, 2, 768, 768], P('batch', 'stream'), may hold values from -12 to 12
- text_pages: int32 [16, 768], P('batch'), may hold values from 0 to 3, as said below
- text_boxes: int32 [16, 2, 768], P('batch'), may hold values from 0 to 15
- norm_gains: float32 [2, 2, 768], P('stream'), may hold values from 0.1 to 1.9
- norm_shifts: float32 [2, 2, 768], P('stream'), may hold values from -1.8 to 1.8
- w_query: bfloat16 [2, 768, 768], P('stream'), may hold values from -0.21875 to 0.21875
- w_key: bfloat16 [2, 768, 768], P('stream'), may hold values from -0.21875 to 0.21875
- w_value: bfloat16 [2, 768, 768], P('stream'), may hold values from -0.21875 to 0.21875
- w_out: bfloat16 [2, 768, 768], P('stream'), may hold values from -1.75 to 1.75
- w_up: bfloat16 [2, 768, 3072], P('stream'), may hold values from -0.21875 to 0.21875
- up_bias: float32 [2, 3072], P('stream'), may hold values from -1.8 to 1.8
- w_down: bfloat16 [2, 3072, 768], P('stream'), may hold values from -0.109375 to 0.109375
- down_bias: float32 [2, 768], P('stream'), may hold values from -1.8 to 1.8
- box_table: float32 [2, 14, 12], P('stream'), may hold values from -4 to 4
- cotangent: float32 [16, 2, 768, 768], P('batch', 'stream'), may hold values from -6 to 6
Outputs:
- block_out: float32 [16, 2, 768, 768], P('batch', 'stream')
- grad_inputs: float32 [16, 2, 768, 768], P('batch', 'stream')
- grad_norm_gains: float32 [2, 2, 768], P('stream')
- grad_norm_shifts: float32 [2, 2, 768], P('stream')
- grad_w_query: float32 [2, 768, 768], P('stream', 'batch')
- grad_w_key: float32 [2, 768, 768], P('stream', 'batch')
- grad_w_value: float32 [2, 768, 768], P('stream', 'batch')
- grad_w_out: float32 [2, 768, 768], P('stream', 'batch')
- grad_w_up: float32 [2, 768, 3072], P('stream', 'batch')
- grad_up_bias: float32 [2, 3072], P('stream')
- grad_w_down: float32 [2, 3072, 768], P('stream', 'batch')
- grad_down_bias: float32 [2, 768], P('stream')
- grad_box_table: float32 [2, 14, 12], P('stream')
- stats: float32 [2], replicated
The draws below stay inside these ranges and needn't reach their ends.
Inputs may be any that keep to these rules, and one draw needn't show every extreme that they name: `text_pages`: each row's text slots hold pages 0, 1, ..., 2 in order, each page non-empty, followed by padding slots marked 3; a row holds 384 to 768 text tokens, and both ends occur.
All inputs are finite; a program needn't handle non-finite values.
Results may differ from the reference program's by a relative error of at most 0.012.
Values may be sent and summed in bfloat16 or wider, within the bound.
A program may use at most 320 MiB of HBM per device.

```python
import jax
import jax.numpy as jnp
from jax import lax

D = 768
HEADS = 12
FF = 3072
HEAD_DIM = 64
GRID = 16
PAGES = 3
BUCKETS = 7
SLOTS = 768
ROWS = 16


def draw_inputs(key, part):
    key = jax.random.fold_in(key, 11)
    first_key = jax.random.fold_in(key, 0)
    row_pos = jnp.arange(ROWS, dtype=jnp.float32)[:, None, None, None]
    ramp = 0.4 + 2.0 * row_pos / (ROWS - 1)
    drawn = jax.random.normal(first_key, (ROWS, 2, SLOTS, D), jnp.float32) * ramp
    return jnp.clip(drawn, -12.0, 12.0)


def draw_text_pages(key, part):
    key = jax.random.fold_in(key, 23)
    key_len, key_one, key_two = jax.random.split(key, 3)
    lengths = jax.random.randint(key_len, (ROWS,), SLOTS // 2, SLOTS + 1)
    lengths = lengths.at[0].set(SLOTS).at[1].set(SLOTS // 2)
    cut_one = lengths // 4 + jax.random.randint(key_one, (ROWS,), 0, SLOTS // 8 + 1)
    cut_two = 5 * lengths // 8 + jax.random.randint(key_two, (ROWS,), 0, SLOTS // 8 + 1)
    positions = jnp.arange(SLOTS, dtype=jnp.int32)[None, :]
    first_part = (positions >= cut_one[:, None]).astype(jnp.int32)
    second_part = (positions >= cut_two[:, None]).astype(jnp.int32)
    padding = (positions >= lengths[:, None]).astype(jnp.int32)
    return first_part + second_part + padding


def with_ends(array, stream_key, least, high):
    place = [jax.random.randint(jax.random.fold_in(stream_key, axis), (), 0, length) for axis, length in enumerate(array.shape)]
    longest = array.shape.index(max(array.shape))
    beside = place[:longest] + [(place[longest] + 1) % array.shape[longest]] + place[longest + 1:]
    return array.at[tuple(place)].set(least).at[tuple(beside)].set(high)


def levels(stream_key, extent, shards, smallest, top_value):
    level = 1.0
    for axis_at, blocks in shards:
        steps = jax.random.uniform(jax.random.fold_in(jax.random.fold_in(stream_key, 6), axis_at), (blocks,), jnp.float32, smallest / len(shards), top_value / len(shards))
        level = level * jnp.repeat(jnp.exp(steps), extent[axis_at] // blocks).reshape((-1,) + (1,) * (len(extent) - 1 - axis_at))
    return level


def noise(stream_key, shape, width, limit, cuts=(), kind=jnp.bfloat16):
    entries = jax.random.normal(stream_key, shape, jnp.float32) * width
    if len(cuts) > 0:
        entries = levels(stream_key, shape, cuts, -0.22, 0.18) * entries
    return jnp.clip(entries, min=-limit, max=limit).astype(kind)


def setup_inputs(seed: int = 0) -> dict:
    key_of = jax.random.split(jax.random.key(seed), 16)
    inputs = draw_inputs(jax.random.fold_in(key_of[15], 71), 0)
    text_pages = draw_text_pages(jax.random.fold_in(key_of[15], 71), 0)
    text_boxes = with_ends(jax.random.randint(key_of[2], (ROWS, 2, SLOTS), 0, GRID), jax.random.fold_in(key_of[2], 1), 0, GRID - 1).astype(jnp.int32)
    norm_gains = jnp.clip(1.0 + 0.18 * jax.random.normal(key_of[3], (2, 2, D), jnp.float32), 0.1, 1.9)
    norm_shifts = noise(key_of[4], (2, 2, D), 0.3, 1.8, ((0, 2),), jnp.float32)
    w_query = noise(key_of[5], (2, D, D), D ** -0.5, 0.21875, ((0, 2),))
    w_key = noise(key_of[6], (2, D, D), D ** -0.5, 0.21875, ((0, 2),))
    w_value = noise(key_of[7], (2, D, D), D ** -0.5, 0.21875, ((0, 2),))
    w_out = noise(key_of[8], (2, D, D), (D // 64) ** -0.5, 1.75, ((0, 2),))
    w_up = noise(key_of[9], (2, D, FF), D ** -0.5, 0.21875, ((0, 2),))
    up_bias = noise(key_of[10], (2, FF), 0.3, 1.8, ((0, 2),), jnp.float32)
    w_down = noise(key_of[11], (2, FF, D), FF ** -0.5, 0.109375, ((0, 2),))
    down_bias = noise(key_of[12], (2, D), 0.3, 1.8, ((0, 2),), jnp.float32)
    box_table = noise(key_of[13], (2, 2 * BUCKETS, HEADS), 1.0, 4.0, ((0, 2),), jnp.float32)
    cotangent = noise(key_of[14], (ROWS, 2, SLOTS, D), 1.0, 6.0, ((0, 16), (1, 2)), jnp.float32)
    return {"inputs": inputs, "text_pages": text_pages, "text_boxes": text_boxes, "norm_gains": norm_gains, "norm_shifts": norm_shifts, "w_query": w_query, "w_key": w_key, "w_value": w_value, "w_out": w_out, "w_up": w_up, "up_bias": up_bias, "w_down": w_down, "down_bias": down_bias, "box_table": box_table, "cotangent": cotangent}


@jax.custom_vjp
def low(v):
    return lax.optimization_barrier(v.astype(jnp.bfloat16)).astype(jnp.float32)

@jax.custom_vjp
def low_back(v):
    return v

def low_keep(v):
    return (low(v), None)

def low_pass(kept, grad):
    return (grad,)

def back_keep(v):
    return (v, None)

def back_low(kept, grad):
    return (low(grad),)
low.defvjp(low_keep, low_pass)
low_back.defvjp(back_keep, back_low)
HIGHEST_PRECISION = lax.Precision.HIGHEST

def layer_norm(values, gain_row, shift_row):
    center = values - lax.optimization_barrier(jnp.mean(values, axis=-1, keepdims=True))
    spread = lax.optimization_barrier(jnp.mean(center * center, axis=-1, keepdims=True))
    return center * lax.rsqrt(spread + 1e-05) * gain_row + shift_row

def relation_bias(rel_table, own_coord, far_coord):
    bucket_count = rel_table.shape[0]
    radius = (bucket_count - 1) // 2
    offset = jnp.clip(own_coord[:, None] - far_coord[None, :], -radius, radius) + radius
    result = jnp.zeros((rel_table.shape[1],) + offset.shape, jnp.float32)
    for bucket in range(bucket_count):
        result = result + rel_table[bucket][:, None, None] * (offset == bucket).astype(jnp.float32)[None]
    return result

def row_forward(weights, x_row, pages_row, boxes_row):
    gains, shifts, w_query, w_key, w_value, w_out, w_up, up_bias, w_down, down_bias, box_table = weights
    positions = jnp.arange(SLOTS, dtype=jnp.int32)
    cell_index = positions % (GRID * GRID)
    page_ids = (pages_row, positions // (GRID * GRID))
    coord_first = (boxes_row[0], cell_index % GRID)
    coord_second = (boxes_row[1], cell_index // GRID)
    valid = ((pages_row < PAGES).astype(jnp.float32), jnp.ones((SLOTS,), jnp.float32))
    queries, keys_all, values_all = ([], [], [])
    for side in range(2):
        normed = low(layer_norm(x_row[side], gains[side, 0], shifts[side, 0]))
        queries.append(low(low_back(jnp.dot(normed, w_query[side], precision=HIGHEST_PRECISION))))
        keys_all.append(low(low_back(jnp.dot(normed, w_key[side], precision=HIGHEST_PRECISION))))
        values_all.append(low(low_back(jnp.dot(normed, w_value[side], precision=HIGHEST_PRECISION))))
    outputs = []
    res_square = jnp.zeros((), jnp.float32)
    sub_square = jnp.zeros((), jnp.float32)
    counted = jnp.zeros((), jnp.float32)
    for side in range(2):
        other = 1 - side
        query_heads = queries[side].reshape(SLOTS, HEADS, HEAD_DIM)
        key_heads = keys_all[other].reshape(SLOTS, HEADS, HEAD_DIM)
        value_heads = values_all[other].reshape(SLOTS, HEADS, HEAD_DIM)
        raw = jnp.einsum('ihd,jhd->hij', query_heads, key_heads, precision=HIGHEST_PRECISION) * HEAD_DIM ** (-0.5)
        raw = raw + relation_bias(box_table[side, :BUCKETS], coord_first[side], coord_first[other])
        raw = raw + relation_bias(box_table[side, BUCKETS:], coord_second[side], coord_second[other])
        scores = low_back(raw)
        allowed = (page_ids[side][:, None] == page_ids[other][None, :]) | (page_ids[side][:, None] == PAGES)
        masked = jnp.where(allowed[None], scores, -1e+30)
        top_score = lax.optimization_barrier(jnp.max(masked, axis=-1, keepdims=True))
        exp_scores = jnp.exp(masked - top_score)
        prob_low = low(exp_scores / lax.optimization_barrier(jnp.sum(exp_scores, axis=-1, keepdims=True)))
        attended = jnp.einsum('hij,jhd->ihd', prob_low, value_heads, precision=HIGHEST_PRECISION).reshape(SLOTS, D)
        attended = low(low_back(attended * valid[side][:, None]))
        branch_one = low_back(jnp.dot(attended, w_out[side], precision=HIGHEST_PRECISION))
        middle = x_row[side] + branch_one
        normed_two = low(layer_norm(middle, gains[side, 1], shifts[side, 1]))
        pre_act = low_back(jnp.dot(normed_two, w_up[side], precision=HIGHEST_PRECISION) + up_bias[side])
        act_low = low(jax.nn.gelu(pre_act))
        branch_two = low_back(jnp.dot(act_low, w_down[side], precision=HIGHEST_PRECISION) + down_bias[side])
        block_side = middle + branch_two
        sublayer = branch_one + branch_two
        res_square = res_square + jnp.sum(valid[side] * lax.optimization_barrier(jnp.sum(block_side * block_side, axis=-1)))
        sub_square = sub_square + jnp.sum(valid[side] * lax.optimization_barrier(jnp.sum(sublayer * sublayer, axis=-1)))
        counted = counted + jnp.sum(valid[side])
        outputs.append(block_side)
    return (jnp.stack(outputs), (res_square, sub_square, counted))

def reference(inputs, text_pages, text_boxes, norm_gains, norm_shifts, w_query, w_key, w_value, w_out, w_up, up_bias, w_down, down_bias, box_table, cotangent):
    weights = tuple((item.astype(jnp.float32) for item in (norm_gains, norm_shifts, w_query, w_key, w_value, w_out, w_up, up_bias, w_down, down_bias, box_table)))

    def forward(block_in, params):

        def one_row(row_items):
            return row_forward(params, row_items[0], row_items[1], row_items[2])
        return lax.map(jax.checkpoint(one_row), (block_in, text_pages, text_boxes))
    block_out, pullback, sums = jax.vjp(forward, inputs.astype(jnp.float32), weights, has_aux=True)
    grad_inputs, grad_params = pullback(cotangent.astype(jnp.float32))
    denominator = jnp.sum(sums[2]) * D
    stats = jnp.stack([jnp.sqrt(jnp.sum(sums[0]) / denominator), jnp.sqrt(jnp.sum(sums[1]) / denominator)])
    return (block_out, grad_inputs, grad_params[0], grad_params[1], grad_params[2], grad_params[3], grad_params[4], grad_params[5], grad_params[6], grad_params[7], grad_params[8], grad_params[9], grad_params[10], stats)
```

```python
import jax
import jax.numpy as jnp
from jax import lax
from jax.experimental import pallas as pl
from jax.experimental.pallas import tpu as pltpu
from jax.sharding import PartitionSpec as P

GRID = 16
PAGES = 3


masked_fill = -1e30


def partner(block, axis, bit):
    count = lax.axis_size(axis)
    route = []
    for low in range(count):
        high = low | 1 << bit
        if high != low and high < count:
            route += [(low, high), (high, low)]
    return lax.ppermute(block, axis, route)


def norm_forward(values, gain_row, shift_row):
    center = values - jnp.mean(values, axis=-1, keepdims=True)
    inverse = lax.rsqrt(jnp.mean(center * center, axis=-1, keepdims=True) + 1e-05)
    normal_part = center * inverse
    return (normal_part * gain_row + shift_row, normal_part, inverse)


def norm_backward(grad_normed, normal_part, inverse, gain_row):
    scaled = grad_normed * gain_row
    first_mean = jnp.mean(scaled, axis=-1, keepdims=True)
    second_mean = jnp.mean(scaled * normal_part, axis=-1, keepdims=True)
    return inverse * (scaled - first_mean - normal_part * second_mean)


def bucket_offset(own_coord, far_coord, bucket_count):
    radius = (bucket_count - 1) // 2
    return jnp.clip(own_coord[:, None] - far_coord[None, :], -radius, radius) + radius


def bias_from(rel_table, offset):
    result = jnp.zeros((rel_table.shape[1],) + offset.shape, jnp.float32)
    for bucket in range(rel_table.shape[0]):
        result = (
            result + rel_table[bucket][:, None, None] * (offset == bucket).astype(jnp.float32)[None]
        )
    return result


def bias_grad(grad_wide, offset, bucket_count):
    return jnp.stack(
        [
            jnp.sum(grad_wide * (offset == bucket).astype(jnp.float32)[None], axis=(1, 2))
            for bucket in range(bucket_count)
        ]
    )


def project(left, right):
    return jnp.einsum("rsd,de->rse", left, right, preferred_element_type=jnp.float32)


def weight_grad(left, right):
    return jnp.einsum("rsd,rse->de", left, right, preferred_element_type=jnp.float32)


def back_project(grad_low, weight):
    return jnp.einsum("rse,de->rsd", grad_low, weight, preferred_element_type=jnp.float32)


MESH = pl.DeviceIdType.MESH


def scatter_kernel(gd, gr, od, orr, cd, cr, yd, yr, zd, zr, ld, lr, csem, crem, ysem, yrem, zsem, zrem, lsem):
    st = lax.axis_index("stream")
    me = lax.axis_index("batch")
    c = lax.rem(me, 2)
    y = lax.rem(lax.div(me, 2), 2)
    z = lax.div(me, 4)
    core_peer = me + 1 - 2 * c
    y_peer = me + 2 - 4 * y
    z_peers = [lax.rem(z + k, 4) * 4 + y * 2 + c for k in (1, 2, 3)]
    barrier = pltpu.get_barrier_semaphore()
    for peer in [core_peer, y_peer] + z_peers:
        pl.semaphore_signal(barrier, inc=1, device_id=(st, peer), device_id_type=MESH)
    pl.semaphore_wait(barrier, 5)
    wide, low = jnp.float32, jnp.bfloat16

    def remote(source, target, send, recv, peer):
        return pltpu.make_async_remote_copy(
            source, target, send, recv, device_id=(st, peer), device_id_type=MESH
        )

    def chunk(p):
        return lax.rem(z + p + 1, 4)

    def core_copy(p):
        if p < 4:
            return remote(gd.at[chunk(p), :, 1 - c], cd.at[p], csem.at[p], crem.at[p], core_peer)
        return remote(gr.at[p - 4, :, :, 1 - c], cr.at[p - 4], csem.at[p], crem.at[p], core_peer)

    def own_copy(p):
        if p < 4:
            return pltpu.make_async_copy(gd.at[chunk(p), :, c], ld.at[p], lsem.at[p])
        return pltpu.make_async_copy(gr.at[p - 4, :, :, c], lr.at[p - 4], lsem.at[p])

    def y_copy(p):
        if p < 4:
            return remote(cd.at[p, 1 - y], yd.at[p], ysem.at[p], yrem.at[p], y_peer)
        return remote(cr.at[p - 4, :, 1 - y], yr.at[p - 4], ysem.at[p], yrem.at[p], y_peer)

    def z_copy(p, k):
        if p < 4:
            return remote(yd.at[p], zd.at[p], zsem.at[p, 0], zrem.at[0, p], z_peers[p])
        zz = lax.rem(z + k, 4)
        return remote(
            yr.at[p - 4, zz], zr.at[p - 4, k - 1], zsem.at[p, k], zrem.at[p - 3, k - 1], z_peers[k - 1]
        )

    order = (0, 4, 1, 5, 2, 6, 3, 7, 8, 9, 10, 11)
    for p in order:
        core_copy(p).start()
        own_copy(p).start()

    def after_core(p):
        own_copy(p).wait()
        core_copy(p).wait()
        if p < 4:
            cd[p] = (cd[p].astype(wide) + ld[p].astype(wide)).astype(low)
        else:
            cr[p - 4] = (cr[p - 4].astype(wide) + lr[p - 4].astype(wide)).astype(low)
        y_copy(p).start()

    def after_y(p):
        y_copy(p).wait()
        if p < 4:
            yd[p] = (yd[p].astype(wide) + cd[p, y].astype(wide)).astype(low)
            if p < 3:
                z_copy(p, 0).start()
        else:
            yr[p - 4] = (yr[p - 4].astype(wide) + cr[p - 4, :, y].astype(wide)).astype(low)
            for k in (1, 2, 3):
                z_copy(p, k).start()

    count = len(order)
    for i in range(count + 2):
        if i < count:
            after_core(order[i])
        if i >= 2:
            after_y(order[i - 2])
    total = yd[3].astype(wide)
    for p in (0, 1, 2):
        z_copy(p, 0).wait()
        total = total + zd[p].astype(wide)
    od[...] = total
    for p in order:
        if p >= 4:
            total = yr[p - 4, z].astype(wide)
            for k in (1, 2, 3):
                z_copy(p, k).wait()
                total = total + zr[p - 4, k - 1].astype(wide)
            orr[p - 4] = total


def scatter_sums(grads, count):
    low = jnp.bfloat16
    w_q, w_k, w_v, w_o, w_u, w_d = [item.astype(low) for item in grads]
    depth = w_q.shape[0]
    if count != 16 or depth % (16 * 16) or w_u.shape[1] != 4 * depth:
        return [
            lax.psum_scatter(item, "batch", scatter_dimension=0, tiled=True) for item in grads
        ]
    rows = depth // 16
    gd = w_d.reshape(4, 2, 2, 4 * rows, depth)
    pieces = [w_u[:, i * depth : (i + 1) * depth] for i in range(4)] + [w_o, w_k, w_v, w_q]
    gr = jnp.stack(pieces).reshape(8, 4, 2, 2, rows, depth)
    hbm = pl.BlockSpec(memory_space=pl.ANY)
    vmem = pl.BlockSpec(memory_space=pltpu.VMEM)
    dma = pltpu.SemaphoreType.DMA
    down, rest = pl.pallas_call(
        scatter_kernel,
        out_shape=[
            jax.ShapeDtypeStruct((4 * rows, depth), jnp.float32),
            jax.ShapeDtypeStruct((8, rows, depth), jnp.float32),
        ],
        in_specs=[hbm, hbm],
        out_specs=[vmem, vmem],
        scratch_shapes=[
            pltpu.VMEM((4, 2, 4 * rows, depth), low),
            pltpu.VMEM((8, 4, 2, rows, depth), low),
            pltpu.VMEM((4, 4 * rows, depth), low),
            pltpu.VMEM((8, 4, rows, depth), low),
            pltpu.VMEM((3, 4 * rows, depth), low),
            pltpu.VMEM((8, 3, rows, depth), low),
            pltpu.VMEM((4, 2, 4 * rows, depth), low),
            pltpu.VMEM((8, 4, 2, rows, depth), low),
            dma((12,)),
            dma((12,)),
            dma((12,)),
            dma((12,)),
            dma((12, 4)),
            dma((9, 3)),
            dma((12,)),
        ],
        compiler_params=pltpu.CompilerParams(
            collective_id=0, has_side_effects=True, vmem_limit_bytes=56 * 2**20
        ),
        name="weight_sums",
    )(gd, gr)
    up = jnp.concatenate([rest[0], rest[1], rest[2], rest[3]], axis=1)
    return [rest[7], rest[5], rest[6], rest[4], up, down]


def on_device(
    inputs,
    text_pages,
    text_boxes,
    norm_gains,
    norm_shifts,
    w_query,
    w_key,
    w_value,
    w_out,
    w_up,
    up_bias,
    w_down,
    down_bias,
    box_table,
    cotangent,
):
    slot_count = inputs.shape[2]
    model_width = inputs.shape[3]
    head_count = box_table.shape[2]
    head_size = model_width // head_count
    bucket_count = box_table.shape[1] // 2
    score_scale = head_size ** (-0.5)
    is_text = lax.axis_index("stream") == 0
    positions = jnp.arange(slot_count, dtype=jnp.int32)
    cell_index = positions % (GRID * GRID)
    vision_page = positions // (GRID * GRID)
    vision_first = cell_index % GRID
    vision_second = cell_index // GRID
    own_valid = jnp.where(is_text, text_pages < PAGES, True).astype(jnp.float32)
    gain_rows = norm_gains[0]
    shift_rows = norm_shifts[0]
    rel_table = box_table[0]
    block_in = inputs[:, 0]
    normed_one, plain_one, inverse_one = norm_forward(block_in, gain_rows[0], shift_rows[0])
    normed_low = normed_one.astype(jnp.bfloat16)
    query = project(normed_low, w_query[0]).astype(jnp.bfloat16)
    own_keys = project(normed_low, w_key[0]).astype(jnp.bfloat16)
    own_values = project(normed_low, w_value[0]).astype(jnp.bfloat16)
    far_keys, far_values = partner((own_keys, own_values), "stream", 0)

    def geometry(row_index):
        text_page = text_pages[row_index]
        own_page = jnp.where(is_text, text_page, vision_page)
        far_page = jnp.where(is_text, vision_page, text_page)
        own_first = jnp.where(is_text, text_boxes[row_index, 0], vision_first)
        far_first = jnp.where(is_text, vision_first, text_boxes[row_index, 0])
        own_second = jnp.where(is_text, text_boxes[row_index, 1], vision_second)
        far_second = jnp.where(is_text, vision_second, text_boxes[row_index, 1])
        allowed = (own_page[:, None] == far_page[None, :]) | (own_page[:, None] == PAGES)
        return (
            allowed,
            bucket_offset(own_first, far_first, bucket_count),
            bucket_offset(own_second, far_second, bucket_count),
        )

    def heads_of(matrix):
        return matrix.reshape(slot_count, head_count, head_size)

    def score_block(row_index, allowed, offset_first, offset_second):
        raw = (
            jnp.einsum(
                "ihd,jhd->hij",
                heads_of(query[row_index]),
                heads_of(far_keys[row_index]),
                preferred_element_type=jnp.float32,
            )
            * score_scale
        )
        raw = (
            raw
            + bias_from(rel_table[:bucket_count], offset_first)
            + bias_from(rel_table[bucket_count:], offset_second)
        )
        return jnp.where(allowed[None], raw, masked_fill)

    row_index = 0
    allowed, offset_first, offset_second = geometry(row_index)
    masked = score_block(row_index, allowed, offset_first, offset_second)
    top_score = jnp.max(masked, axis=-1, keepdims=True)
    exp_scores = jnp.exp(masked - top_score)
    row_total = jnp.sum(exp_scores, axis=-1, keepdims=True)
    prob_low = (exp_scores / row_total).astype(jnp.bfloat16)
    attended = jnp.einsum(
        "hij,jhd->ihd",
        prob_low,
        heads_of(far_values[row_index]),
        preferred_element_type=jnp.float32,
    ).reshape(slot_count, model_width)
    attended_rows = [(attended * own_valid[row_index][:, None]).astype(jnp.bfloat16)]
    log_totals = [top_score + jnp.log(row_total)]
    attended_low = jnp.stack(attended_rows)
    branch_one = project(attended_low, w_out[0])
    middle = block_in + branch_one
    normed_two, plain_two, inverse_two = norm_forward(middle, gain_rows[1], shift_rows[1])
    normed_two_low = normed_two.astype(jnp.bfloat16)
    pre_act = project(normed_two_low, w_up[0]) + up_bias[0]
    act_low = jax.nn.gelu(pre_act).astype(jnp.bfloat16)
    branch_two = project(act_low, w_down[0]) + down_bias[0]
    block_out = middle + branch_two
    sublayer = branch_one + branch_two
    totals = lax.psum(
        (
            jnp.sum(own_valid * jnp.sum(block_out * block_out, axis=-1)),
            jnp.sum(own_valid * jnp.sum(sublayer * sublayer, axis=-1)),
            jnp.sum(own_valid),
        ),
        ("stream", "batch"),
    )
    denominator = totals[2] * model_width
    stats = jnp.stack([jnp.sqrt(totals[0] / denominator), jnp.sqrt(totals[1] / denominator)])
    grad_out = cotangent[:, 0]
    grad_out_low = grad_out.astype(jnp.bfloat16)
    grad_w_down = weight_grad(act_low, grad_out_low)
    grad_down_bias = jnp.sum(grad_out_low.astype(jnp.float32), axis=(0, 1))
    grad_act = back_project(grad_out_low, w_down[0])
    gelu_back = jax.vjp(jax.nn.gelu, pre_act)[1]
    grad_pre_low = gelu_back(grad_act)[0].astype(jnp.bfloat16)
    grad_w_up = weight_grad(normed_two_low, grad_pre_low)
    grad_up_bias = jnp.sum(grad_pre_low.astype(jnp.float32), axis=(0, 1))
    grad_normed_two = back_project(grad_pre_low, w_up[0])
    grad_gain_two = jnp.sum(grad_normed_two * plain_two, axis=(0, 1))
    grad_shift_two = jnp.sum(grad_normed_two, axis=(0, 1))
    grad_middle = grad_out + norm_backward(grad_normed_two, plain_two, inverse_two, gain_rows[1])
    grad_middle_low = grad_middle.astype(jnp.bfloat16)
    grad_w_out = weight_grad(attended_low, grad_middle_low)
    grad_attended = back_project(grad_middle_low, w_out[0]).astype(jnp.bfloat16) * own_valid[
        :, :, None
    ].astype(jnp.bfloat16)
    query_grad_rows, key_grad_rows, value_grad_rows = ([], [], [])
    row_index = 0
    allowed, offset_first, offset_second = geometry(row_index)
    masked = score_block(row_index, allowed, offset_first, offset_second)
    prob = jnp.exp(masked - log_totals[row_index])
    grad_heads = heads_of(grad_attended[row_index])
    grad_prob = jnp.einsum(
        "ihd,jhd->hij",
        grad_heads,
        heads_of(far_values[row_index]),
        preferred_element_type=jnp.float32,
    )
    inner_sum = jnp.sum(prob * grad_prob, axis=-1, keepdims=True)
    grad_score_low = (prob * (grad_prob - inner_sum)).astype(jnp.bfloat16)
    grad_score_wide = grad_score_low.astype(jnp.float32)
    grad_table = jnp.concatenate(
        [
            bias_grad(grad_score_wide, offset_first, bucket_count),
            bias_grad(grad_score_wide, offset_second, bucket_count),
        ],
        axis=0,
    )
    query_grad = (
        jnp.einsum(
            "hij,jhd->ihd",
            grad_score_low,
            heads_of(far_keys[row_index]),
            preferred_element_type=jnp.float32,
        )
        * score_scale
    )
    key_grad = (
        jnp.einsum(
            "hij,ihd->jhd",
            grad_score_low,
            heads_of(query[row_index]),
            preferred_element_type=jnp.float32,
        )
        * score_scale
    )
    value_grad = jnp.einsum(
        "hij,ihd->jhd", prob.astype(jnp.bfloat16), grad_heads, preferred_element_type=jnp.float32
    )
    query_grad_rows.append(query_grad.reshape(slot_count, model_width).astype(jnp.bfloat16))
    key_grad_rows.append(key_grad.reshape(slot_count, model_width).astype(jnp.bfloat16))
    value_grad_rows.append(value_grad.reshape(slot_count, model_width).astype(jnp.bfloat16))
    grad_query_low = jnp.stack(query_grad_rows)
    own_key_grad, own_value_grad = partner(
        (jnp.stack(key_grad_rows), jnp.stack(value_grad_rows)), "stream", 0
    )
    grad_w_query = weight_grad(normed_low, grad_query_low)
    grad_w_key = weight_grad(normed_low, own_key_grad)
    grad_w_value = weight_grad(normed_low, own_value_grad)
    grad_normed_one = (
        back_project(grad_query_low, w_query[0])
        + back_project(own_key_grad, w_key[0])
        + back_project(own_value_grad, w_value[0])
    )
    grad_gain_one = jnp.sum(grad_normed_one * plain_one, axis=(0, 1))
    grad_shift_one = jnp.sum(grad_normed_one, axis=(0, 1))
    grad_inputs = grad_middle + norm_backward(grad_normed_one, plain_one, inverse_one, gain_rows[0])
    big_sums = scatter_sums(
        (grad_w_query, grad_w_key, grad_w_value, grad_w_out, grad_w_up, grad_w_down),
        lax.axis_size("batch"),
    )
    small_sums = lax.psum(
        (
            jnp.stack([grad_gain_one, grad_gain_two]),
            jnp.stack([grad_shift_one, grad_shift_two]),
            grad_up_bias,
            grad_down_bias,
            grad_table,
        ),
        "batch",
    )
    return (
        block_out[:, None],
        grad_inputs[:, None],
        small_sums[0][None],
        small_sums[1][None],
        big_sums[0][None],
        big_sums[1][None],
        big_sums[2][None],
        big_sums[3][None],
        big_sums[4][None],
        small_sums[2][None],
        big_sums[5][None],
        small_sums[3][None],
        small_sums[4][None],
        stats,
    )


def solution(mesh):
    placed = (
        P("batch", "stream", None, None),
        P("batch", None),
        P("batch", None, None),
        P("stream", None, None),
        P("stream", None, None),
        P("stream", None, None),
        P("stream", None, None),
        P("stream", None, None),
        P("stream", None, None),
        P("stream", None, None),
        P("stream", None),
        P("stream", None, None),
        P("stream", None),
        P("stream", None, None),
        P("batch", "stream", None, None),
    )
    return jax.shard_map(
        on_device,
        mesh=mesh,
        in_specs=placed,
        out_specs=(
            P("batch", "stream", None, None),
            P("batch", "stream", None, None),
            P("stream", None, None),
            P("stream", None, None),
            P("stream", "batch", None),
            P("stream", "batch", None),
            P("stream", "batch", None),
            P("stream", "batch", None),
            P("stream", "batch", None),
            P("stream", None),
            P("stream", "batch", None),
            P("stream", None),
            P("stream", None, None),
            P(),
        ),
        check_vma=False,
    )
```

```python
import functools

import jax
import jax.numpy as jnp
from jax import lax
from jax.experimental import pallas as pl
from jax.experimental.pallas import tpu as pltpu
from jax.sharding import PartitionSpec as P

GRID = 16
PAGES = 3
MESH = pl.DeviceIdType.MESH
LOG2E = 1.4426950408889634
LN2 = 0.6931471805599453
GELU_IN = 0.7978845608028654
GELU_CUBE = 0.044715
masked_fill = -1e30
f32 = jnp.float32
bf16 = jnp.bfloat16


def dot(left, right, form="nn"):
    dims = {"nn": (1, 0), "nt": (1, 1), "tn": (0, 0)}[form]
    return lax.dot_general(
        left, right, (((dims[0],), (dims[1],)), ((), ())), preferred_element_type=f32
    )


def plain_norm(values):
    center = values - jnp.mean(values, axis=-1, keepdims=True)
    inverse = lax.rsqrt(jnp.mean(center * center, axis=-1, keepdims=True) + 1e-05)
    return center * inverse, inverse


def norm_backward(grad_normed, plain, inverse, gain_row):
    scaled = grad_normed * gain_row
    first_mean = jnp.mean(scaled, axis=-1, keepdims=True)
    second_mean = jnp.mean(scaled * plain, axis=-1, keepdims=True)
    return inverse * (scaled - first_mean - plain * second_mean)


def head_rows(first, half, width):
    empty = jnp.zeros((half.shape[0], width), half.dtype)
    return [half, empty] if first else [empty, half]


def attend_kernel(
    normed, far, wq, wk, wv, feat, bias, valid_row, q_o, k_o, v_o, att_o, lse_o, q_t, v_t, att_t
):
    width = normed.shape[1]
    slots = normed.shape[0]
    heads = bias.shape[0]
    size = width // heads
    q_o[...] = (dot(normed[...], wq[...]) * (LOG2E * size**-0.5)).astype(bf16)
    q_t[...] = q_o[...].T
    k_o[...] = dot(far[...], wk[...]).astype(bf16)
    v_o[...] = dot(far[...], wv[...]).astype(bf16)
    v_t[...] = v_o[...].T
    ones = jnp.ones((16, slots), bf16)
    pad = jnp.zeros((2 * size - bias.shape[1], slots), bf16)

    def pair(p, carry):
        start = pl.multiple_of(p * 2 * size, 2 * size)
        left = jnp.concatenate([k_o[:, pl.ds(start, 2 * size)], feat[...]], axis=1)
        for hh in range(2):
            rows = pl.ds(pl.multiple_of(start + hh * size, size), size)
            right = jnp.concatenate(
                head_rows(hh == 0, q_t[rows, :], slots) + [bias[2 * p + hh], pad], axis=0
            )
            scores = dot(left, right)
            top = jnp.max(scores, axis=0, keepdims=True)
            weight = jnp.exp2(scores - top).astype(bf16)
            found = dot(jnp.concatenate([v_t[rows, :], ones], axis=0), weight)
            total = found[size : size + 1]
            att_t[rows, :] = (found[:size] * (valid_row[...] / total)).astype(bf16)
            lse_o[2 * p + hh] = top + jnp.log2(total)
        return carry

    lax.fori_loop(0, heads // 2, pair, 0)
    att_o[...] = att_t[...].T


SLOT = {
    name: i
    for i, name in enumerate(
        ("att", "wo", "n2", "n2t", "g2", "wu0", "wu1", "wd0", "wd1", "sd0", "sd1", "sr0", "sr1", "q", "k", "v", "back")
    )
}
SLOT.update(act=13, gp=14, gm=2, go=3, got=4, far=5, q_t=6, k_t=7, dk=8, so=9, send=10, dv=11)
SLOT.update(normed=0, wq=1, wv=2, wk=12, dq=13, sk=6, sv=7, sq=3, dq_t=8)


def layer_kernel(
    x, cot, att, q, k, v, normed, far, wq, wk, wv, wo, wup, wdn,
    lse, up_bias, down_bias, gains, shifts, valid_col, valid_row, feat, feat_t, bias, offsets,
    block_o, grad_o, down_o, up_o, wo_o, wq_o, wk_o, wv_o, gains_o, shifts_o, down_bias_o, up_bias_o, table_o,
    pool, wide, delta, cells, cd, cr, yd, yr, zd, zr, hop, hop_in, sums, sums_in, table_in,
    in_sem, w_sem, out_sem, csem, crem, ysem, yrem, zsem, zrem, xsem, xrem, hsem, hrem, asem, arem, bsem, brem,
):
    slots, width = x.shape
    heads = bias.shape[0]
    size = width // heads
    st = lax.axis_index("stream")
    me = lax.axis_index("batch")
    c = lax.rem(me, 2)
    y = lax.rem(lax.div(me, 2), 2)
    z = lax.div(me, 4)
    core_peer = (st, me + 1 - 2 * c)
    y_peer = (st, me + 2 - 4 * y)
    z_at = [lax.rem(z + i, 4) for i in range(4)]
    z_peers = [(st, z_at[i] * 4 + y * 2 + c) for i in range(4)]
    x_peer = (1 - st, me)
    one_peer = (st, me + 4 - 8 * lax.rem(z, 2))
    two_peer = (st, me + 8 - 16 * lax.div(z, 2))

    def slot(name):
        return pool.at[SLOT[name]]

    def remote(source, target, send, recv, peer):
        return pltpu.make_async_remote_copy(
            source, target, send, recv, device_id=peer, device_id_type=MESH
        )

    singles = dict(
        x=(x, wide.at[0]), cot=(cot, wide.at[1]), att=(att, slot("att")), wo=(wo, slot("wo")),
        q=(q, slot("q")), k=(k, slot("k")), v=(v, slot("v")), wk=(wk, slot("wk")), wv=(wv, slot("wv")),
        far=(far, slot("far")), normed=(normed, slot("normed")), wq=(wq, slot("wq")),
    )
    load_at = {name: i for i, name in enumerate(singles)}

    def load(name):
        return pltpu.make_async_copy(*singles[name], in_sem.at[load_at[name]])

    def chunk_of(t):
        return lax.rem(z + t + 1, 4)

    def chunk_loads(t):
        at = pl.multiple_of(chunk_of(t) * width, width)
        two = lax.rem(t, 2)
        return (
            pltpu.make_async_copy(
                wup.at[:, pl.ds(at, width)], pool.at[SLOT["wu0"] + two], w_sem.at[two, 0]
            ),
            pltpu.make_async_copy(
                wdn.at[pl.ds(at, width), :], pool.at[SLOT["wd0"] + two], w_sem.at[two, 1]
            ),
        )

    for name in ("att", "wo", "x", "cot"):
        load(name).start()
    for copy in chunk_loads(0):
        copy.start()

    barrier = pltpu.get_barrier_semaphore()
    peers = [core_peer, y_peer, x_peer] + z_peers[1:]
    for peer in peers:
        pl.semaphore_signal(barrier, inc=1, device_id=peer, device_id_type=MESH)
    pl.semaphore_wait(barrier, len(peers))

    def down_view(at):
        return pool.at[at].reshape(2, 2, width // 4, width)

    def rest_view(at):
        return pool.at[at].reshape(4, 2, 2, width // 16, width)

    def core_down(t):
        at = SLOT["sd0"] + lax.rem(t, 2)
        return remote(down_view(at).at[:, 1 - c], cd.at[t], csem.at[t], crem.at[t], core_peer)

    def core_rest(p, at):
        return remote(
            rest_view(at).at[:, :, 1 - c], cr.at[p], csem.at[4 + p], crem.at[4 + p], core_peer
        )

    def y_down(t):
        return remote(cd.at[t, 1 - y], yd.at[t], ysem.at[t], yrem.at[t], y_peer)

    def y_rest(p):
        return remote(cr.at[p, :, 1 - y], yr.at[p], ysem.at[4 + p], yrem.at[4 + p], y_peer)

    def z_down(t):
        return remote(yd.at[t], zd.at[t], zsem.at[0, t], zrem.at[0, t], z_peers[t + 1])

    def z_rest(p, i):
        q = chunk_of(p) if p < 4 else p
        return remote(
            yr.at[p, z_at[i]], zr.at[q, i - 1], zsem.at[1 + p, i - 1], zrem.at[1 + q, i - 1], z_peers[i]
        )

    def z_here(q, i):
        return remote(
            yr.at[q, z_at[i]], zr.at[q, i - 1], zsem.at[1 + q, i - 1], zrem.at[1 + q, i - 1], z_peers[i]
        )

    def add_low(left, right):
        return (left.astype(f32) + right.astype(f32)).astype(bf16)

    def after_core_down(t):
        core_down(t).wait()
        cd[t] = add_low(cd[t], down_view(SLOT["sd0"] + lax.rem(t, 2))[:, c])
        y_down(t).start()

    def after_core_rest(p, at):
        core_rest(p, at).wait()
        cr[p] = add_low(cr[p], rest_view(at)[:, :, c])
        y_rest(p).start()

    def after_y_down(t):
        y_down(t).wait()
        yd[t] = add_low(yd[t], cd[t, y])
        if t < 3:
            z_down(t).start()

    def after_y_rest(p):
        y_rest(p).wait()
        yr[p] = add_low(yr[p], cr[p, :, y])
        for i in (1, 2, 3):
            z_rest(p, i).start()

    def end_down():
        total = yd[3].astype(f32)
        for t in range(3):
            z_down(t).wait()
            total = total + zd[t].astype(f32)
        down_o[...] = total

    def end_rest(q):
        held = lax.rem(q - z + 3, 4) if q < 4 else q
        total = yr[held, z].astype(f32)
        for i in (1, 2, 3):
            z_here(q, i).wait()
            total = total + zr[q, i - 1].astype(f32)
        return total

    load("att").wait()
    load("wo").wait()
    load("x").wait()
    load("cot").wait()
    sums[...] = jnp.zeros_like(sums)
    third = slots // 3
    spans = [pl.ds(part * third, third) for part in range(3)]
    for span in spans:
        middle = wide[0, span, :] + dot(pool[SLOT["att"], span, :], pool[SLOT["wo"]])
        wide[2, span, :] = middle
        wide[3, span, :] = middle + down_bias[...]
        plain, inverse = plain_norm(middle)
        pool[SLOT["n2"], span, :] = (plain * gains[1:2, :] + shifts[1:2, :]).astype(bf16)
        low = wide[1, span, :].astype(bf16)
        pool[SLOT["g2"], span, :] = low
        sums[4:5, :] += jnp.sum(low.astype(f32), axis=0, keepdims=True)
    pool[SLOT["n2t"]] = pool[SLOT["n2"]].T
    wide[4] = jnp.zeros((slots, width), f32)

    def feed(t, carry):
        two = lax.rem(t, 2)
        at = chunk_of(t)
        for copy in chunk_loads(t):
            copy.wait()

        @pl.when(t < 3)
        def _():
            for copy in chunk_loads(t + 1):
                copy.start()

        w_u = pool.at[SLOT["wu0"] + two]
        w_d = pool.at[SLOT["wd0"] + two]
        for part in range(3):
            cols = slice(part * third, (part + 1) * third)
            pre = dot(pool[SLOT["n2"]], w_u[:, cols]) + up_bias[at, :, cols]
            grad_act = dot(pool[SLOT["g2"]], w_d[cols, :], "nt")
            square = pre * pre
            gate = jnp.tanh(pre * (GELU_IN + (GELU_IN * GELU_CUBE) * square))
            gate_half = 0.5 + 0.5 * gate
            pool[SLOT["act"], :, cols] = (pre * gate_half).astype(bf16)
            slope = pre * (GELU_IN + (3.0 * GELU_IN * GELU_CUBE) * square)
            grad_pre = (grad_act * (gate_half * (1.0 + (1.0 - gate) * slope))).astype(bf16)
            pool[SLOT["gp"], :, cols] = grad_pre
            sums[pl.ds(5 + at, 1), cols] = jnp.sum(grad_pre.astype(f32), axis=0, keepdims=True)
        pool[SLOT["sd0"] + two] = dot(pool[SLOT["act"]], pool[SLOT["g2"]], "tn").astype(bf16)
        core_down(t).start()

        @pl.when(t > 0)
        def _():
            after_core_rest(t - 1, SLOT["sr0"] + 1 - two)

        pool[SLOT["sr0"] + two] = dot(pool[SLOT["n2t"]], pool[SLOT["gp"]]).astype(bf16)
        core_rest(t, SLOT["sr0"] + two).start()
        wide[3] = wide[3] + dot(pool[SLOT["act"]], w_d[...])
        after_core_down(t)
        wide[4] = wide[4] + dot(pool[SLOT["gp"]], w_u[...], "nt")
        return carry

    lax.fori_loop(0, 4, feed, 0)
    after_core_rest(3, SLOT["sr1"])
    for name in ("far", "q", "k", "v"):
        load(name).start()

    pltpu.make_async_copy(wide.at[3], block_o, out_sem.at[0]).start()
    cells[168:176, :] = jnp.zeros((8, width), f32)
    cells[170:171, :] = valid_row[...]
    for span in spans:
        block = wide[3, span, :]
        own = valid_col[span, :]
        sub = block - wide[0, span, :]
        cells[168:169, :] += jnp.sum(own * block * block, axis=0, keepdims=True)
        cells[169:170, :] += jnp.sum(own * sub * sub, axis=0, keepdims=True)
        plain, inverse = plain_norm(wide[2, span, :])
        grad_two = wide[4, span, :]
        sums[1:2, :] += jnp.sum(grad_two * plain, axis=0, keepdims=True)
        sums[3:4, :] += jnp.sum(grad_two, axis=0, keepdims=True)
        middle = wide[1, span, :] + norm_backward(grad_two, plain, inverse, gains[1:2, :])
        wide[2, span, :] = middle
        pool[SLOT["gm"], span, :] = middle.astype(bf16)
    pool[SLOT["so"]] = dot(pool[SLOT["att"]], pool[SLOT["gm"]], "tn").astype(bf16)
    core_rest(4, SLOT["so"]).start()
    own = valid_col[...].astype(bf16)
    pool[SLOT["go"]] = dot(pool[SLOT["gm"]], pool[SLOT["wo"]], "nt").astype(bf16) * own
    pool[SLOT["got"]] = pool[SLOT["go"]].T
    pool[SLOT["q_t"]] = pool[SLOT["att"]].T
    group = 4 * size
    for i in range(heads // 4):
        rows = slice(i * group, (i + 1) * group)
        both = pool[SLOT["q_t"], rows, :].astype(f32) * pool[SLOT["got"], rows, :].astype(f32)
        delta[4 * i : 4 * i + 4] = jnp.sum(both.reshape(4, size, slots), axis=1, keepdims=True)
    after_core_rest(4, SLOT["so"])
    after_y_down(0)
    after_y_rest(0)
    for name in ("normed", "wq", "wk", "wv"):
        load(name).start()
    pltpu.make_async_copy(wide.at[3], block_o, out_sem.at[0]).wait()

    for name in ("q", "k", "v"):
        load(name).wait()
    pool[SLOT["q_t"]] = pool[SLOT["q"]].T
    pool[SLOT["k_t"]] = pool[SLOT["k"]].T
    pad = jnp.zeros((2 * size - bias.shape[1], slots), bf16)
    stride = size + 2 * GRID
    dq_acc = wide.at[pl.ds(3, 2)].reshape(2 * slots, width)
    lane = lax.broadcasted_iota(jnp.int32, (third, 2 * size), 1)
    for part in range(3):
        span = spans[part]

        def pair(p, carry):
            start = pl.multiple_of(p * 2 * size, 2 * size)
            pair_cols = pl.ds(start, 2 * size)
            left = jnp.concatenate([pool[SLOT["k"], span, pair_cols], feat[span, :]], axis=1)
            v_pair = pool[SLOT["v"], span, pair_cols]
            go_pair = pool[SLOT["go"], :, pair_cols]
            q_pair = pool[SLOT["q"], :, pair_cols]
            grads_v, grads_k = [], []
            for hh in range(2):
                head = 2 * p + hh
                rows = pl.ds(pl.multiple_of(start + hh * size, size), size)
                right = jnp.concatenate(
                    head_rows(hh == 0, pool[SLOT["q_t"], rows, :], slots) + [bias[head], pad],
                    axis=0,
                )
                prob = jnp.exp2(dot(left, right) - lse[head])
                right = jnp.concatenate(
                    head_rows(hh == 0, pool[SLOT["got"], rows, :], slots), axis=0
                )
                grad_prob = dot(v_pair, right)
                grad_score = (prob * (grad_prob - delta[head])).astype(bf16)
                grads_v.append(dot(prob.astype(bf16), go_pair))
                grads_k.append(dot(grad_score, q_pair))
                key_rows = jnp.concatenate(
                    [pool[SLOT["k_t"], rows, span], feat_t[:, span]], axis=0
                )
                found = dot(key_rows, grad_score)
                at = pl.ds(pl.multiple_of(head * stride, 8), stride)
                if part == 0:
                    dq_acc[at, :] = found
                else:
                    dq_acc[at, :] = dq_acc[at, :] + found
            pool[SLOT["dv"], span, pair_cols] = jnp.where(lane < size, *grads_v).astype(bf16)
            pool[SLOT["dk"], span, pair_cols] = (jnp.where(lane < size, *grads_k) * LN2).astype(bf16)
            return carry

        lax.fori_loop(0, heads // 2, pair, 0)
        if part == 0:
            load("wk").wait()
            load("wv").wait()
        pool[SLOT["send"], span, :] = (
            dot(pool[SLOT["dk"], span, :], pool[SLOT["wk"]], "nt")
            + dot(pool[SLOT["dv"], span, :], pool[SLOT["wv"]], "nt")
        ).astype(bf16)
        remote(
            slot("send").at[span, :], slot("back").at[span, :], xsem.at[part], xrem.at[part], x_peer
        ).start()
        if part == 0:
            after_y_down(1)
            after_y_rest(1)
        elif part == 1:
            after_y_down(2)
            after_y_rest(2)

    load("far").wait()
    pool[SLOT["sk"]] = dot(pool[SLOT["far"]], pool[SLOT["dk"]], "tn").astype(bf16)
    core_rest(5, SLOT["sk"]).start()
    pool[SLOT["sv"]] = dot(pool[SLOT["far"]], pool[SLOT["dv"]], "tn").astype(bf16)
    core_rest(6, SLOT["sv"]).start()
    after_core_rest(5, SLOT["sk"])
    for head in range(heads):
        pool[SLOT["dq_t"], head * size : (head + 1) * size, :] = (
            dq_acc[head * stride : head * stride + size, :] * size**-0.5
        ).astype(bf16)
    pool[SLOT["dq"]] = pool[SLOT["dq_t"]].T
    load("normed").wait()
    load("wq").wait()
    pool[SLOT["sq"]] = dot(pool[SLOT["normed"]], pool[SLOT["dq"]], "tn").astype(bf16)
    core_rest(7, SLOT["sq"]).start()
    after_core_rest(6, SLOT["sv"])
    wide[1] = dot(pool[SLOT["dq"]], pool[SLOT["wq"]], "nt")
    after_core_rest(7, SLOT["sq"])
    after_y_down(3)
    after_y_rest(3)

    def table_rows(head, carry):
        at = pl.multiple_of(head * stride + size, 8)
        cell = dq_acc[pl.ds(at, 2 * GRID), :]
        for bucket in range(7):
            kept = jnp.where(offsets[...] == bucket, cell, 0.0)
            cells[pl.ds(bucket * heads + head, 1), :] = jnp.sum(kept[:GRID], axis=0, keepdims=True)
            cells[pl.ds((7 + bucket) * heads + head, 1), :] = jnp.sum(
                kept[GRID:], axis=0, keepdims=True
            )
        return carry

    lax.fori_loop(0, heads, table_rows, 0)
    table_o[...] = lax.dot_general(
        jnp.ones((8, width), f32),
        cells[...],
        (((1,), (1,)), ((), ())),
        preferred_element_type=f32,
        precision=lax.Precision.HIGHEST,
    )

    after_y_rest(4)
    for part in range(3):
        span = spans[part]
        remote(
            slot("send").at[span, :], slot("back").at[span, :], xsem.at[part], xrem.at[part], x_peer
        ).wait()
    for span in spans:
        grad_one = wide[1, span, :] + pool[SLOT["back"], span, :].astype(f32)
        plain, inverse = plain_norm(wide[0, span, :])
        sums[0:1, :] += jnp.sum(grad_one * plain, axis=0, keepdims=True)
        sums[2:3, :] += jnp.sum(grad_one, axis=0, keepdims=True)
        wide[1, span, :] = wide[2, span, :] + norm_backward(
            grad_one, plain, inverse, gains[0:1, :]
        )
    pltpu.make_async_copy(wide.at[1], grad_o, out_sem.at[1]).start()

    def small_copies(i, peer):
        return (
            remote(sums, sums_in.at[i], asem.at[i], arem.at[i], peer),
            remote(table_o, table_in.at[i], bsem.at[i], brem.at[i], peer),
        )

    def small_start(i, peer):
        for copy in small_copies(i, peer):
            copy.start()

    def small_end(i, peer):
        for copy in small_copies(i, peer):
            copy.wait()
        sums[...] = sums[...] + sums_in[i]
        table_o[...] = table_o[...] + table_in[i]

    def hop_copy(i):
        return remote(hop.at[i], hop_in.at[i], hsem.at[i], hrem.at[i], x_peer)

    small_start(0, core_peer)
    after_y_rest(5)
    small_end(0, core_peer)
    small_start(1, y_peer)
    end_down()
    for q in range(4):
        up_o[:, q * width : (q + 1) * width] = end_rest(q)
    small_end(1, y_peer)
    small_start(2, one_peer)
    wo_o[...] = end_rest(4)
    after_y_rest(6)
    small_end(2, one_peer)
    small_start(3, two_peer)
    hop[0] = end_rest(5).astype(bf16)
    hop_copy(0).start()
    small_end(3, two_peer)
    last = remote(table_o, table_in.at[4], bsem.at[4], brem.at[4], x_peer)
    last.start()
    after_y_rest(7)
    hop[1] = end_rest(6).astype(bf16)
    hop_copy(1).start()
    last.wait()
    column = lax.broadcasted_iota(jnp.int32, table_o.shape, 1)
    table_o[...] = table_o[...] + jnp.where(column >= 168, table_in[4], 0.0)
    wq_o[...] = end_rest(7)
    gains_o[...] = sums[0:2, :]
    shifts_o[...] = sums[2:4, :]
    down_bias_o[...] = sums[4:5, :]
    for q in range(4):
        up_bias_o[:, q * width : (q + 1) * width] = sums[5 + q : 6 + q, :]
    hop_copy(0).wait()
    wk_o[...] = hop_in[0].astype(f32)
    hop_copy(1).wait()
    wv_o[...] = hop_in[1].astype(f32)
    pltpu.make_async_copy(wide.at[1], grad_o, out_sem.at[1]).wait()


def features(first, second, page):
    cell = jnp.arange(GRID, dtype=jnp.int32)
    one = first[:, None] == cell[None, :]
    two = second[:, None] == cell[None, :]
    pages = page[:, None] == jnp.arange(PAGES + 1, dtype=jnp.int32)[None, :]
    hot = jnp.concatenate([one, two, one, two, pages], axis=1).astype(bf16)
    return jnp.pad(hot, ((0, 0), (0, 128 - hot.shape[1])))


def bias_rows(rel_table, first, second, page):
    buckets = rel_table.shape[0] // 2
    radius = (buckets - 1) // 2
    cell = jnp.arange(GRID, dtype=jnp.int32)[:, None]
    offsets = [
        jnp.clip(coord[None, :] - cell, -radius, radius) + radius for coord in (first, second)
    ]
    exact = []
    for part, offset in enumerate(offsets):
        total = jnp.zeros((rel_table.shape[1],) + offset.shape, f32)
        for bucket in range(buckets):
            entry = rel_table[part * buckets + bucket][:, None, None]
            total = jnp.where((offset == bucket)[None], entry, total)
        exact.append(total * LOG2E)
    exact = jnp.concatenate(exact, axis=1)
    high = lax.reduce_precision(exact, 8, 7)
    low = exact - high
    pages = jnp.arange(PAGES + 1, dtype=jnp.int32)[:, None]
    allowed = (page[None, :] == pages) | (page[None, :] == PAGES)
    mask = jnp.where(allowed, 0.0, masked_fill)
    mask = jnp.broadcast_to(mask[None], (exact.shape[0],) + mask.shape)
    rows = jnp.concatenate([high, low, mask], axis=1).astype(bf16)
    rows = jnp.pad(rows, ((0, 0), (0, -rows.shape[1] % 16), (0, 0)))
    return rows, jnp.concatenate(offsets, axis=0)


def far_weight(weight, count):
    rows = weight.shape[0] // count
    part = lax.dynamic_slice_in_dim(weight, lax.axis_index("batch") * rows, rows, 0)
    part = lax.ppermute(part, "stream", [(0, 1), (1, 0)])
    return lax.all_gather(part, "batch", axis=0, tiled=True)


def on_device(
    inputs,
    text_pages,
    text_boxes,
    norm_gains,
    norm_shifts,
    w_query,
    w_key,
    w_value,
    w_out,
    w_up,
    up_bias,
    w_down,
    down_bias,
    box_table,
    cotangent,
):
    slots, width = inputs.shape[2:]
    heads = box_table.shape[2]
    count = lax.axis_size("batch")
    x = inputs[0, 0]
    plain, _ = plain_norm(x)
    normed = (plain * norm_gains[0, 0] + norm_shifts[0, 0]).astype(bf16)
    far = lax.ppermute(normed, "stream", [(0, 1), (1, 0)])
    far_key = far_weight(w_key[0], count)
    far_value = far_weight(w_value[0], count)

    is_text = lax.axis_index("stream") == 0
    positions = jnp.arange(slots, dtype=jnp.int32)
    cell = positions % (GRID * GRID)
    text = (text_boxes[0, 0], text_boxes[0, 1], text_pages[0])
    vision = (cell % GRID, cell // GRID, positions // (GRID * GRID))
    own = [jnp.where(is_text, a, b) for a, b in zip(text, vision)]
    other = [jnp.where(is_text, b, a) for a, b in zip(text, vision)]
    valid = jnp.where(is_text, text_pages[0] < PAGES, True).astype(f32)
    feat = features(*other)
    feat_t = feat[:, : 2 * GRID].T
    bias, offsets = bias_rows(box_table[0], *own)

    matrix = jax.ShapeDtypeStruct((slots, width), bf16)
    vmem = pl.BlockSpec(memory_space=pltpu.VMEM)
    hbm = pl.BlockSpec(memory_space=pl.ANY)
    limit = 61 * 2**20
    q, k, v, att, lse = pl.pallas_call(
        attend_kernel,
        out_shape=[matrix] * 4 + [jax.ShapeDtypeStruct((heads, 1, slots), f32)],
        in_specs=[vmem] * 8,
        out_specs=[vmem] * 5,
        scratch_shapes=[pltpu.VMEM((slots, width), bf16)] * 3,
        compiler_params=pltpu.CompilerParams(vmem_limit_bytes=limit),
        name="attend",
    )(normed, far, w_query[0], far_key, far_value, feat, bias, valid[None, :])

    part = width // 16
    wide_shape = lambda *shape: jax.ShapeDtypeStruct(shape, f32)
    dma = pltpu.SemaphoreType.DMA
    outs = pl.pallas_call(
        layer_kernel,
        out_shape=[
            wide_shape(slots, width),
            wide_shape(slots, width),
            wide_shape(4 * part, width),
            wide_shape(part, 4 * width),
            wide_shape(part, width),
            wide_shape(part, width),
            wide_shape(part, width),
            wide_shape(part, width),
            wide_shape(2, width),
            wide_shape(2, width),
            wide_shape(1, width),
            wide_shape(1, 4 * width),
            wide_shape(8, 176),
        ],
        in_specs=[hbm] * 14 + [vmem] * 11,
        out_specs=[hbm] * 2 + [vmem] * 11,
        scratch_shapes=[
            pltpu.VMEM((17, slots, width), bf16),
            pltpu.VMEM((5, slots, width), f32),
            pltpu.VMEM((heads, 1, slots), f32),
            pltpu.VMEM((176, width), f32),
            pltpu.VMEM((4, 2, 4 * part, width), bf16),
            pltpu.VMEM((8, 4, 2, part, width), bf16),
            pltpu.VMEM((4, 4 * part, width), bf16),
            pltpu.VMEM((8, 4, part, width), bf16),
            pltpu.VMEM((3, 4 * part, width), bf16),
            pltpu.VMEM((8, 3, part, width), bf16),
            pltpu.VMEM((2, part, width), bf16),
            pltpu.VMEM((2, part, width), bf16),
            pltpu.VMEM((16, width), f32),
            pltpu.VMEM((4, 16, width), f32),
            pltpu.VMEM((5, 8, 176), f32),
            dma((12,)),
            dma((2, 2)),
            dma((2,)),
            dma((12,)),
            dma((12,)),
            dma((12,)),
            dma((12,)),
            dma((9, 3)),
            dma((9, 3)),
            dma((3,)),
            dma((3,)),
            dma((2,)),
            dma((2,)),
            dma((4,)),
            dma((4,)),
            dma((5,)),
            dma((5,)),
        ],
        compiler_params=pltpu.CompilerParams(
            collective_id=0, has_side_effects=True, vmem_limit_bytes=limit
        ),
        name="layer",
    )(
        x,
        cotangent[0, 0],
        att,
        q,
        k,
        v,
        normed,
        far,
        w_query[0],
        far_key,
        far_value,
        w_out[0],
        w_up[0],
        w_down[0],
        lse,
        up_bias.reshape(4, 1, width),
        down_bias,
        norm_gains[0],
        norm_shifts[0],
        valid[:, None],
        valid[None, :],
        feat,
        feat_t,
        bias,
        offsets,
    )
    block, grad_in, down, up, out, query, key, value, gains, shifts, down_b, up_b, table = outs
    grad_table = table[0, : 14 * heads].reshape(1, 14, heads)
    sums = table[0, 14 * heads : 14 * heads + 3]
    stats = jnp.sqrt(sums[:2] / (sums[2] * width))
    return (
        block[None, None],
        grad_in[None, None],
        gains[None],
        shifts[None],
        query[None],
        key[None],
        value[None],
        out[None],
        up[None],
        up_b,
        down[None],
        down_b,
        grad_table,
        stats,
    )


def partner(block, axis, bit):
    count = lax.axis_size(axis)
    route = []
    for low in range(count):
        high = low | 1 << bit
        if high != low and high < count:
            route += [(low, high), (high, low)]
    return lax.ppermute(block, axis, route)


def norm_forward(values, gain_row, shift_row):
    center = values - jnp.mean(values, axis=-1, keepdims=True)
    inverse = lax.rsqrt(jnp.mean(center * center, axis=-1, keepdims=True) + 1e-05)
    normal_part = center * inverse
    return (normal_part * gain_row + shift_row, normal_part, inverse)


def general_norm_backward(grad_normed, normal_part, inverse, gain_row):
    scaled = grad_normed * gain_row
    first_mean = jnp.mean(scaled, axis=-1, keepdims=True)
    second_mean = jnp.mean(scaled * normal_part, axis=-1, keepdims=True)
    return inverse * (scaled - first_mean - normal_part * second_mean)


def bucket_offset(own_coord, far_coord, bucket_count):
    radius = (bucket_count - 1) // 2
    return jnp.clip(own_coord[:, None] - far_coord[None, :], -radius, radius) + radius


def bias_from(rel_table, offset):
    result = jnp.zeros((rel_table.shape[1],) + offset.shape, f32)
    for bucket in range(rel_table.shape[0]):
        result = (
            result + rel_table[bucket][:, None, None] * (offset == bucket).astype(f32)[None]
        )
    return result


def bias_grad(grad_wide, offset, bucket_count):
    return jnp.stack(
        [
            jnp.sum(grad_wide * (offset == bucket).astype(f32)[None], axis=(1, 2))
            for bucket in range(bucket_count)
        ]
    )


def project(left, right):
    return jnp.einsum("rsd,de->rse", left, right, preferred_element_type=f32)


def weight_grad(left, right):
    return jnp.einsum("rsd,rse->de", left, right, preferred_element_type=f32)


def back_project(grad_low, weight):
    return jnp.einsum("rse,de->rsd", grad_low, weight, preferred_element_type=f32)


def general_device(
    inputs,
    text_pages,
    text_boxes,
    norm_gains,
    norm_shifts,
    w_query,
    w_key,
    w_value,
    w_out,
    w_up,
    up_bias,
    w_down,
    down_bias,
    box_table,
    cotangent,
):
    slot_count = inputs.shape[2]
    model_width = inputs.shape[3]
    head_count = box_table.shape[2]
    head_size = model_width // head_count
    bucket_count = box_table.shape[1] // 2
    score_scale = head_size ** (-0.5)
    is_text = lax.axis_index("stream") == 0
    positions = jnp.arange(slot_count, dtype=jnp.int32)
    cell_index = positions % (GRID * GRID)
    vision_page = positions // (GRID * GRID)
    vision_first = cell_index % GRID
    vision_second = cell_index // GRID
    own_valid = jnp.where(is_text, text_pages < PAGES, True).astype(f32)
    gain_rows = norm_gains[0]
    shift_rows = norm_shifts[0]
    rel_table = box_table[0]
    block_in = inputs[:, 0]
    normed_one, plain_one, inverse_one = norm_forward(block_in, gain_rows[0], shift_rows[0])
    normed_low = normed_one.astype(bf16)
    query = project(normed_low, w_query[0]).astype(bf16)
    own_keys = project(normed_low, w_key[0]).astype(bf16)
    own_values = project(normed_low, w_value[0]).astype(bf16)
    far_keys, far_values = partner((own_keys, own_values), "stream", 0)

    def geometry(row_index):
        text_page = text_pages[row_index]
        own_page = jnp.where(is_text, text_page, vision_page)
        far_page = jnp.where(is_text, vision_page, text_page)
        own_first = jnp.where(is_text, text_boxes[row_index, 0], vision_first)
        far_first = jnp.where(is_text, vision_first, text_boxes[row_index, 0])
        own_second = jnp.where(is_text, text_boxes[row_index, 1], vision_second)
        far_second = jnp.where(is_text, vision_second, text_boxes[row_index, 1])
        allowed = (own_page[:, None] == far_page[None, :]) | (own_page[:, None] == PAGES)
        return (
            allowed,
            bucket_offset(own_first, far_first, bucket_count),
            bucket_offset(own_second, far_second, bucket_count),
        )

    def heads_of(matrix):
        return matrix.reshape(slot_count, head_count, head_size)

    def score_block(row_index, allowed, offset_first, offset_second):
        raw = (
            jnp.einsum(
                "ihd,jhd->hij",
                heads_of(query[row_index]),
                heads_of(far_keys[row_index]),
                preferred_element_type=f32,
            )
            * score_scale
        )
        raw = (
            raw
            + bias_from(rel_table[:bucket_count], offset_first)
            + bias_from(rel_table[bucket_count:], offset_second)
        )
        return jnp.where(allowed[None], raw, masked_fill)

    row_index = 0
    allowed, offset_first, offset_second = geometry(row_index)
    masked = score_block(row_index, allowed, offset_first, offset_second)
    top_score = jnp.max(masked, axis=-1, keepdims=True)
    exp_scores = jnp.exp(masked - top_score)
    row_total = jnp.sum(exp_scores, axis=-1, keepdims=True)
    prob_low = (exp_scores / row_total).astype(bf16)
    attended = jnp.einsum(
        "hij,jhd->ihd",
        prob_low,
        heads_of(far_values[row_index]),
        preferred_element_type=f32,
    ).reshape(slot_count, model_width)
    attended_rows = [(attended * own_valid[row_index][:, None]).astype(bf16)]
    log_totals = [top_score + jnp.log(row_total)]
    attended_low = jnp.stack(attended_rows)
    branch_one = project(attended_low, w_out[0])
    middle = block_in + branch_one
    normed_two, plain_two, inverse_two = norm_forward(middle, gain_rows[1], shift_rows[1])
    normed_two_low = normed_two.astype(bf16)
    pre_act = project(normed_two_low, w_up[0]) + up_bias[0]
    act_low = jax.nn.gelu(pre_act).astype(bf16)
    branch_two = project(act_low, w_down[0]) + down_bias[0]
    block_out = middle + branch_two
    sublayer = branch_one + branch_two
    totals = lax.psum(
        (
            jnp.sum(own_valid * jnp.sum(block_out * block_out, axis=-1)),
            jnp.sum(own_valid * jnp.sum(sublayer * sublayer, axis=-1)),
            jnp.sum(own_valid),
        ),
        ("stream", "batch"),
    )
    denominator = totals[2] * model_width
    stats = jnp.stack([jnp.sqrt(totals[0] / denominator), jnp.sqrt(totals[1] / denominator)])
    grad_out = cotangent[:, 0]
    grad_out_low = grad_out.astype(bf16)
    grad_w_down = weight_grad(act_low, grad_out_low)
    grad_down_bias = jnp.sum(grad_out_low.astype(f32), axis=(0, 1))
    grad_act = back_project(grad_out_low, w_down[0])
    gelu_back = jax.vjp(jax.nn.gelu, pre_act)[1]
    grad_pre_low = gelu_back(grad_act)[0].astype(bf16)
    grad_w_up = weight_grad(normed_two_low, grad_pre_low)
    grad_up_bias = jnp.sum(grad_pre_low.astype(f32), axis=(0, 1))
    grad_normed_two = back_project(grad_pre_low, w_up[0])
    grad_gain_two = jnp.sum(grad_normed_two * plain_two, axis=(0, 1))
    grad_shift_two = jnp.sum(grad_normed_two, axis=(0, 1))
    grad_middle = grad_out + general_norm_backward(grad_normed_two, plain_two, inverse_two, gain_rows[1])
    grad_middle_low = grad_middle.astype(bf16)
    grad_w_out = weight_grad(attended_low, grad_middle_low)
    grad_attended = back_project(grad_middle_low, w_out[0]).astype(bf16) * own_valid[
        :, :, None
    ].astype(bf16)
    query_grad_rows, key_grad_rows, value_grad_rows = ([], [], [])
    row_index = 0
    allowed, offset_first, offset_second = geometry(row_index)
    masked = score_block(row_index, allowed, offset_first, offset_second)
    prob = jnp.exp(masked - log_totals[row_index])
    grad_heads = heads_of(grad_attended[row_index])
    grad_prob = jnp.einsum(
        "ihd,jhd->hij",
        grad_heads,
        heads_of(far_values[row_index]),
        preferred_element_type=f32,
    )
    inner_sum = jnp.sum(prob * grad_prob, axis=-1, keepdims=True)
    grad_score_low = (prob * (grad_prob - inner_sum)).astype(bf16)
    grad_score_wide = grad_score_low.astype(f32)
    grad_table = jnp.concatenate(
        [
            bias_grad(grad_score_wide, offset_first, bucket_count),
            bias_grad(grad_score_wide, offset_second, bucket_count),
        ],
        axis=0,
    )
    query_grad = (
        jnp.einsum(
            "hij,jhd->ihd",
            grad_score_low,
            heads_of(far_keys[row_index]),
            preferred_element_type=f32,
        )
        * score_scale
    )
    key_grad = (
        jnp.einsum(
            "hij,ihd->jhd",
            grad_score_low,
            heads_of(query[row_index]),
            preferred_element_type=f32,
        )
        * score_scale
    )
    value_grad = jnp.einsum(
        "hij,ihd->jhd", prob.astype(bf16), grad_heads, preferred_element_type=f32
    )
    query_grad_rows.append(query_grad.reshape(slot_count, model_width).astype(bf16))
    key_grad_rows.append(key_grad.reshape(slot_count, model_width).astype(bf16))
    value_grad_rows.append(value_grad.reshape(slot_count, model_width).astype(bf16))
    grad_query_low = jnp.stack(query_grad_rows)
    own_key_grad, own_value_grad = partner(
        (jnp.stack(key_grad_rows), jnp.stack(value_grad_rows)), "stream", 0
    )
    grad_w_query = weight_grad(normed_low, grad_query_low)
    grad_w_key = weight_grad(normed_low, own_key_grad)
    grad_w_value = weight_grad(normed_low, own_value_grad)
    grad_normed_one = (
        back_project(grad_query_low, w_query[0])
        + back_project(own_key_grad, w_key[0])
        + back_project(own_value_grad, w_value[0])
    )
    grad_gain_one = jnp.sum(grad_normed_one * plain_one, axis=(0, 1))
    grad_shift_one = jnp.sum(grad_normed_one, axis=(0, 1))
    grad_inputs = grad_middle + general_norm_backward(grad_normed_one, plain_one, inverse_one, gain_rows[0])
    big_sums = (
        lax.psum_scatter(grad_w_query, "batch", scatter_dimension=0, tiled=True),
        lax.psum_scatter(grad_w_key, "batch", scatter_dimension=0, tiled=True),
        lax.psum_scatter(grad_w_value, "batch", scatter_dimension=0, tiled=True),
        lax.psum_scatter(grad_w_out, "batch", scatter_dimension=0, tiled=True),
        lax.psum_scatter(grad_w_up, "batch", scatter_dimension=0, tiled=True),
        lax.psum_scatter(grad_w_down, "batch", scatter_dimension=0, tiled=True),
    )
    small_sums = lax.psum(
        (
            jnp.stack([grad_gain_one, grad_gain_two]),
            jnp.stack([grad_shift_one, grad_shift_two]),
            grad_up_bias,
            grad_down_bias,
            grad_table,
        ),
        "batch",
    )
    return (
        block_out[:, None],
        grad_inputs[:, None],
        small_sums[0][None],
        small_sums[1][None],
        big_sums[0][None],
        big_sums[1][None],
        big_sums[2][None],
        big_sums[3][None],
        big_sums[4][None],
        small_sums[2][None],
        big_sums[5][None],
        small_sums[3][None],
        small_sums[4][None],
        stats,
    )


def solution(mesh):
    sided = lambda dims: P("stream", *([None] * (dims - 1)))
    rows = P("batch", "stream", None, None)
    shard = P("stream", "batch", None)
    placed = (
        (rows, P("batch", None), P("batch", None, None), sided(3), sided(3))
        + (sided(3),) * 5
        + (sided(2), sided(3), sided(2), sided(3), rows)
    )
    fits = mesh.shape["batch"] == 16 and mesh.shape["stream"] == 2
    return jax.shard_map(
        on_device if fits else general_device,
        mesh=mesh,
        in_specs=placed,
        out_specs=(
            (rows, rows, sided(3), sided(3))
            + (shard,) * 5
            + (sided(2), shard, sided(2), sided(3), P())
        ),
        check_vma=False,
    )
```

```python
import jax
import jax.numpy as jnp
from jax import lax
from jax.experimental import pallas as pl
from jax.experimental.pallas import tpu as pltpu
from jax.sharding import PartitionSpec as P

GRID = 16
PAGES = 3
MESH = pl.DeviceIdType.MESH
LOG2E = 1.4426950408889634
LN2 = 0.6931471805599453
TOGETHER = 2
GELU_IN = 0.7978845608028654
GELU_CUBE = 0.044715
masked_fill = -1e30
f32 = jnp.float32
bf16 = jnp.bfloat16


def dot(left, right, form="nn"):
    dims = {"nn": (1, 0), "nt": (1, 1), "tn": (0, 0)}[form]
    return lax.dot_general(
        left, right, (((dims[0],), (dims[1],)), ((), ())), preferred_element_type=f32
    )


def stack(parts):
    return jnp.concatenate(parts, axis=0)


def plain_norm(values):
    center = values - jnp.mean(values, axis=-1, keepdims=True)
    inverse = lax.rsqrt(jnp.mean(center * center, axis=-1, keepdims=True) + 1e-05)
    return center * inverse, inverse


def norm_backward(grad_normed, plain, inverse, gain_row):
    scaled = grad_normed * gain_row
    first_mean = jnp.mean(scaled, axis=-1, keepdims=True)
    second_mean = jnp.mean(scaled * plain, axis=-1, keepdims=True)
    return inverse * (scaled - first_mean - plain * second_mean)


NAMES = (
    "ft", "wk", "wv", "back", "q_t", "k_t", "v_t", "att", "wo", "n2", "g2",
    "wu0", "wu1", "wd0", "wd1", "sd0", "sd1", "sr0", "sr1", "act", "gp",
)
SLOT = {name: i for i, name in enumerate(NAMES)}
for name, place in dict(
    nt="n2", wq="g2", gm="n2", go="g2", dq="wu0", dk="wu1", dv="wd0", send="wd1",
    so="sd0", sk="sd1", sv="sr0", sq="sr1", nt_again="act", wq_again="gp",
).items():
    SLOT[name] = SLOT[place]


def layer_kernel(
    x, cot, wq, wk, wv, wo, wup, wdn,
    up_bias, down_bias, gains, shifts, pages, boxes, rel_table,
    block_o, grad_o, nt_o, down_o, up_o, wo_o, wq_o, hop_o, sums_o, late_o, table_o,
    pool, wide, bias, lse, delta, page_low, page_col, cells,
    cd, cr, yd, yr, zd, zr, hop, hop_in, sums_in, late_in, table_in, table_far,
    in_sem, w_sem, out_sem, csem, crem, ysem, yrem, zsem, zrem, xsem, xrem, hsem, hrem,
    asem, arem, bsem, brem, lsem, lrem, fsem, frem, gxs, gxr, gzs, gzr, gys, gyr, gcs, gcr,
):
    slots, width = x.shape
    heads = lse.shape[0]
    size = width // heads
    third = slots // 3
    spans = [pl.ds(part * third, third) for part in range(3)]
    thirds = [slice(part * third, (part + 1) * third) for part in range(3)]
    part_rows = width // 16
    st = lax.axis_index("stream")
    me = lax.axis_index("batch")
    c = lax.rem(me, 2)
    y = lax.rem(lax.div(me, 2), 2)
    z = lax.div(me, 4)
    place = lax.rem(me, 4)
    core_peer = (st, me + 1 - 2 * c)
    y_peer = (st, me + 2 - 4 * y)
    z_at = [lax.rem(z + i, 4) for i in range(4)]
    z_peers = [(st, z_at[i] * 4 + place) for i in range(4)]
    place_at = [lax.rem(place + i, 4) for i in range(4)]
    place_peers = [(st, z * 4 + place_at[i]) for i in range(4)]
    x_peer = (1 - st, me)

    def slot(name):
        return pool.at[SLOT[name]]

    def remote(source, target, send, recv, peer):
        return pltpu.make_async_remote_copy(
            source, target, send, recv, device_id=peer, device_id_type=MESH
        )

    singles = dict(
        x=(x, wide.at[0]), cot=(cot, wide.at[1]), wo=(wo, slot("wo")), wq=(wq, slot("wq")),
        x_again=(x, wide.at[3]), wq_again=(wq, slot("wq_again")), nt_again=(nt_o, slot("nt_again")),
    )
    load_at = {name: i for i, name in enumerate(singles)}

    def load(name):
        return pltpu.make_async_copy(*singles[name], in_sem.at[load_at[name]])

    def chunk_of(t):
        return lax.rem(z + t + 1, 4)

    def chunk_loads(t):
        at = pl.multiple_of(chunk_of(t) * width, width)
        two = lax.rem(t, 2)
        return (
            pltpu.make_async_copy(
                wup.at[:, pl.ds(at, width)], pool.at[SLOT["wu0"] + two], w_sem.at[two, 0]
            ),
            pltpu.make_async_copy(
                wdn.at[pl.ds(at, width), :], pool.at[SLOT["wd0"] + two], w_sem.at[two, 1]
            ),
        )

    load("x").start()
    load("wq").start()
    load("cot").start()
    load("wo").start()
    for copy in chunk_loads(0):
        copy.start()

    barrier = pltpu.get_barrier_semaphore()
    peers = place_peers[1:] + z_peers[1:] + [x_peer]
    for peer in peers:
        pl.semaphore_signal(barrier, inc=1, device_id=peer, device_id_type=MESH)
    pl.semaphore_wait(barrier, len(peers))

    def slices(i):
        return slot(("wk", "wv")[i]).reshape(4, 2, 2, part_rows, width)

    def gather_x(i):
        source = (wk, wv)[i].at[pl.ds(pl.multiple_of(me * part_rows, 16), part_rows), :]
        return remote(source, slices(i).at[z, y, c], gxs.at[i], gxr.at[i], x_peer)

    def gather_z(i, k):
        own = slices(i).at[z, y, c]
        return remote(own, own, gzs.at[i, k - 1], gzr.at[i, k - 1], z_peers[k])

    def gather_z_here(i, k):
        found = slices(i).at[lax.rem(z + 4 - k, 4), y, c]
        return remote(found, found, gzs.at[i, k - 1], gzr.at[i, k - 1], z_peers[k])

    def gather_y(i, mine=True):
        held = slices(i).at[:, y if mine else 1 - y, c]
        return remote(held, held, gys.at[i], gyr.at[i], y_peer)

    def gather_core(i, mine=True):
        held = slices(i).at[:, :, c if mine else 1 - c]
        return remote(held, held, gcs.at[i], gcr.at[i], core_peer)

    gather_x(0).start()
    gather_x(1).start()

    def far_rows(part):
        return remote(
            slot("nt").at[:, thirds[part]],
            slot("ft").at[:, thirds[part]],
            xsem.at[part],
            xrem.at[part],
            x_peer,
        )

    load("x").wait()
    for part, span in enumerate(spans):
        plain, inverse = plain_norm(wide[0, span, :])
        low = (plain * gains[0:1, :] + shifts[0:1, :]).astype(bf16)
        pool[SLOT["nt"], :, thirds[part]] = low.T
        far_rows(part).start()
    pltpu.make_async_copy(slot("nt"), nt_o, out_sem.at[2]).start()

    page_row = pages[...].astype(f32)
    side = st.astype(f32)
    valid_row = jnp.maximum(side, jnp.where(page_row < PAGES - 0.5, 1.0, 0.0))
    page_rows = [jnp.where(page_row == p, 1.0, 0.0) for p in range(PAGES)]
    for p in range(PAGES):
        page_low[p] = jnp.broadcast_to(page_rows[p], (size, slots)).astype(bf16)
    page_col[...] = jnp.broadcast_to(page_row, (128, slots)).T
    cell = lax.broadcasted_iota(jnp.int32, (GRID, third), 0)
    spot = lax.broadcasted_iota(jnp.int32, (GRID, third), 1)
    spot_first = jnp.where(lax.rem(spot, GRID) == cell, 1.0, 0.0)
    spot_second = jnp.where(lax.div(spot, GRID) == cell, 1.0, 0.0)
    spot_once = stack([spot_first, spot_second]).astype(bf16)
    spot_twice = stack([spot_once, spot_once])
    buckets = rel_table.shape[0] // 2
    radius = (buckets - 1) // 2
    toward = 1 - 2 * st
    cell = lax.broadcasted_iota(jnp.int32, (GRID, slots), 0)
    offsets = [
        jnp.clip(toward * (boxes[axis : axis + 1, :] - cell), -radius, radius) + radius
        for axis in range(2)
    ]

    def bias_rows(head, carry):
        exact = []
        for axis in range(2):
            total = jnp.zeros((GRID, slots), f32)
            for bucket in range(buckets):
                total = jnp.where(
                    offsets[axis] == bucket, rel_table[axis * buckets + bucket, head], total
                )
            total = total * LOG2E
            if axis == 0:
                total = jnp.where(page_row > PAGES - 0.5, masked_fill, total)
            exact.append(total)
        exact = stack(exact)
        high = exact.astype(bf16)
        bias[head, : 2 * GRID, :] = high
        bias[head, 2 * GRID :, :] = (exact - high.astype(f32)).astype(bf16)
        return carry

    lax.fori_loop(0, heads, bias_rows, 0)

    load("wq").wait()
    pool[SLOT["q_t"]] = (dot(pool[SLOT["wq"]], pool[SLOT["nt"]], "tn") * (LOG2E * size**-0.5)).astype(
        bf16
    )
    sums_o[...] = jnp.zeros_like(sums_o)
    late_o[...] = jnp.zeros_like(late_o)
    load("cot").wait()
    for i in range(2):
        gather_x(i).wait()
        for k in (1, 2, 3):
            gather_z(i, k).start()
    for i in range(2):
        for k in (1, 2, 3):
            gather_z(i, k).wait_send()
            gather_z_here(i, k).wait_recv()
        gather_y(i).start()
    for i in range(2):
        gather_y(i).wait_send()
        gather_y(i, False).wait_recv()
        gather_core(i).start()
    for i in range(2):
        gather_core(i).wait_send()
        gather_core(i, False).wait_recv()
    for part in range(3):
        far_rows(part).wait()
        cols = thirds[part]
        pool[SLOT["k_t"], :, cols] = dot(pool[SLOT["wk"]], pool[SLOT["ft"], :, cols], "tn").astype(
            bf16
        )
        pool[SLOT["v_t"], :, cols] = dot(pool[SLOT["wv"]], pool[SLOT["ft"], :, cols], "tn").astype(
            bf16
        )

    def by_page(name, rows):
        return [pool[SLOT[name], rows, cols] for cols in thirds]

    def masked(name, rows):
        held = pool[SLOT[name], rows, :]
        return [held * page_low[p] for p in range(PAGES)]

    def fold(found):
        total = found[:size] * page_rows[0]
        for p in range(1, PAGES):
            total = total + found[p * size : (p + 1) * size] * page_rows[p]
        return total

    def column(p):
        return page_col[...] == p

    def spread(rows):
        middle, last = [jnp.concatenate([column(p)] * 2, axis=1) for p in (1, 2)]
        return jnp.where(middle, rows[1], jnp.where(last, rows[2], rows[0]))

    def rows_of(head):
        return pl.ds(pl.multiple_of(head * size, size), size)

    def in_pairs(step):
        def several(i, carry):
            for j in range(TOGETHER):
                step(TOGETHER * i + j, carry)
            return carry

        lax.fori_loop(0, heads // TOGETHER, several, 0)

    def text_forward(head, carry):
        rows = rows_of(head)
        scores = dot(
            stack(by_page("k_t", rows) + [spot_twice]),
            stack(masked("q_t", rows) + [bias[head]]),
            "tn",
        )
        top = jnp.max(scores, axis=0, keepdims=True)
        weight = jnp.exp2(scores - top).astype(bf16)
        found = dot(stack(by_page("v_t", rows) + [jnp.ones((16, third), bf16)]), weight)
        total = found[PAGES * size : PAGES * size + 1]
        pool[SLOT["att"], rows, :] = (fold(found) * (valid_row / total)).astype(bf16)
        lse[head] = top + jnp.log2(total)
        return carry

    def vision_forward(head, carry):
        rows = rows_of(head)
        scores = dot(
            stack(masked("k_t", rows) + [bias[head]]),
            stack(by_page("q_t", rows) + [spot_twice]),
            "tn",
        )
        tops = []
        for p in range(PAGES):
            inside = jnp.concatenate([column(p)] * 2, axis=1)
            tops.append(
                jnp.max(jnp.where(inside, scores, 2.0 * masked_fill), axis=0, keepdims=True)
            )
        weight = jnp.exp2(scores - spread(tops)).astype(bf16)
        counts = [page_low[p, :1, :] for p in range(PAGES)]
        counts = stack(counts + [jnp.zeros((16 - PAGES, slots), bf16)])
        found = dot(stack(masked("v_t", rows) + [counts]), weight)
        for p, cols in enumerate(thirds):
            total = found[PAGES * size + p : PAGES * size + p + 1]
            pool[SLOT["att"], rows, cols] = (found[p * size : (p + 1) * size] / total).astype(bf16)
            lse[head, :, cols] = tops[p] + jnp.log2(total)
        return carry

    @pl.when(st == 0)
    def _():
        in_pairs(text_forward)

    @pl.when(st == 1)
    def _():
        in_pairs(vision_forward)

    def down_view(at):
        return pool.at[at].reshape(2, 2, width // 4, width)

    def rest_view(at):
        return pool.at[at].reshape(4, 2, 2, part_rows, width)

    def core_down(t):
        at = SLOT["sd0"] + lax.rem(t, 2)
        return remote(down_view(at).at[:, 1 - c], cd.at[t], csem.at[t], crem.at[t], core_peer)

    def core_rest(p, at):
        return remote(
            rest_view(at).at[:, :, 1 - c], cr.at[p], csem.at[4 + p], crem.at[4 + p], core_peer
        )

    def y_down(t):
        return remote(cd.at[t, 1 - y], yd.at[t], ysem.at[t], yrem.at[t], y_peer)

    def y_rest(p):
        return remote(cr.at[p, :, 1 - y], yr.at[p], ysem.at[4 + p], yrem.at[4 + p], y_peer)

    def z_peer_of(t):
        return (st, chunk_of(t) * 4 + place)

    def z_down(t):
        return remote(yd.at[t], zd.at[t], zsem.at[0, t], zrem.at[0, t], z_peer_of(t))

    def z_rest(p, i):
        q = chunk_of(p) if p < 4 else p
        return remote(
            yr.at[p, z_at[i]], zr.at[q, i - 1], zsem.at[1 + p, i - 1], zrem.at[1 + q, i - 1], z_peers[i]
        )

    def z_here(q, i):
        return remote(
            yr.at[q, z_at[i]], zr.at[q, i - 1], zsem.at[1 + q, i - 1], zrem.at[1 + q, i - 1], z_peers[i]
        )

    def add_low(left, right):
        return (left.astype(f32) + right.astype(f32)).astype(bf16)

    def after_core_down(t):
        core_down(t).wait()
        cd[t] = add_low(cd[t], down_view(SLOT["sd0"] + lax.rem(t, 2))[:, c])
        y_down(t).start()

    def after_core_rest(p, at):
        core_rest(p, at).wait()
        cr[p] = add_low(cr[p], rest_view(at)[:, :, c])
        y_rest(p).start()

    def after_y_down(t, on=True):
        y_down(t).wait()
        yd[t] = add_low(yd[t], cd[t, y])
        if on:
            z_down(t).start()

    def after_y_rest(p):
        y_rest(p).wait()
        yr[p] = add_low(yr[p], cr[p, :, y])
        for i in (1, 2, 3):
            z_rest(p, i).start()

    def end_down():
        total = yd[3].astype(f32)
        for t in range(3):
            z_down(t).wait()
            total = total + zd[t].astype(f32)
        down_o[...] = total

    def end_rest(q):
        held = lax.rem(q - z + 3, 4) if q < 4 else q
        total = yr[held, z].astype(f32)
        for i in (1, 2, 3):
            z_here(q, i).wait()
            total = total + zr[q, i - 1].astype(f32)
        return total

    pltpu.make_async_copy(slot("nt"), nt_o, out_sem.at[2]).wait()
    load("wo").wait()
    for part, span in enumerate(spans):
        middle = wide[0, span, :] + dot(
            pool[SLOT["att"], :, thirds[part]], pool[SLOT["wo"]], "tn"
        )
        wide[0, span, :] = middle
        wide[2, span, :] = middle + down_bias[...]
        plain, inverse = plain_norm(middle)
        pool[SLOT["n2"], span, :] = (plain * gains[1:2, :] + shifts[1:2, :]).astype(bf16)
        low = wide[1, span, :].astype(bf16)
        pool[SLOT["g2"], span, :] = low
        sums_o[4:5, :] += jnp.sum(low.astype(f32), axis=0, keepdims=True)
    wide[3] = jnp.zeros((slots, width), f32)

    def feed(t, carry):
        two = lax.rem(t, 2)
        at = chunk_of(t)
        for copy in chunk_loads(t):
            copy.wait()

        @pl.when(t < 3)
        def _():
            for copy in chunk_loads(t + 1):
                copy.start()

        w_u = pool.at[SLOT["wu0"] + two]
        w_d = pool.at[SLOT["wd0"] + two]
        for cols in thirds:
            pre = dot(pool[SLOT["n2"]], w_u[:, cols]) + up_bias[at, :, cols]
            grad_act = dot(pool[SLOT["g2"]], w_d[cols, :], "nt")
            square = pre * pre
            gate = jnp.tanh(pre * (GELU_IN + (GELU_IN * GELU_CUBE) * square))
            gate_half = 0.5 + 0.5 * gate
            pool[SLOT["act"], :, cols] = (pre * gate_half).astype(bf16)
            slope = pre * (GELU_IN + (3.0 * GELU_IN * GELU_CUBE) * square)
            grad_pre = (grad_act * (gate_half * (1.0 + (1.0 - gate) * slope))).astype(bf16)
            pool[SLOT["gp"], :, cols] = grad_pre
            sums_o[pl.ds(5 + at, 1), cols] = jnp.sum(grad_pre.astype(f32), axis=0, keepdims=True)
        pool[SLOT["sd0"] + two] = dot(pool[SLOT["act"]], pool[SLOT["g2"]], "tn").astype(bf16)
        core_down(t).start()

        @pl.when(t > 0)
        def _():
            after_core_rest(t - 1, SLOT["sr0"] + 1 - two)

        pool[SLOT["sr0"] + two] = dot(pool[SLOT["n2"]], pool[SLOT["gp"]], "tn").astype(bf16)
        core_rest(t, SLOT["sr0"] + two).start()

        @pl.when(t == 3)
        def _():
            after_y_rest(0)

        wide[2] = wide[2] + dot(pool[SLOT["act"]], w_d[...])
        after_core_down(t)
        wide[3] = wide[3] + dot(pool[SLOT["gp"]], w_u[...], "nt")

        @pl.when(t > 1)
        def _():
            after_y_down(t - 2, True)

        return carry

    lax.fori_loop(0, 4, feed, 0)
    after_core_rest(3, SLOT["sr1"])

    pltpu.make_async_copy(wide.at[2], block_o, out_sem.at[0]).start()
    for span in spans:
        plain, inverse = plain_norm(wide[0, span, :])
        grad_two = wide[3, span, :]
        sums_o[1:2, :] += jnp.sum(grad_two * plain, axis=0, keepdims=True)
        sums_o[3:4, :] += jnp.sum(grad_two, axis=0, keepdims=True)
        middle = wide[1, span, :] + norm_backward(grad_two, plain, inverse, gains[1:2, :])
        wide[0, span, :] = middle
        pool[SLOT["gm"], span, :] = middle.astype(bf16)
    load("x_again").start()
    load("wq_again").start()
    load("nt_again").start()
    pool[SLOT["go"]] = (dot(pool[SLOT["wo"]], pool[SLOT["gm"]], "nt") * valid_row).astype(bf16)
    group = 4 * size
    for i in range(heads // 4):
        rows = slice(i * group, (i + 1) * group)
        both = pool[SLOT["att"], rows, :].astype(f32) * pool[SLOT["go"], rows, :].astype(f32)
        delta[4 * i : 4 * i + 4] = jnp.sum(both.reshape(4, size, slots), axis=1, keepdims=True)
    pool[SLOT["so"]] = dot(pool[SLOT["att"]], pool[SLOT["gm"]]).astype(bf16)
    core_rest(4, SLOT["so"]).start()
    after_core_rest(4, SLOT["so"])
    after_y_rest(1)

    def table_rows(head, found):
        for axis in range(2):
            here = found[axis * GRID : (axis + 1) * GRID]
            for bucket in range(buckets):
                kept = jnp.where(offsets[axis] == bucket, here, 0.0)
                cells[pl.ds((axis * buckets + bucket) * 16 + head, 1), :] = jnp.sum(
                    kept, axis=0, keepdims=True
                )

    def text_backward(head, carry):
        rows = rows_of(head)
        keys = by_page("k_t", rows)
        queries = masked("q_t", rows)
        grads = stack(masked("go", rows))
        scores = dot(stack(keys + [spot_twice]), stack(queries + [bias[head]]), "tn")
        prob = jnp.exp2(scores - lse[head])
        grad_prob = dot(stack(by_page("v_t", rows)), grads, "tn")
        grad_score = (prob * (grad_prob - delta[head])).astype(bf16)
        found = dot(grads, prob.astype(bf16), "nt")
        for p, cols in enumerate(thirds):
            pool[SLOT["dv"], rows, cols] = found[p * size : (p + 1) * size].astype(bf16)
        found = dot(stack(queries), grad_score, "nt") * LN2
        for p, cols in enumerate(thirds):
            pool[SLOT["dk"], rows, cols] = found[p * size : (p + 1) * size].astype(bf16)
        found = dot(stack(keys + [spot_once]), grad_score)
        pool[SLOT["dq"], rows, :] = (fold(found) * size**-0.5).astype(bf16)
        table_rows(head, found[PAGES * size :])
        return carry

    def vision_backward(head, carry):
        rows = rows_of(head)
        keys = masked("k_t", rows)
        queries = by_page("q_t", rows)
        grads = stack(by_page("go", rows))
        scores = dot(stack(keys + [bias[head]]), stack(queries + [spot_twice]), "tn")
        prob = jnp.exp2(scores - spread([lse[head, :, cols] for cols in thirds]))
        grad_prob = dot(stack(masked("v_t", rows)), grads, "tn")
        inner = spread([delta[head, :, cols] for cols in thirds])
        grad_score = (prob * (grad_prob - inner)).astype(bf16)
        pool[SLOT["dv"], rows, :] = fold(dot(grads, prob.astype(bf16), "nt")).astype(bf16)
        found = dot(stack(queries + [spot_once]), grad_score, "nt")
        pool[SLOT["dk"], rows, :] = (fold(found) * LN2).astype(bf16)
        table_rows(head, found[PAGES * size :])
        found = dot(stack(keys), grad_score) * size**-0.5
        for p, cols in enumerate(thirds):
            pool[SLOT["dq"], rows, cols] = found[p * size : (p + 1) * size].astype(bf16)
        return carry

    cells[...] = jnp.zeros_like(cells)

    @pl.when(st == 0)
    def _():
        in_pairs(text_backward)

    @pl.when(st == 1)
    def _():
        in_pairs(vision_backward)

    after_y_down(2)
    after_y_rest(2)

    def back_rows(part):
        return remote(
            slot("send").at[:, thirds[part]],
            slot("back").at[:, thirds[part]],
            xsem.at[3 + part],
            xrem.at[3 + part],
            x_peer,
        )

    for part, cols in enumerate(thirds):
        pool[SLOT["send"], :, cols] = (
            dot(pool[SLOT["wk"]], pool[SLOT["dk"], :, cols])
            + dot(pool[SLOT["wv"]], pool[SLOT["dv"], :, cols])
        ).astype(bf16)
        back_rows(part).start()
    after_y_down(3, False)
    pool[SLOT["sk"]] = dot(pool[SLOT["ft"]], pool[SLOT["dk"]], "nt").astype(bf16)
    core_rest(5, SLOT["sk"]).start()
    pool[SLOT["sv"]] = dot(pool[SLOT["ft"]], pool[SLOT["dv"]], "nt").astype(bf16)
    core_rest(6, SLOT["sv"]).start()
    after_core_rest(5, SLOT["sk"])
    load("nt_again").wait()
    pool[SLOT["sq"]] = dot(pool[SLOT["nt_again"]], pool[SLOT["dq"]], "nt").astype(bf16)
    core_rest(7, SLOT["sq"]).start()
    after_core_rest(6, SLOT["sv"])
    load("wq_again").wait()
    wide[1] = dot(pool[SLOT["wq_again"]], pool[SLOT["dq"]])
    after_core_rest(7, SLOT["sq"])

    load("x_again").wait()
    base = 2 * buckets * 16
    cells[base + 2 : base + 3, :] = valid_row
    for span in spans:
        block = wide[2, span, :]
        own = jnp.maximum(side, jnp.where(page_col[span, 0:1] < PAGES - 0.5, 1.0, 0.0))
        sub = block - wide[3, span, :]
        cells[base : base + 1, :] += jnp.sum(own * block * block, axis=0, keepdims=True)
        cells[base + 1 : base + 2, :] += jnp.sum(own * sub * sub, axis=0, keepdims=True)
    table_o[...] = lax.dot_general(
        jnp.ones((8, width), f32),
        cells[...],
        (((1,), (1,)), ((), ())),
        preferred_element_type=f32,
        precision=lax.Precision.HIGHEST,
    )

    def exchange(mine, found, send, recv, peers, at, start):
        for k in (1, 2, 3):
            copy = remote(mine, found.at[at[0]], send.at[k - 1], recv.at[k - 1], peers[k])
            if start:
                copy.start()
            else:
                copy.wait_send()
                there = lax.rem(at[0] + 4 - k, 4)
                remote(mine, found.at[there], send.at[k - 1], recv.at[k - 1], peers[k]).wait_recv()
        if not start:
            found[at[0]] = mine[...]
            mine[...] = ((found[0] + found[1]) + found[2]) + found[3]

    def small(stage, start):
        peers, at = ((place_peers, place_at), (z_peers, z_at))[stage]
        exchange(sums_o, sums_in.at[stage], asem.at[stage], arem.at[stage], peers, at, start)
        exchange(table_o, table_in.at[stage], bsem.at[stage], brem.at[stage], peers, at, start)

    def last_small(stage, start):
        peers, at = ((place_peers, place_at), (z_peers, z_at))[stage]
        exchange(late_o, late_in.at[stage], lsem.at[stage], lrem.at[stage], peers, at, start)

    def hop_copy(i):
        return remote(hop.at[i], hop_in.at[i], hsem.at[i], hrem.at[i], x_peer)

    small(0, True)
    after_y_rest(3)
    small(0, False)
    small(1, True)
    end_down()
    for q in range(4):
        up_o[:, q * width : (q + 1) * width] = end_rest(q)
    after_y_rest(4)
    small(1, False)
    table_swap = remote(table_o, table_far, fsem, frem, x_peer)
    table_swap.start()
    after_y_rest(5)
    after_y_rest(6)

    pltpu.make_async_copy(wide.at[2], block_o, out_sem.at[0]).wait()
    for part, span in enumerate(spans):
        cols = thirds[part]
        back_rows(part).wait()
        grad_one = (wide[1, :, cols] + pool[SLOT["back"], :, cols].astype(f32)).T
        plain, inverse = plain_norm(wide[3, span, :])
        late_o[0:1, :] += jnp.sum(grad_one * plain, axis=0, keepdims=True)
        late_o[1:2, :] += jnp.sum(grad_one, axis=0, keepdims=True)
        wide[2, span, :] = wide[0, span, :] + norm_backward(
            grad_one, plain, inverse, gains[0:1, :]
        )
    pltpu.make_async_copy(wide.at[2], grad_o, out_sem.at[1]).start()
    last_small(0, True)
    after_y_rest(7)
    wo_o[...] = end_rest(4)
    hop[0] = end_rest(5).astype(bf16)
    hop_copy(0).start()
    last_small(0, False)
    last_small(1, True)
    hop[1] = end_rest(6).astype(bf16)
    hop_copy(1).start()
    wq_o[...] = end_rest(7)
    table_swap.wait()
    lane = lax.broadcasted_iota(jnp.int32, table_o.shape, 1)
    table_o[...] = table_o[...] + jnp.where(lane >= base, table_far[...], 0.0)
    last_small(1, False)
    for i in range(2):
        hop_copy(i).wait()
        hop_o[i] = hop_in[i].astype(f32)
    pltpu.make_async_copy(wide.at[2], grad_o, out_sem.at[1]).wait()


def hand_over(
    block, grad_in, down, up, out, query, hop, sums, late, table,
    block_o, grad_o, gains_o, shifts_o, query_o, key_o, value_o, out_o, up_o, up_bias_o, down_o, down_bias_o, table_o, stats_o,
    held, down_h, up_h, out_h, query_h, hop_h, sums_h, late_h, table_h, in_sem, out_sem, sem,
):
    slots, width = block.shape
    step = slots // 4
    moves = []
    for i, (source, target) in enumerate(((block, block_o), (grad_in, grad_o))):
        for j in range(4):
            span = pl.ds(j * step, step)
            moves.append(
                (
                    pltpu.make_async_copy(
                        source.at[span, :], held.at[i, span, :], in_sem.at[i, j]
                    ),
                    pltpu.make_async_copy(
                        held.at[i, span, :], target.at[span, :], out_sem.at[i, j]
                    ),
                )
            )
    for move in moves:
        move[0].start()
    small = ((down, down_h), (up, up_h), (out, out_h), (query, query_h), (hop, hop_h), (sums, sums_h), (late, late_h), (table, table_h))
    small = [pltpu.make_async_copy(*pair, sem.at[i]) for i, pair in enumerate(small)]
    for copy in small:
        copy.start()
    for copy in small:
        copy.wait()
    up_o[...] = up_h[...]
    down_o[...] = down_h[...]
    gains_o[0:1, :] = late_h[0:1, :]
    gains_o[1:2, :] = sums_h[1:2, :]
    shifts_o[0:1, :] = late_h[1:2, :]
    shifts_o[1:2, :] = sums_h[3:4, :]
    down_bias_o[...] = sums_h[4:5, :]
    for q in range(4):
        up_bias_o[:, q * width : (q + 1) * width] = sums_h[5 + q : 6 + q, :]
    query_o[...] = query_h[...]
    key_o[...] = hop_h[0]
    value_o[...] = hop_h[1]
    out_o[...] = out_h[...]
    rows, heads = table_o.shape
    for row in range(rows):
        table_o[row : row + 1, :] = table_h[0:1, row * 16 : row * 16 + heads]
    total = table_h[0:1, rows * 16 : rows * 16 + 2]
    count = table_h[0:1, rows * 16 + 2 : rows * 16 + 3]
    stats_o[...] = jnp.sqrt(total / (count * width))
    for move in moves:
        move[0].wait()
        move[1].start()
    for move in moves:
        move[1].wait()


def on_device(
    inputs,
    text_pages,
    text_boxes,
    norm_gains,
    norm_shifts,
    w_query,
    w_key,
    w_value,
    w_out,
    w_up,
    up_bias,
    w_down,
    down_bias,
    box_table,
    cotangent,
):
    slots, width = inputs.shape[2:]
    rel_rows, heads = box_table.shape[1:]
    size = width // heads
    part = width // 16
    shape = lambda *dims: jax.ShapeDtypeStruct(dims, f32)
    vmem = pl.BlockSpec(memory_space=pltpu.VMEM)
    smem = pl.BlockSpec(memory_space=pltpu.SMEM)
    hbm = pl.BlockSpec(memory_space=pl.ANY)
    dma = pltpu.SemaphoreType.DMA
    cell_rows = rel_rows * 16 + 16
    low = lambda *dims: pltpu.VMEM(dims, bf16)
    full = lambda *dims: pltpu.VMEM(dims, f32)
    block, grad_in, _, down, up, out, query, hop, sums, late, table = pl.pallas_call(
        layer_kernel,
        out_shape=[
            shape(slots, width),
            shape(slots, width),
            jax.ShapeDtypeStruct((width, slots), bf16),
            shape(4 * part, width),
            shape(part, 4 * width),
            shape(part, width),
            shape(part, width),
            shape(2, part, width),
            shape(16, width),
            shape(8, width),
            shape(8, cell_rows),
        ],
        in_specs=[hbm] * 8 + [vmem] * 6 + [smem],
        out_specs=[hbm] * 3 + [vmem] * 8,
        scratch_shapes=[
            low(len(NAMES), slots, width),
            full(4, slots, width),
            low(heads, 4 * GRID, slots),
            full(heads, 1, slots),
            full(heads, 1, slots),
            low(PAGES, size, slots),
            full(slots, 128),
            full(cell_rows, width),
            low(4, 2, 4 * part, width),
            low(8, 4, 2, part, width),
            low(4, 4 * part, width),
            low(8, 4, part, width),
            low(3, 4 * part, width),
            low(8, 3, part, width),
            low(2, part, width),
            low(2, part, width),
            full(2, 4, 16, width),
            full(2, 4, 8, width),
            full(2, 4, 8, cell_rows),
            full(8, cell_rows),
            dma((7,)),
            dma((2, 2)),
            dma((3,)),
            dma((12,)),
            dma((12,)),
            dma((12,)),
            dma((12,)),
            dma((9, 3)),
            dma((9, 3)),
            dma((6,)),
            dma((6,)),
            dma((2,)),
            dma((2,)),
            dma((2, 3)),
            dma((2, 3)),
            dma((2, 3)),
            dma((2, 3)),
            dma((2, 3)),
            dma((2, 3)),
            dma,
            dma,
            dma((2,)),
            dma((2,)),
            dma((2, 3)),
            dma((2, 3)),
            dma((2,)),
            dma((2,)),
            dma((2,)),
            dma((2,)),
        ],
        compiler_params=pltpu.CompilerParams(
            collective_id=0, has_side_effects=True, vmem_limit_bytes=61 * 2**20
        ),
        name="layer",
    )(
        inputs[0, 0],
        cotangent[0, 0],
        w_query[0],
        w_key[0],
        w_value[0],
        w_out[0],
        w_up[0],
        w_down[0],
        up_bias.reshape(4, 1, width),
        down_bias,
        norm_gains[0],
        norm_shifts[0],
        text_pages,
        text_boxes[0],
        box_table[0],
    )
    outs = pl.pallas_call(
        hand_over,
        out_shape=[
            shape(slots, width),
            shape(slots, width),
            shape(2, width),
            shape(2, width),
            shape(part, width),
            shape(part, width),
            shape(part, width),
            shape(part, width),
            shape(part, 4 * width),
            shape(1, 4 * width),
            shape(4 * part, width),
            shape(1, width),
            shape(rel_rows, heads),
            shape(1, 2),
        ],
        in_specs=[hbm] * 10,
        out_specs=[hbm] * 2 + [vmem] * 12,
        scratch_shapes=[
            full(2, slots, width),
            full(4 * part, width),
            full(part, 4 * width),
            full(part, width),
            full(part, width),
            full(2, part, width),
            full(16, width),
            full(8, width),
            full(8, cell_rows),
            dma((2, 4)),
            dma((2, 4)),
            dma((8,)),
        ],
        compiler_params=pltpu.CompilerParams(vmem_limit_bytes=61 * 2**20),
        name="hand_over",
    )(block, grad_in, down, up, out, query, hop, sums, late, table)
    block, grad_in, gains, shifts, query, key, value, out, up, up_b, down, down_b, table, stats = outs
    return (
        block[None, None],
        grad_in[None, None],
        gains[None],
        shifts[None],
        query[None],
        key[None],
        value[None],
        out[None],
        up[None],
        up_b,
        down[None],
        down_b,
        table[None],
        stats[0],
    )


def partner(block, axis, bit):
    count = lax.axis_size(axis)
    route = []
    for low in range(count):
        high = low | 1 << bit
        if high != low and high < count:
            route += [(low, high), (high, low)]
    return lax.ppermute(block, axis, route)


def norm_forward(values, gain_row, shift_row):
    center = values - jnp.mean(values, axis=-1, keepdims=True)
    inverse = lax.rsqrt(jnp.mean(center * center, axis=-1, keepdims=True) + 1e-05)
    normal_part = center * inverse
    return (normal_part * gain_row + shift_row, normal_part, inverse)


def general_norm_backward(grad_normed, normal_part, inverse, gain_row):
    scaled = grad_normed * gain_row
    first_mean = jnp.mean(scaled, axis=-1, keepdims=True)
    second_mean = jnp.mean(scaled * normal_part, axis=-1, keepdims=True)
    return inverse * (scaled - first_mean - normal_part * second_mean)


def bucket_offset(own_coord, far_coord, bucket_count):
    radius = (bucket_count - 1) // 2
    return jnp.clip(own_coord[:, None] - far_coord[None, :], -radius, radius) + radius


def bias_from(rel_table, offset):
    result = jnp.zeros((rel_table.shape[1],) + offset.shape, f32)
    for bucket in range(rel_table.shape[0]):
        result = (
            result + rel_table[bucket][:, None, None] * (offset == bucket).astype(f32)[None]
        )
    return result


def bias_grad(grad_wide, offset, bucket_count):
    return jnp.stack(
        [
            jnp.sum(grad_wide * (offset == bucket).astype(f32)[None], axis=(1, 2))
            for bucket in range(bucket_count)
        ]
    )


def project(left, right):
    return jnp.einsum("rsd,de->rse", left, right, preferred_element_type=f32)


def weight_grad(left, right):
    return jnp.einsum("rsd,rse->de", left, right, preferred_element_type=f32)


def back_project(grad_low, weight):
    return jnp.einsum("rse,de->rsd", grad_low, weight, preferred_element_type=f32)


def general_device(
    inputs,
    text_pages,
    text_boxes,
    norm_gains,
    norm_shifts,
    w_query,
    w_key,
    w_value,
    w_out,
    w_up,
    up_bias,
    w_down,
    down_bias,
    box_table,
    cotangent,
):
    slot_count = inputs.shape[2]
    model_width = inputs.shape[3]
    head_count = box_table.shape[2]
    head_size = model_width // head_count
    bucket_count = box_table.shape[1] // 2
    score_scale = head_size ** (-0.5)
    is_text = lax.axis_index("stream") == 0
    positions = jnp.arange(slot_count, dtype=jnp.int32)
    cell_index = positions % (GRID * GRID)
    vision_page = positions // (GRID * GRID)
    vision_first = cell_index % GRID
    vision_second = cell_index // GRID
    own_valid = jnp.where(is_text, text_pages < PAGES, True).astype(f32)
    gain_rows = norm_gains[0]
    shift_rows = norm_shifts[0]
    rel_table = box_table[0]
    block_in = inputs[:, 0]
    normed_one, plain_one, inverse_one = norm_forward(block_in, gain_rows[0], shift_rows[0])
    normed_low = normed_one.astype(bf16)
    query = project(normed_low, w_query[0]).astype(bf16)
    own_keys = project(normed_low, w_key[0]).astype(bf16)
    own_values = project(normed_low, w_value[0]).astype(bf16)
    far_keys, far_values = partner((own_keys, own_values), "stream", 0)

    def geometry(row_index):
        text_page = text_pages[row_index]
        own_page = jnp.where(is_text, text_page, vision_page)
        far_page = jnp.where(is_text, vision_page, text_page)
        own_first = jnp.where(is_text, text_boxes[row_index, 0], vision_first)
        far_first = jnp.where(is_text, vision_first, text_boxes[row_index, 0])
        own_second = jnp.where(is_text, text_boxes[row_index, 1], vision_second)
        far_second = jnp.where(is_text, vision_second, text_boxes[row_index, 1])
        allowed = (own_page[:, None] == far_page[None, :]) | (own_page[:, None] == PAGES)
        return (
            allowed,
            bucket_offset(own_first, far_first, bucket_count),
            bucket_offset(own_second, far_second, bucket_count),
        )

    def heads_of(matrix):
        return matrix.reshape(slot_count, head_count, head_size)

    def score_block(row_index, allowed, offset_first, offset_second):
        raw = (
            jnp.einsum(
                "ihd,jhd->hij",
                heads_of(query[row_index]),
                heads_of(far_keys[row_index]),
                preferred_element_type=f32,
            )
            * score_scale
        )
        raw = (
            raw
            + bias_from(rel_table[:bucket_count], offset_first)
            + bias_from(rel_table[bucket_count:], offset_second)
        )
        return jnp.where(allowed[None], raw, masked_fill)

    row_index = 0
    allowed, offset_first, offset_second = geometry(row_index)
    masked = score_block(row_index, allowed, offset_first, offset_second)
    top_score = jnp.max(masked, axis=-1, keepdims=True)
    exp_scores = jnp.exp(masked - top_score)
    row_total = jnp.sum(exp_scores, axis=-1, keepdims=True)
    prob_low = (exp_scores / row_total).astype(bf16)
    attended = jnp.einsum(
        "hij,jhd->ihd",
        prob_low,
        heads_of(far_values[row_index]),
        preferred_element_type=f32,
    ).reshape(slot_count, model_width)
    attended_rows = [(attended * own_valid[row_index][:, None]).astype(bf16)]
    log_totals = [top_score + jnp.log(row_total)]
    attended_low = jnp.stack(attended_rows)
    branch_one = project(attended_low, w_out[0])
    middle = block_in + branch_one
    normed_two, plain_two, inverse_two = norm_forward(middle, gain_rows[1], shift_rows[1])
    normed_two_low = normed_two.astype(bf16)
    pre_act = project(normed_two_low, w_up[0]) + up_bias[0]
    act_low = jax.nn.gelu(pre_act).astype(bf16)
    branch_two = project(act_low, w_down[0]) + down_bias[0]
    block_out = middle + branch_two
    sublayer = branch_one + branch_two
    totals = lax.psum(
        (
            jnp.sum(own_valid * jnp.sum(block_out * block_out, axis=-1)),
            jnp.sum(own_valid * jnp.sum(sublayer * sublayer, axis=-1)),
            jnp.sum(own_valid),
        ),
        ("stream", "batch"),
    )
    denominator = totals[2] * model_width
    stats = jnp.stack([jnp.sqrt(totals[0] / denominator), jnp.sqrt(totals[1] / denominator)])
    grad_out = cotangent[:, 0]
    grad_out_low = grad_out.astype(bf16)
    grad_w_down = weight_grad(act_low, grad_out_low)
    grad_down_bias = jnp.sum(grad_out_low.astype(f32), axis=(0, 1))
    grad_act = back_project(grad_out_low, w_down[0])
    gelu_back = jax.vjp(jax.nn.gelu, pre_act)[1]
    grad_pre_low = gelu_back(grad_act)[0].astype(bf16)
    grad_w_up = weight_grad(normed_two_low, grad_pre_low)
    grad_up_bias = jnp.sum(grad_pre_low.astype(f32), axis=(0, 1))
    grad_normed_two = back_project(grad_pre_low, w_up[0])
    grad_gain_two = jnp.sum(grad_normed_two * plain_two, axis=(0, 1))
    grad_shift_two = jnp.sum(grad_normed_two, axis=(0, 1))
    grad_middle = grad_out + general_norm_backward(grad_normed_two, plain_two, inverse_two, gain_rows[1])
    grad_middle_low = grad_middle.astype(bf16)
    grad_w_out = weight_grad(attended_low, grad_middle_low)
    grad_attended = back_project(grad_middle_low, w_out[0]).astype(bf16) * own_valid[
        :, :, None
    ].astype(bf16)
    query_grad_rows, key_grad_rows, value_grad_rows = ([], [], [])
    row_index = 0
    allowed, offset_first, offset_second = geometry(row_index)
    masked = score_block(row_index, allowed, offset_first, offset_second)
    prob = jnp.exp(masked - log_totals[row_index])
    grad_heads = heads_of(grad_attended[row_index])
    grad_prob = jnp.einsum(
        "ihd,jhd->hij",
        grad_heads,
        heads_of(far_values[row_index]),
        preferred_element_type=f32,
    )
    inner_sum = jnp.sum(prob * grad_prob, axis=-1, keepdims=True)
    grad_score_low = (prob * (grad_prob - inner_sum)).astype(bf16)
    grad_score_wide = grad_score_low.astype(f32)
    grad_table = jnp.concatenate(
        [
            bias_grad(grad_score_wide, offset_first, bucket_count),
            bias_grad(grad_score_wide, offset_second, bucket_count),
        ],
        axis=0,
    )
    query_grad = (
        jnp.einsum(
            "hij,jhd->ihd",
            grad_score_low,
            heads_of(far_keys[row_index]),
            preferred_element_type=f32,
        )
        * score_scale
    )
    key_grad = (
        jnp.einsum(
            "hij,ihd->jhd",
            grad_score_low,
            heads_of(query[row_index]),
            preferred_element_type=f32,
        )
        * score_scale
    )
    value_grad = jnp.einsum(
        "hij,ihd->jhd", prob.astype(bf16), grad_heads, preferred_element_type=f32
    )
    query_grad_rows.append(query_grad.reshape(slot_count, model_width).astype(bf16))
    key_grad_rows.append(key_grad.reshape(slot_count, model_width).astype(bf16))
    value_grad_rows.append(value_grad.reshape(slot_count, model_width).astype(bf16))
    grad_query_low = jnp.stack(query_grad_rows)
    own_key_grad, own_value_grad = partner(
        (jnp.stack(key_grad_rows), jnp.stack(value_grad_rows)), "stream", 0
    )
    grad_w_query = weight_grad(normed_low, grad_query_low)
    grad_w_key = weight_grad(normed_low, own_key_grad)
    grad_w_value = weight_grad(normed_low, own_value_grad)
    grad_normed_one = (
        back_project(grad_query_low, w_query[0])
        + back_project(own_key_grad, w_key[0])
        + back_project(own_value_grad, w_value[0])
    )
    grad_gain_one = jnp.sum(grad_normed_one * plain_one, axis=(0, 1))
    grad_shift_one = jnp.sum(grad_normed_one, axis=(0, 1))
    grad_inputs = grad_middle + general_norm_backward(grad_normed_one, plain_one, inverse_one, gain_rows[0])
    big_sums = (
        lax.psum_scatter(grad_w_query, "batch", scatter_dimension=0, tiled=True),
        lax.psum_scatter(grad_w_key, "batch", scatter_dimension=0, tiled=True),
        lax.psum_scatter(grad_w_value, "batch", scatter_dimension=0, tiled=True),
        lax.psum_scatter(grad_w_out, "batch", scatter_dimension=0, tiled=True),
        lax.psum_scatter(grad_w_up, "batch", scatter_dimension=0, tiled=True),
        lax.psum_scatter(grad_w_down, "batch", scatter_dimension=0, tiled=True),
    )
    small_sums = lax.psum(
        (
            jnp.stack([grad_gain_one, grad_gain_two]),
            jnp.stack([grad_shift_one, grad_shift_two]),
            grad_up_bias,
            grad_down_bias,
            grad_table,
        ),
        "batch",
    )
    return (
        block_out[:, None],
        grad_inputs[:, None],
        small_sums[0][None],
        small_sums[1][None],
        big_sums[0][None],
        big_sums[1][None],
        big_sums[2][None],
        big_sums[3][None],
        big_sums[4][None],
        small_sums[2][None],
        big_sums[5][None],
        small_sums[3][None],
        small_sums[4][None],
        stats,
    )


def solution(mesh):
    sided = lambda dims: P("stream", *([None] * (dims - 1)))
    rows = P("batch", "stream", None, None)
    shard = P("stream", "batch", None)
    placed = (
        (rows, P("batch", None), P("batch", None, None), sided(3), sided(3))
        + (sided(3),) * 5
        + (sided(2), sided(3), sided(2), sided(3), rows)
    )
    fits = mesh.shape["batch"] == 16 and mesh.shape["stream"] == 2
    return jax.shard_map(
        on_device if fits else general_device,
        mesh=mesh,
        in_specs=placed,
        out_specs=(
            (rows, rows, sided(3), sided(3))
            + (shard,) * 5
            + (sided(2), shard, sided(2), sided(3), P())
        ),
        check_vma=False,
    )
```

```python
import jax
import jax.numpy as jnp
from jax import lax
from jax.experimental import pallas as pl
from jax.experimental.pallas import tpu as pltpu
from jax.sharding import PartitionSpec as P

GRID = 16
PAGES = 3
MESH = pl.DeviceIdType.MESH
LOG2E = 1.4426950408889634
LN2 = 0.6931471805599453
TOGETHER = 4
GELU_IN = 0.7978845608028654
GELU_CUBE = 0.044715
masked_fill = -1e30
f32 = jnp.float32
bf16 = jnp.bfloat16


def dot(left, right, form="nn"):
    dims = {"nn": (1, 0), "nt": (1, 1), "tn": (0, 0)}[form]
    return lax.dot_general(
        left, right, (((dims[0],), (dims[1],)), ((), ())), preferred_element_type=f32
    )


def stack(parts):
    return jnp.concatenate(parts, axis=0)


def plain_norm(values):
    center = values - jnp.mean(values, axis=-1, keepdims=True)
    inverse = lax.rsqrt(jnp.mean(center * center, axis=-1, keepdims=True) + 1e-05)
    return center * inverse, inverse


def norm_backward(grad_normed, plain, inverse, gain_row):
    scaled = grad_normed * gain_row
    first_mean = jnp.mean(scaled, axis=-1, keepdims=True)
    second_mean = jnp.mean(scaled * plain, axis=-1, keepdims=True)
    return inverse * (scaled - first_mean - plain * second_mean)


NAMES = (
    "ft", "wk", "wv", "back", "q_t", "k_t", "v_t", "att", "wo", "n2", "g2", "act", "gp",
    "wu", "wd", "sd", "sr",
)
RINGS = 4
SHARED = dict(
    nt=("n2",), wq=("act",), gm=("n2",), go=("g2",), dq=("wu", 0), dk=("wu", 1), dv=("wd", 0),
    send=("wd", 1), so=("sd", 0), sk=("sd", 1), sv=("sr", 0), sq=("sr", 1), sr1=("sr", 1),
    nt_again=("act",), wq_again=("gp",), sr0=("sr", 0),
)


def layer_kernel(
    x, cot, wq, wk, wv, wo, wup, wdn,
    up_bias, down_bias, gains, shifts, pages, boxes, rel_hbm,
    block_o, grad_o, nt_o, ga_o, down_o, up_o, wo_o, wq_o, hop_o, sums_o, late_o, table_o,
    buffers, wides, rel_table, bias, lse, delta, page_low, page_col, cells,
    cd, cr, yd, yr, zd, zr, hop, hop_in, sums_in, late_in, table_in, table_far,
    in_sem, w_sem, out_sem, csem, crem, ysem, yrem, zsem, zrem, xsem, xrem, hsem, hrem,
    asem, arem, bsem, brem, lsem, lrem, tsem, trem, gxs, gxr, gzs, gzr, gys, gyr, gcs, gcr,
):
    slots, width = x.shape
    heads = lse.shape[0]
    size = width // heads
    third = slots // 3
    thirds = [slice(part * third, (part + 1) * third) for part in range(3)]
    part_rows = width // 16
    st = lax.axis_index("stream")
    me = lax.axis_index("batch")
    c = lax.rem(me, 2)
    y = lax.rem(lax.div(me, 2), 2)
    z = lax.div(me, 4)
    place = lax.rem(me, 4)
    core_peer = (st, me + 1 - 2 * c)
    y_peer = (st, me + 2 - 4 * y)
    z_at = [lax.rem(z + i, 4) for i in range(4)]
    z_peers = [(st, z_at[i] * 4 + place) for i in range(4)]
    place_at = [lax.rem(place + i, 4) for i in range(4)]
    place_peers = [(st, z * 4 + place_at[i]) for i in range(4)]
    x_peer = (1 - st, me)

    def span_of(j):
        return pl.ds(pl.multiple_of(j * third, third), third)

    def unrolled_third(step):
        for j in range(3):
            step(j, pl.ds(j * third, third))

    def each_third(step):
        def body(j, carry):
            step(j, span_of(j))
            return carry

        lax.fori_loop(0, 3, body, 0)

    S = dict(zip(NAMES, buffers))
    for name, (held, *at) in SHARED.items():
        S[name] = S[held].at[at[0]] if at else S[held]
    W = wides

    def slot(name):
        return S[name]

    def remote(source, target, send, recv, peer):
        return pltpu.make_async_remote_copy(
            source, target, send, recv, device_id=peer, device_id_type=MESH
        )

    singles = dict(
        x=(x, W[0]), cot=(cot, W[1]), wo=(wo, slot("wo")), wq=(wq, slot("wq")),
        x_again=(x, W[3]), wq_again=(wq, slot("wq_again")), nt_again=(nt_o, slot("nt_again")),
    )
    load_at = {name: i for i, name in enumerate(singles)}

    def load(name):
        return pltpu.make_async_copy(*singles[name], in_sem.at[load_at[name]])

    def chunk_of(t):
        return lax.rem(z + t + 1, 4)

    def up_load(t):
        at = pl.multiple_of(chunk_of(t) * width, width)
        two = lax.rem(t, 2)
        return pltpu.make_async_copy(
            wup.at[:, pl.ds(at, width)], S["wu"].at[two], w_sem.at[two, 0]
        )

    def down_load(t):
        at = pl.multiple_of(chunk_of(t) * width, width)
        two = lax.rem(t, 2)
        return pltpu.make_async_copy(
            wdn.at[pl.ds(at, width), :], S["wd"].at[two], w_sem.at[two, 1]
        )

    def act_load(t):
        return pltpu.make_async_copy(ga_o.at[t], W[1], w_sem.at[2, 0])

    def act_save(t):
        return pltpu.make_async_copy(W[2 + t % 2], ga_o.at[t], w_sem.at[2, 1 + t % 2])

    load("x").start()
    rel_copy = pltpu.make_async_copy(rel_hbm, rel_table, out_sem.at[1])
    rel_copy.start()
    load("wq").start()
    load("cot").start()
    load("wo").start()
    down_load(0).start()
    down_load(1).start()
    up_load(0).start()

    barrier = pltpu.get_barrier_semaphore()
    peers = place_peers[1:] + z_peers[1:] + [x_peer]
    for peer in peers:
        pl.semaphore_signal(barrier, inc=1, device_id=peer, device_id_type=MESH)
    pl.semaphore_wait(barrier, len(peers))

    def slices(i):
        return S[("wk", "wv")[i]].reshape(4, 2, 2, part_rows, width)

    def gather_x(i):
        source = (wk, wv)[i].at[pl.ds(pl.multiple_of(me * part_rows, 16), part_rows), :]
        return remote(source, slices(i).at[z, y, c], gxs.at[i], gxr.at[i], x_peer)

    def gather_z(i, k):
        own = slices(i).at[z, y, c]
        return remote(own, own, gzs.at[i, k - 1], gzr.at[i, k - 1], z_peers[k])

    def gather_z_here(i, k):
        found = slices(i).at[lax.rem(z + 4 - k, 4), y, c]
        return remote(found, found, gzs.at[i, k - 1], gzr.at[i, k - 1], z_peers[k])

    def gather_y(i, mine=True):
        held = slices(i).at[:, y if mine else 1 - y, c]
        return remote(held, held, gys.at[i], gyr.at[i], y_peer)

    def gather_core(i, mine=True):
        held = slices(i).at[:, :, c if mine else 1 - c]
        return remote(held, held, gcs.at[i], gcr.at[i], core_peer)

    gather_x(0).start()
    gather_x(1).start()

    def far_rows(part):
        return remote(
            slot("nt").at[:, span_of(part)],
            slot("ft").at[:, span_of(part)],
            xsem.at[part],
            xrem.at[part],
            x_peer,
        )

    load("x").wait()

    @unrolled_third
    def _(part, span):
        plain, inverse = plain_norm(W[0][span, :])
        low = (plain * gains[0:1, :] + shifts[0:1, :]).astype(bf16)
        S["nt"][:, span] = low.T
        far_rows(part).start()

    pltpu.make_async_copy(slot("nt"), nt_o, out_sem.at[2]).start()

    page_row = pages[...].astype(f32)
    side = st.astype(f32)
    valid_row = jnp.maximum(side, jnp.where(page_row < PAGES - 0.5, 1.0, 0.0))
    page_rows = [jnp.where(page_row == p, 1.0, 0.0) for p in range(PAGES)]
    for p in range(PAGES):
        page_low[p] = jnp.broadcast_to(page_rows[p], (size, slots)).astype(bf16)
    page_col[...] = jnp.broadcast_to(page_row, (128, slots)).T
    cell = lax.broadcasted_iota(jnp.int32, (GRID, third), 0)
    spot = lax.broadcasted_iota(jnp.int32, (GRID, third), 1)
    spot_first = jnp.where(lax.rem(spot, GRID) == cell, 1.0, 0.0)
    spot_second = jnp.where(lax.div(spot, GRID) == cell, 1.0, 0.0)
    spot_once = stack([spot_first, spot_second]).astype(bf16)
    spot_twice = stack([spot_once, spot_once])
    buckets = rel_table.shape[2] // 2
    radius = (buckets - 1) // 2
    toward = 1 - 2 * st
    cell = lax.broadcasted_iota(jnp.int32, (GRID, slots), 0)
    offsets = [
        jnp.clip(toward * (boxes[axis : axis + 1, :] - cell), -radius, radius) + radius
        for axis in range(2)
    ]

    rel_copy.wait()

    def bias_rows(head, carry):
        exact = []
        for axis in range(2):
            total = jnp.zeros((GRID, slots), f32)
            for bucket in range(buckets):
                total = jnp.where(
                    offsets[axis] == bucket, rel_table[head, 0, axis * buckets + bucket], total
                )
            total = total * LOG2E
            if axis == 0:
                total = jnp.where(page_row > PAGES - 0.5, masked_fill, total)
            exact.append(total)
        exact = stack(exact)
        high = exact.astype(bf16)
        bias[head, : 2 * GRID, :] = high
        bias[head, 2 * GRID :, :] = (exact - high.astype(f32)).astype(bf16)
        return carry

    lax.fori_loop(0, heads, bias_rows, 0)

    load("wq").wait()

    @unrolled_third
    def _(part, span):
        found = dot(S["wq"][:, span], S["nt"][...], "tn")
        S["q_t"][span, :] = (found * (LOG2E * size**-0.5)).astype(bf16)

    sums_o[...] = jnp.zeros_like(sums_o)
    late_o[...] = jnp.zeros_like(late_o)
    for i in range(2):
        gather_x(i).wait()
        for k in (1, 2, 3):
            gather_z(i, k).start()

    load("cot").wait()

    @unrolled_third
    def _(part, span):
        low = W[1][span, :].astype(bf16)
        S["g2"][span, :] = low
        sums_o[4:5, :] += jnp.sum(low.astype(f32), axis=0, keepdims=True)

    for t in range(4):
        down_load(t).wait()
        if t > 1:
            act_save(t - 2).wait()

        @unrolled_third
        def _(part, span):
            W[2 + t % 2][span, :] = dot(S["g2"][span, :], S["wd"][t % 2], "nt")

        act_save(t).start()
        down_load((t + 2) % 4).start()
        if t < 2:
            for k in (1, 2, 3):
                gather_z(t, k).wait_send()
                gather_z_here(t, k).wait_recv()
            gather_y(t).start()

    for i in range(2):
        gather_y(i).wait_send()
        gather_y(i, False).wait_recv()
        gather_core(i).start()

    for i, (weight, result) in enumerate((("wk", "k_t"), ("wv", "v_t"))):
        gather_core(i).wait_send()
        gather_core(i, False).wait_recv()

        @unrolled_third
        def _(part, span):
            if i == 0:
                far_rows(part).wait()
            S[result][:, span] = dot(S[weight][...], S["ft"][:, span], "tn").astype(bf16)

    act_save(2).wait()
    act_save(3).wait()
    act_load(0).start()

    def by_page(name, rows):
        return [S[name][rows, cols] for cols in thirds]

    def masked(name, rows):
        held = S[name][rows, :]
        return [held * page_low[p] for p in range(PAGES)]

    def fold(found):
        total = found[:size] * page_rows[0]
        for p in range(1, PAGES):
            total = total + found[p * size : (p + 1) * size] * page_rows[p]
        return total

    def column(p):
        return page_col[...] == p

    def spread(rows):
        middle, last = [jnp.concatenate([column(p)] * 2, axis=1) for p in (1, 2)]
        return jnp.where(middle, rows[1], jnp.where(last, rows[2], rows[0]))

    def rows_of(head):
        return pl.ds(pl.multiple_of(head * size, size), size)

    def in_pairs(step):
        def several(i, carry):
            for j in range(TOGETHER):
                step(TOGETHER * i + j, carry)
            return carry

        lax.fori_loop(0, heads // TOGETHER, several, 0)

    def text_forward(head, carry):
        rows = rows_of(head)
        scores = dot(
            stack(by_page("k_t", rows) + [spot_twice]),
            stack(masked("q_t", rows) + [bias[head]]),
            "tn",
        )
        top = jnp.max(scores, axis=0, keepdims=True)
        weight = jnp.exp2(scores - top).astype(bf16)
        found = dot(stack(by_page("v_t", rows) + [jnp.ones((16, third), bf16)]), weight)
        total = found[PAGES * size : PAGES * size + 1]
        S["att"][rows, :] = (fold(found) * (valid_row / total)).astype(bf16)
        lse[head] = top + jnp.log2(total)
        return carry

    def vision_forward(head, carry):
        rows = rows_of(head)
        scores = dot(
            stack(masked("k_t", rows) + [bias[head]]),
            stack(by_page("q_t", rows) + [spot_twice]),
            "tn",
        )
        tops = []
        for p in range(PAGES):
            inside = jnp.concatenate([column(p)] * 2, axis=1)
            tops.append(
                jnp.max(jnp.where(inside, scores, 2.0 * masked_fill), axis=0, keepdims=True)
            )
        weight = jnp.exp2(scores - spread(tops)).astype(bf16)
        counts = [page_low[p, :1, :] for p in range(PAGES)]
        counts = stack(counts + [jnp.zeros((16 - PAGES, slots), bf16)])
        found = dot(stack(masked("v_t", rows) + [counts]), weight)
        for p, cols in enumerate(thirds):
            total = found[PAGES * size + p : PAGES * size + p + 1]
            S["att"][rows, cols] = (found[p * size : (p + 1) * size] / total).astype(bf16)
            lse[head, :, cols] = tops[p] + jnp.log2(total)
        return carry

    @pl.when(st == 0)
    def _():
        in_pairs(text_forward)

    @pl.when(st == 1)
    def _():
        in_pairs(vision_forward)

    def down_view(at):
        return at.reshape(2, 2, width // 4, width)

    def rest_view(at):
        return at.reshape(4, 2, 2, part_rows, width)

    def add_low(left, right):
        return left + right

    def core_down(t):
        at = S["sd"].at[lax.rem(t, 2)]
        return remote(down_view(at).at[:, 1 - c], cd.at[t], csem.at[t], crem.at[t], core_peer)

    def core_rest(p, at):
        return remote(
            rest_view(at).at[:, :, 1 - c], cr.at[p], csem.at[4 + p], crem.at[4 + p], core_peer
        )

    def y_down(t):
        return remote(cd.at[t, 1 - y], yd.at[t], ysem.at[t], yrem.at[t], y_peer)

    def y_rest(p):
        return remote(cr.at[p, :, 1 - y], yr.at[p], ysem.at[4 + p], yrem.at[4 + p], y_peer)

    def z_down(t):
        return remote(yd.at[t], zd.at[t], zsem.at[0, t], zrem.at[0, t], z_peers[t + 1])

    def z_rest(p, i):
        q = chunk_of(p) if p < 4 else p
        return remote(
            yr.at[p, z_at[i]], zr.at[q, i - 1], zsem.at[1 + p, i - 1], zrem.at[1 + q, i - 1], z_peers[i]
        )

    def z_here(q, i):
        return remote(
            yr.at[q, z_at[i]], zr.at[q, i - 1], zsem.at[1 + q, i - 1], zrem.at[1 + q, i - 1], z_peers[i]
        )

    def after_core_down(t):
        core_down(t).wait()
        held = down_view(S["sd"].at[lax.rem(t, 2)])

        def part(i, carry):
            rows = pl.ds(pl.multiple_of(lax.rem(i, 2) * (2 * part_rows), 16), 2 * part_rows)
            j = lax.div(i, 2)
            cd[t, j, rows] = add_low(cd[t, j, rows], held[j, c, rows])
            return carry

        lax.fori_loop(0, 4, part, 0)
        y_down(t).start()

    def after_core(p, at):
        core_rest(p, at).wait()
        held = rest_view(at)

        def part(i, carry):
            cr[p, i] = add_low(cr[p, i], held[i, :, c])
            return carry

        lax.fori_loop(0, 4, part, 0)
        y_rest(p).start()

    def after_y_down(t):
        y_down(t).wait()

        def part(i, carry):
            rows = pl.ds(pl.multiple_of(i * (2 * part_rows), 16), 2 * part_rows)
            yd[t, rows] = add_low(yd[t, rows], cd[t, y, rows])
            return carry

        lax.fori_loop(0, 2, part, 0)
        if t < 3:
            z_down(t).start()

    def after_y(p):
        y_rest(p).wait()

        def part(i, carry):
            yr[p, i] = add_low(yr[p, i], cr[p, i, y])
            return carry

        lax.fori_loop(0, 4, part, 0)
        for i in (1, 2, 3):
            z_rest(p, i).start()

    def end_down():
        total = yd[3].astype(f32)
        for t in range(3):
            z_down(t).wait()
            total = total + zd[t].astype(f32)
        down_o[...] = total

    def end_rest(q):
        held = lax.rem(q - z + 3, 4) if q < 4 else q
        total = yr[held, z].astype(f32)
        for i in (1, 2, 3):
            z_here(q, i).wait()
            total = total + zr[q, i - 1].astype(f32)
        return total

    def exchange(mine, found, send, recv, peers, at, start):
        for k in (1, 2, 3):
            copy = remote(mine, found.at[at[0]], send.at[k - 1], recv.at[k - 1], peers[k])
            if start:
                copy.start()
            else:
                copy.wait_send()
                there = lax.rem(at[0] + 4 - k, 4)
                remote(mine, found.at[there], send.at[k - 1], recv.at[k - 1], peers[k]).wait_recv()
        if not start:
            found[at[0]] = mine[...]
            mine[...] = ((found[0] + found[1]) + found[2]) + found[3]

    def small_sums(stage, start):
        peers, at = ((place_peers, place_at), (z_peers, z_at))[stage]
        exchange(sums_o, sums_in.at[stage], asem.at[stage], arem.at[stage], peers, at, start)

    def small_table(stage, start):
        peers, at = ((place_peers, place_at), (z_peers, z_at))[stage]
        exchange(table_o, table_in.at[stage], bsem.at[stage], brem.at[stage], peers, at, start)

    pltpu.make_async_copy(slot("nt"), nt_o, out_sem.at[2]).wait()
    load("wo").wait()

    @unrolled_third
    def _(part, span):
        middle = W[0][span, :] + dot(S["att"][:, span], S["wo"][...], "tn")
        W[0][span, :] = middle
        W[2][span, :] = middle + down_bias[...]
        W[3][span, :] = jnp.zeros((third, width), f32)
        plain, inverse = plain_norm(middle)
        S["n2"][span, :] = (plain * gains[1:2, :] + shifts[1:2, :]).astype(bf16)

    def feed(t, carry):
        two = lax.rem(t, 2)
        at = chunk_of(t)
        up_load(t).wait()
        down_load(t).wait()
        act_load(t).wait()

        @pl.when(t < 3)
        def _():
            up_load(t + 1).start()

            @pl.when(t > 0)
            def _():
                down_load(t + 1).start()

        w_u = S["wu"].at[two]
        w_d = S["wd"].at[two]

        @unrolled_third
        def _(part, cols):
            pre = dot(S["n2"][...], w_u[:, cols]) + up_bias[at, :, cols]
            square = pre * pre
            gate = jnp.tanh(pre * (GELU_IN + (GELU_IN * GELU_CUBE) * square))
            gate_half = 0.5 + 0.5 * gate
            act = (pre * gate_half).astype(bf16)
            S["act"][:, cols] = act
            S["sd"][two, cols, :] = dot(act, S["g2"][...], "tn").astype(bf16)
            slope = pre * (GELU_IN + (3.0 * GELU_IN * GELU_CUBE) * square)
            grad_act = W[1][:, cols]
            grad_pre = (grad_act * (gate_half * (1.0 + (1.0 - gate) * slope))).astype(bf16)
            S["gp"][:, cols] = grad_pre
            sums_o[pl.ds(5 + at, 1), cols] = jnp.sum(grad_pre.astype(f32), axis=0, keepdims=True)

        @pl.when(t < 3)
        def _():
            act_load(t + 1).start()

        @pl.when(t == 3)
        def _():
            load("cot").start()

        core_down(t).start()

        @unrolled_third
        def _(part, cols):
            S["sr"][two, :, cols] = dot(S["n2"][...], S["gp"][:, cols], "tn").astype(bf16)

        core_rest(t, S["sr"].at[two]).start()
        after_core_down(t)

        @pl.when(t > 0)
        def _():
            after_core(t - 1, S["sr"].at[1 - two])

        @unrolled_third
        def _(part, span):
            W[2][span, :] = W[2][span, :] + dot(S["act"][span, :], w_d[...])
            W[3][span, :] = W[3][span, :] + dot(S["gp"][span, :], w_u[...], "nt")

        @pl.when(t == 2)
        def _():
            after_y_down(0)

        @pl.when(t == 3)
        def _():
            after_y(0)

        return carry

    lax.fori_loop(0, 4, feed, 0)
    after_core(3, S["sr1"])
    after_y_down(1)
    load("cot").wait()

    pltpu.make_async_copy(W[2], block_o, out_sem.at[0]).start()

    @unrolled_third
    def _(part, span):
        plain, inverse = plain_norm(W[0][span, :])
        grad_two = W[3][span, :]
        sums_o[1:2, :] += jnp.sum(grad_two * plain, axis=0, keepdims=True)
        sums_o[3:4, :] += jnp.sum(grad_two, axis=0, keepdims=True)
        middle = W[1][span, :] + norm_backward(grad_two, plain, inverse, gains[1:2, :])
        W[0][span, :] = middle
        S["gm"][span, :] = middle.astype(bf16)

    load("x_again").start()
    load("wq_again").start()
    load("nt_again").start()

    @unrolled_third
    def _(part, rows):
        grad_att = (dot(S["wo"][rows, :], S["gm"][...], "nt") * valid_row).astype(bf16)
        S["go"][rows, :] = grad_att
        both = S["att"][rows, :].astype(f32) * grad_att.astype(f32)
        delta[pl.ds(4 * part, 4)] = jnp.sum(both.reshape(4, size, slots), axis=1, keepdims=True)

    after_y(1)

    def table_rows(head, found):
        for axis in range(2):
            here = found[axis * GRID : (axis + 1) * GRID]
            for bucket in range(buckets):
                kept = jnp.where(offsets[axis] == bucket, here, 0.0)
                cells[pl.ds(head * 16 + axis * buckets + bucket, 1), :] = jnp.sum(
                    kept, axis=0, keepdims=True
                )

    def text_backward(head, carry):
        rows = rows_of(head)
        keys = by_page("k_t", rows)
        queries = masked("q_t", rows)
        grads = stack(masked("go", rows))
        scores = dot(stack(keys + [spot_twice]), stack(queries + [bias[head]]), "tn")
        prob = jnp.exp2(scores - lse[head])
        grad_prob = dot(stack(by_page("v_t", rows)), grads, "tn")
        grad_score = (prob * (grad_prob - delta[head])).astype(bf16)
        found = dot(grads, prob.astype(bf16), "nt")
        for p, cols in enumerate(thirds):
            S["dv"][rows, cols] = found[p * size : (p + 1) * size].astype(bf16)
        found = dot(stack(queries), grad_score, "nt") * LN2
        for p, cols in enumerate(thirds):
            S["dk"][rows, cols] = found[p * size : (p + 1) * size].astype(bf16)
        found = dot(stack(keys + [spot_once]), grad_score)
        S["dq"][rows, :] = (fold(found) * size**-0.5).astype(bf16)
        table_rows(head, found[PAGES * size :])
        return carry

    def vision_backward(head, carry):
        rows = rows_of(head)
        keys = masked("k_t", rows)
        queries = by_page("q_t", rows)
        grads = stack(by_page("go", rows))
        scores = dot(stack(keys + [bias[head]]), stack(queries + [spot_twice]), "tn")
        prob = jnp.exp2(scores - spread([lse[head, :, cols] for cols in thirds]))
        grad_prob = dot(stack(masked("v_t", rows)), grads, "tn")
        inner = spread([delta[head, :, cols] for cols in thirds])
        grad_score = (prob * (grad_prob - inner)).astype(bf16)
        S["dv"][rows, :] = fold(dot(grads, prob.astype(bf16), "nt")).astype(bf16)
        found = dot(stack(queries + [spot_once]), grad_score, "nt")
        S["dk"][rows, :] = (fold(found) * LN2).astype(bf16)
        table_rows(head, found[PAGES * size :])
        found = dot(stack(keys), grad_score) * size**-0.5
        for p, cols in enumerate(thirds):
            S["dq"][rows, cols] = found[p * size : (p + 1) * size].astype(bf16)
        return carry

    cells[...] = jnp.zeros_like(cells)

    @pl.when(st == 0)
    def _():
        in_pairs(text_backward)

    @pl.when(st == 1)
    def _():
        in_pairs(vision_backward)

    after_y_down(2)

    load("x_again").wait()
    base = heads * 16
    cells[base + 2 : base + 3, :] = valid_row

    @unrolled_third
    def _(part, span):
        block = W[2][span, :]
        own = jnp.maximum(side, jnp.where(page_col[span, 0:1] < PAGES - 0.5, 1.0, 0.0))
        sub = block - W[3][span, :]
        cells[base : base + 1, :] += jnp.sum(own * block * block, axis=0, keepdims=True)
        cells[base + 1 : base + 2, :] += jnp.sum(own * sub * sub, axis=0, keepdims=True)

    table_o[...] = lax.dot_general(
        jnp.ones((8, width), f32),
        cells[...],
        (((1,), (1,)), ((), ())),
        preferred_element_type=f32,
        precision=lax.Precision.HIGHEST,
    )

    small_sums(0, True)
    small_table(0, True)

    def back_rows(part):
        return remote(
            slot("send").at[:, span_of(part)],
            slot("back").at[:, span_of(part)],
            xsem.at[3 + part],
            xrem.at[3 + part],
            x_peer,
        )

    @unrolled_third
    def _(part, cols):
        S["send"][:, cols] = (
            dot(S["wk"][...], S["dk"][:, cols])
            + dot(S["wv"][...], S["dv"][:, cols])
        ).astype(bf16)
        back_rows(part).start()


    @unrolled_third
    def _(part, span):
        S["so"][span, :] = dot(S["att"][span, :], S["gm"][...]).astype(bf16)

    core_rest(4, S["so"]).start()
    after_y(2)

    @unrolled_third
    def _(part, span):
        S["sk"][span, :] = dot(S["ft"][span, :], S["dk"][...], "nt").astype(
            bf16
        )

    core_rest(5, S["sk"]).start()
    after_core(4, S["so"])

    @unrolled_third
    def _(part, span):
        S["sv"][span, :] = dot(S["ft"][span, :], S["dv"][...], "nt").astype(
            bf16
        )

    core_rest(6, S["sv"]).start()
    after_core(5, S["sk"])
    load("nt_again").wait()

    @unrolled_third
    def _(part, span):
        S["sq"][span, :] = dot(S["nt_again"][span, :], S["dq"][...], "nt").astype(
            bf16
        )

    core_rest(7, S["sq"]).start()
    after_core(6, S["sv"])
    load("wq_again").wait()

    @unrolled_third
    def _(part, span):
        W[1][span, :] = dot(S["wq_again"][span, :], S["dq"][...])

    after_core(7, S["sq"])
    after_y_down(3)

    def last_small(stage, start):
        peers, at = ((place_peers, place_at), (z_peers, z_at))[stage]
        exchange(late_o, late_in.at[stage], lsem.at[stage], lrem.at[stage], peers, at, start)

    table_swap = remote(table_o, table_far, tsem, trem, x_peer)

    def hop_copy(i):
        return remote(hop.at[i], hop_in.at[i], hsem.at[i], hrem.at[i], x_peer)

    after_y(3)
    pltpu.make_async_copy(W[2], block_o, out_sem.at[0]).wait()

    @each_third
    def _(part, span):
        back_rows(part).wait()
        grad_one = (W[1][:, span] + S["back"][:, span].astype(f32)).T
        plain, inverse = plain_norm(W[3][span, :])
        late_o[0:1, :] += jnp.sum(grad_one * plain, axis=0, keepdims=True)
        late_o[1:2, :] += jnp.sum(grad_one, axis=0, keepdims=True)
        W[2][span, :] = W[0][span, :] + norm_backward(
            grad_one, plain, inverse, gains[0:1, :]
        )

        @pl.when(part == 0)
        def _():
            small_sums(0, False)
            small_sums(1, True)
            small_table(0, False)
            small_table(1, True)

        @pl.when(part == 1)
        def _():
            after_y(4)

    pltpu.make_async_copy(W[2], grad_o, out_sem.at[1]).start()
    last_small(0, True)
    after_y(5)
    end_down()
    for q in range(4):
        up_o[:, q * width : (q + 1) * width] = end_rest(q)
    after_y(6)
    last_small(0, False)
    last_small(1, True)
    wo_o[...] = end_rest(4)
    hop[0] = end_rest(5).astype(bf16)
    hop_copy(0).start()
    after_y(7)
    small_sums(1, False)
    small_table(1, False)
    table_swap.start()
    last_small(1, False)
    hop[1] = end_rest(6).astype(bf16)
    hop_copy(1).start()
    wq_o[...] = end_rest(7)
    table_swap.wait()
    lane = lax.broadcasted_iota(jnp.int32, table_o.shape, 1)
    table_o[...] = table_o[...] + jnp.where(lane >= base, table_far[...], 0.0)
    for i in range(2):
        hop_copy(i).wait()
        hop_o[i] = hop_in[i].astype(f32)
    pltpu.make_async_copy(W[2], grad_o, out_sem.at[1]).wait()


def hand_over(
    block, grad_in, down, up, out, query, hop, sums, late, table,
    block_o, grad_o, gains_o, shifts_o, query_o, key_o, value_o, out_o, up_o, up_bias_o, down_o, down_bias_o, table_o, stats_o,
    held, down_h, up_h, out_h, query_h, hop_h, sums_h, late_h, table_h, in_sem, out_sem, sem,
):
    slots, width = block.shape
    step = slots // 4
    moves = []
    for i, (source, target) in enumerate(((block, block_o), (grad_in, grad_o))):
        for j in range(4):
            span = pl.ds(j * step, step)
            moves.append(
                (
                    pltpu.make_async_copy(
                        source.at[span, :], held.at[i, span, :], in_sem.at[i, j]
                    ),
                    pltpu.make_async_copy(
                        held.at[i, span, :], target.at[span, :], out_sem.at[i, j]
                    ),
                )
            )
    for move in moves:
        move[0].start()
    small = ((down, down_h), (up, up_h), (out, out_h), (query, query_h), (hop, hop_h), (sums, sums_h), (late, late_h), (table, table_h))
    small = [pltpu.make_async_copy(*pair, sem.at[i]) for i, pair in enumerate(small)]
    for copy in small:
        copy.start()
    for copy in small:
        copy.wait()
    up_o[...] = up_h[...]
    down_o[...] = down_h[...]
    gains_o[0:1, :] = late_h[0:1, :]
    gains_o[1:2, :] = sums_h[1:2, :]
    shifts_o[0:1, :] = late_h[1:2, :]
    shifts_o[1:2, :] = sums_h[3:4, :]
    down_bias_o[...] = sums_h[4:5, :]
    for q in range(4):
        up_bias_o[:, q * width : (q + 1) * width] = sums_h[5 + q : 6 + q, :]
    query_o[...] = query_h[...]
    key_o[...] = hop_h[0]
    value_o[...] = hop_h[1]
    out_o[...] = out_h[...]
    heads, _, rows = table_o.shape
    for head in range(heads):
        table_o[head] = table_h[0:1, head * 16 : head * 16 + rows]
    total = table_h[0:1, heads * 16 : heads * 16 + 2]
    count = table_h[0:1, heads * 16 + 2 : heads * 16 + 3]
    stats_o[...] = jnp.sqrt(total / (count * width))
    for move in moves:
        move[0].wait()
        move[1].start()
    for move in moves:
        move[1].wait()


def on_device(
    inputs,
    text_pages,
    text_boxes,
    norm_gains,
    norm_shifts,
    w_query,
    w_key,
    w_value,
    w_out,
    w_up,
    up_bias,
    w_down,
    down_bias,
    box_table,
    cotangent,
):
    slots, width = inputs.shape[2:]
    rel_rows, heads = box_table.shape[1:]
    size = width // heads
    part = width // 16
    shape = lambda *dims: jax.ShapeDtypeStruct(dims, f32)
    vmem = pl.BlockSpec(memory_space=pltpu.VMEM)
    hbm = pl.BlockSpec(memory_space=pl.ANY)
    dma = pltpu.SemaphoreType.DMA
    cell_rows = heads * 16 + 16
    low = lambda *dims: pltpu.VMEM(dims, bf16)
    full = lambda *dims: pltpu.VMEM(dims, f32)
    block, grad_in, _, _, down, up, out, query, hop, sums, late, table = pl.pallas_call(
        layer_kernel,
        out_shape=[
            shape(slots, width),
            shape(slots, width),
            jax.ShapeDtypeStruct((width, slots), bf16),
            shape(4, slots, width),
            shape(4 * part, width),
            shape(part, 4 * width),
            shape(part, width),
            shape(part, width),
            shape(2, part, width),
            shape(16, width),
            shape(8, width),
            shape(8, cell_rows),
        ],
        in_specs=[hbm] * 8 + [vmem] * 6 + [hbm],
        out_specs=[hbm] * 4 + [vmem] * 8,
        scratch_shapes=[
            [low(slots, width)] * (len(NAMES) - RINGS) + [low(2, slots, width)] * RINGS,
            [full(slots, width)] * 4,
            pltpu.SMEM((heads, 1, rel_rows), f32),
            low(heads, 4 * GRID, slots),
            full(heads, 1, slots),
            full(heads, 1, slots),
            low(PAGES, size, slots),
            full(slots, 128),
            full(cell_rows, width),
            low(4, 2, 4 * part, width),
            low(8, 4, 2, part, width),
            low(4, 4 * part, width),
            low(8, 4, part, width),
            low(3, 4 * part, width),
            low(8, 3, part, width),
            low(2, part, width),
            low(2, part, width),
            full(2, 4, 16, width),
            full(2, 4, 8, width),
            full(2, 4, 8, cell_rows),
            full(8, cell_rows),
            dma((7,)),
            dma((3, 3)),
            dma((3,)),
            dma((12,)),
            dma((12,)),
            dma((12,)),
            dma((12,)),
            dma((9, 3)),
            dma((9, 3)),
            dma((6,)),
            dma((6,)),
            dma((2,)),
            dma((2,)),
            dma((2, 3)),
            dma((2, 3)),
            dma((2, 3)),
            dma((2, 3)),
            dma((2, 3)),
            dma((2, 3)),
            dma,
            dma,
            dma((2,)),
            dma((2,)),
            dma((2, 3)),
            dma((2, 3)),
            dma((2,)),
            dma((2,)),
            dma((2,)),
            dma((2,)),
        ],
        compiler_params=pltpu.CompilerParams(
            collective_id=0, has_side_effects=True, vmem_limit_bytes=61 * 2**20
        ),
        name="layer",
    )(
        inputs[0, 0],
        cotangent[0, 0],
        w_query[0],
        w_key[0],
        w_value[0],
        w_out[0],
        w_up[0],
        w_down[0],
        up_bias.reshape(4, 1, width),
        down_bias,
        norm_gains[0],
        norm_shifts[0],
        text_pages,
        text_boxes[0],
        box_table.transpose(2, 0, 1),
    )
    outs = pl.pallas_call(
        hand_over,
        out_shape=[
            shape(slots, width),
            shape(slots, width),
            shape(2, width),
            shape(2, width),
            shape(part, width),
            shape(part, width),
            shape(part, width),
            shape(part, width),
            shape(part, 4 * width),
            shape(1, 4 * width),
            shape(4 * part, width),
            shape(1, width),
            shape(heads, 1, rel_rows),
            shape(1, 2),
        ],
        in_specs=[hbm] * 10,
        out_specs=[hbm] * 2 + [vmem] * 12,
        scratch_shapes=[
            full(2, slots, width),
            full(4 * part, width),
            full(part, 4 * width),
            full(part, width),
            full(part, width),
            full(2, part, width),
            full(16, width),
            full(8, width),
            full(8, cell_rows),
            dma((2, 4)),
            dma((2, 4)),
            dma((8,)),
        ],
        compiler_params=pltpu.CompilerParams(vmem_limit_bytes=61 * 2**20),
        name="hand_over",
    )(block, grad_in, down, up, out, query, hop, sums, late, table)
    block, grad_in, gains, shifts, query, key, value, out, up, up_b, down, down_b, table, stats = outs
    return (
        block[None, None],
        grad_in[None, None],
        gains[None],
        shifts[None],
        query[None],
        key[None],
        value[None],
        out[None],
        up[None],
        up_b,
        down[None],
        down_b,
        table.transpose(1, 2, 0),
        stats[0],
    )


def partner(block, axis, bit):
    count = lax.axis_size(axis)
    route = []
    for low in range(count):
        high = low | 1 << bit
        if high != low and high < count:
            route += [(low, high), (high, low)]
    return lax.ppermute(block, axis, route)


def norm_forward(values, gain_row, shift_row):
    center = values - jnp.mean(values, axis=-1, keepdims=True)
    inverse = lax.rsqrt(jnp.mean(center * center, axis=-1, keepdims=True) + 1e-05)
    normal_part = center * inverse
    return (normal_part * gain_row + shift_row, normal_part, inverse)


def general_norm_backward(grad_normed, normal_part, inverse, gain_row):
    scaled = grad_normed * gain_row
    first_mean = jnp.mean(scaled, axis=-1, keepdims=True)
    second_mean = jnp.mean(scaled * normal_part, axis=-1, keepdims=True)
    return inverse * (scaled - first_mean - normal_part * second_mean)


def bucket_offset(own_coord, far_coord, bucket_count):
    radius = (bucket_count - 1) // 2
    return jnp.clip(own_coord[:, None] - far_coord[None, :], -radius, radius) + radius


def bias_from(rel_table, offset):
    result = jnp.zeros((rel_table.shape[1],) + offset.shape, f32)
    for bucket in range(rel_table.shape[0]):
        result = (
            result + rel_table[bucket][:, None, None] * (offset == bucket).astype(f32)[None]
        )
    return result


def bias_grad(grad_wide, offset, bucket_count):
    return jnp.stack(
        [
            jnp.sum(grad_wide * (offset == bucket).astype(f32)[None], axis=(1, 2))
            for bucket in range(bucket_count)
        ]
    )


def project(left, right):
    return jnp.einsum("rsd,de->rse", left, right, preferred_element_type=f32)


def weight_grad(left, right):
    return jnp.einsum("rsd,rse->de", left, right, preferred_element_type=f32)


def back_project(grad_low, weight):
    return jnp.einsum("rse,de->rsd", grad_low, weight, preferred_element_type=f32)


def general_device(
    inputs,
    text_pages,
    text_boxes,
    norm_gains,
    norm_shifts,
    w_query,
    w_key,
    w_value,
    w_out,
    w_up,
    up_bias,
    w_down,
    down_bias,
    box_table,
    cotangent,
):
    slot_count = inputs.shape[2]
    model_width = inputs.shape[3]
    head_count = box_table.shape[2]
    head_size = model_width // head_count
    bucket_count = box_table.shape[1] // 2
    score_scale = head_size ** (-0.5)
    is_text = lax.axis_index("stream") == 0
    positions = jnp.arange(slot_count, dtype=jnp.int32)
    cell_index = positions % (GRID * GRID)
    vision_page = positions // (GRID * GRID)
    vision_first = cell_index % GRID
    vision_second = cell_index // GRID
    own_valid = jnp.where(is_text, text_pages < PAGES, True).astype(f32)
    gain_rows = norm_gains[0]
    shift_rows = norm_shifts[0]
    rel_table = box_table[0]
    block_in = inputs[:, 0]
    normed_one, plain_one, inverse_one = norm_forward(block_in, gain_rows[0], shift_rows[0])
    normed_low = normed_one.astype(bf16)
    query = project(normed_low, w_query[0]).astype(bf16)
    own_keys = project(normed_low, w_key[0]).astype(bf16)
    own_values = project(normed_low, w_value[0]).astype(bf16)
    far_keys, far_values = partner((own_keys, own_values), "stream", 0)

    def geometry(row_index):
        text_page = text_pages[row_index]
        own_page = jnp.where(is_text, text_page, vision_page)
        far_page = jnp.where(is_text, vision_page, text_page)
        own_first = jnp.where(is_text, text_boxes[row_index, 0], vision_first)
        far_first = jnp.where(is_text, vision_first, text_boxes[row_index, 0])
        own_second = jnp.where(is_text, text_boxes[row_index, 1], vision_second)
        far_second = jnp.where(is_text, vision_second, text_boxes[row_index, 1])
        allowed = (own_page[:, None] == far_page[None, :]) | (own_page[:, None] == PAGES)
        return (
            allowed,
            bucket_offset(own_first, far_first, bucket_count),
            bucket_offset(own_second, far_second, bucket_count),
        )

    def heads_of(matrix):
        return matrix.reshape(slot_count, head_count, head_size)

    def score_block(row_index, allowed, offset_first, offset_second):
        raw = (
            jnp.einsum(
                "ihd,jhd->hij",
                heads_of(query[row_index]),
                heads_of(far_keys[row_index]),
                preferred_element_type=f32,
            )
            * score_scale
        )
        raw = (
            raw
            + bias_from(rel_table[:bucket_count], offset_first)
            + bias_from(rel_table[bucket_count:], offset_second)
        )
        return jnp.where(allowed[None], raw, masked_fill)

    row_index = 0
    allowed, offset_first, offset_second = geometry(row_index)
    masked = score_block(row_index, allowed, offset_first, offset_second)
    top_score = jnp.max(masked, axis=-1, keepdims=True)
    exp_scores = jnp.exp(masked - top_score)
    row_total = jnp.sum(exp_scores, axis=-1, keepdims=True)
    prob_low = (exp_scores / row_total).astype(bf16)
    attended = jnp.einsum(
        "hij,jhd->ihd",
        prob_low,
        heads_of(far_values[row_index]),
        preferred_element_type=f32,
    ).reshape(slot_count, model_width)
    attended_rows = [(attended * own_valid[row_index][:, None]).astype(bf16)]
    log_totals = [top_score + jnp.log(row_total)]
    attended_low = jnp.stack(attended_rows)
    branch_one = project(attended_low, w_out[0])
    middle = block_in + branch_one
    normed_two, plain_two, inverse_two = norm_forward(middle, gain_rows[1], shift_rows[1])
    normed_two_low = normed_two.astype(bf16)
    pre_act = project(normed_two_low, w_up[0]) + up_bias[0]
    act_low = jax.nn.gelu(pre_act).astype(bf16)
    branch_two = project(act_low, w_down[0]) + down_bias[0]
    block_out = middle + branch_two
    sublayer = branch_one + branch_two
    totals = lax.psum(
        (
            jnp.sum(own_valid * jnp.sum(block_out * block_out, axis=-1)),
            jnp.sum(own_valid * jnp.sum(sublayer * sublayer, axis=-1)),
            jnp.sum(own_valid),
        ),
        ("stream", "batch"),
    )
    denominator = totals[2] * model_width
    stats = jnp.stack([jnp.sqrt(totals[0] / denominator), jnp.sqrt(totals[1] / denominator)])
    grad_out = cotangent[:, 0]
    grad_out_low = grad_out.astype(bf16)
    grad_w_down = weight_grad(act_low, grad_out_low)
    grad_down_bias = jnp.sum(grad_out_low.astype(f32), axis=(0, 1))
    grad_act = back_project(grad_out_low, w_down[0])
    gelu_back = jax.vjp(jax.nn.gelu, pre_act)[1]
    grad_pre_low = gelu_back(grad_act)[0].astype(bf16)
    grad_w_up = weight_grad(normed_two_low, grad_pre_low)
    grad_up_bias = jnp.sum(grad_pre_low.astype(f32), axis=(0, 1))
    grad_normed_two = back_project(grad_pre_low, w_up[0])
    grad_gain_two = jnp.sum(grad_normed_two * plain_two, axis=(0, 1))
    grad_shift_two = jnp.sum(grad_normed_two, axis=(0, 1))
    grad_middle = grad_out + general_norm_backward(grad_normed_two, plain_two, inverse_two, gain_rows[1])
    grad_middle_low = grad_middle.astype(bf16)
    grad_w_out = weight_grad(attended_low, grad_middle_low)
    grad_attended = back_project(grad_middle_low, w_out[0]).astype(bf16) * own_valid[
        :, :, None
    ].astype(bf16)
    query_grad_rows, key_grad_rows, value_grad_rows = ([], [], [])
    row_index = 0
    allowed, offset_first, offset_second = geometry(row_index)
    masked = score_block(row_index, allowed, offset_first, offset_second)
    prob = jnp.exp(masked - log_totals[row_index])
    grad_heads = heads_of(grad_attended[row_index])
    grad_prob = jnp.einsum(
        "ihd,jhd->hij",
        grad_heads,
        heads_of(far_values[row_index]),
        preferred_element_type=f32,
    )
    inner_sum = jnp.sum(prob * grad_prob, axis=-1, keepdims=True)
    grad_score_low = (prob * (grad_prob - inner_sum)).astype(bf16)
    grad_score_wide = grad_score_low.astype(f32)
    grad_table = jnp.concatenate(
        [
            bias_grad(grad_score_wide, offset_first, bucket_count),
            bias_grad(grad_score_wide, offset_second, bucket_count),
        ],
        axis=0,
    )
    query_grad = (
        jnp.einsum(
            "hij,jhd->ihd",
            grad_score_low,
            heads_of(far_keys[row_index]),
            preferred_element_type=f32,
        )
        * score_scale
    )
    key_grad = (
        jnp.einsum(
            "hij,ihd->jhd",
            grad_score_low,
            heads_of(query[row_index]),
            preferred_element_type=f32,
        )
        * score_scale
    )
    value_grad = jnp.einsum(
        "hij,ihd->jhd", prob.astype(bf16), grad_heads, preferred_element_type=f32
    )
    query_grad_rows.append(query_grad.reshape(slot_count, model_width).astype(bf16))
    key_grad_rows.append(key_grad.reshape(slot_count, model_width).astype(bf16))
    value_grad_rows.append(value_grad.reshape(slot_count, model_width).astype(bf16))
    grad_query_low = jnp.stack(query_grad_rows)
    own_key_grad, own_value_grad = partner(
        (jnp.stack(key_grad_rows), jnp.stack(value_grad_rows)), "stream", 0
    )
    grad_w_query = weight_grad(normed_low, grad_query_low)
    grad_w_key = weight_grad(normed_low, own_key_grad)
    grad_w_value = weight_grad(normed_low, own_value_grad)
    grad_normed_one = (
        back_project(grad_query_low, w_query[0])
        + back_project(own_key_grad, w_key[0])
        + back_project(own_value_grad, w_value[0])
    )
    grad_gain_one = jnp.sum(grad_normed_one * plain_one, axis=(0, 1))
    grad_shift_one = jnp.sum(grad_normed_one, axis=(0, 1))
    grad_inputs = grad_middle + general_norm_backward(grad_normed_one, plain_one, inverse_one, gain_rows[0])
    big_sums = (
        lax.psum_scatter(grad_w_query, "batch", scatter_dimension=0, tiled=True),
        lax.psum_scatter(grad_w_key, "batch", scatter_dimension=0, tiled=True),
        lax.psum_scatter(grad_w_value, "batch", scatter_dimension=0, tiled=True),
        lax.psum_scatter(grad_w_out, "batch", scatter_dimension=0, tiled=True),
        lax.psum_scatter(grad_w_up, "batch", scatter_dimension=0, tiled=True),
        lax.psum_scatter(grad_w_down, "batch", scatter_dimension=0, tiled=True),
    )
    small_sums = lax.psum(
        (
            jnp.stack([grad_gain_one, grad_gain_two]),
            jnp.stack([grad_shift_one, grad_shift_two]),
            grad_up_bias,
            grad_down_bias,
            grad_table,
        ),
        "batch",
    )
    return (
        block_out[:, None],
        grad_inputs[:, None],
        small_sums[0][None],
        small_sums[1][None],
        big_sums[0][None],
        big_sums[1][None],
        big_sums[2][None],
        big_sums[3][None],
        big_sums[4][None],
        small_sums[2][None],
        big_sums[5][None],
        small_sums[3][None],
        small_sums[4][None],
        stats,
    )


def solution(mesh):
    sided = lambda dims: P("stream", *([None] * (dims - 1)))
    rows = P("batch", "stream", None, None)
    shard = P("stream", "batch", None)
    placed = (
        (rows, P("batch", None), P("batch", None, None), sided(3), sided(3))
        + (sided(3),) * 5
        + (sided(2), sided(3), sided(2), sided(3), rows)
    )
    fits = mesh.shape["batch"] == 16 and mesh.shape["stream"] == 2
    return jax.shard_map(
        on_device if fits else general_device,
        mesh=mesh,
        in_specs=placed,
        out_specs=(
            (rows, rows, sided(3), sided(3))
            + (shard,) * 5
            + (sided(2), shard, sided(2), sided(3), P())
        ),
        check_vma=False,
    )
```

```python
import jax
import jax.numpy as jnp
from jax import lax
from jax.experimental import pallas as pl
from jax.experimental.pallas import tpu as pltpu
from jax.sharding import PartitionSpec as P

GRID = 16
PAGES = 3
MESH = pl.DeviceIdType.MESH
LOG2E = 1.4426950408889634
LN2 = 0.6931471805599453
TOGETHER = 4
GELU_IN = 0.7978845608028654
GELU_CUBE = 0.044715
masked_fill = -1e30
f32 = jnp.float32
bf16 = jnp.bfloat16


def dot(left, right, form="nn"):
    dims = {"nn": (1, 0), "nt": (1, 1), "tn": (0, 0)}[form]
    return lax.dot_general(
        left, right, (((dims[0],), (dims[1],)), ((), ())), preferred_element_type=f32
    )


def stack(parts):
    return jnp.concatenate(parts, axis=0)


def plain_norm(values):
    center = values - jnp.mean(values, axis=-1, keepdims=True)
    inverse = lax.rsqrt(jnp.mean(center * center, axis=-1, keepdims=True) + 1e-05)
    return center * inverse, inverse


def norm_backward(grad_normed, plain, inverse, gain_row):
    scaled = grad_normed * gain_row
    first_mean = jnp.mean(scaled, axis=-1, keepdims=True)
    second_mean = jnp.mean(scaled * plain, axis=-1, keepdims=True)
    return inverse * (scaled - first_mean - plain * second_mean)


NAMES = (
    "ft", "wk", "wv", "back", "q_t", "k_t", "v_t", "att", "wo", "n2", "g2", "act", "gp",
    "wu", "wd", "sd", "sr",
)
RINGS = 4
SHARED = dict(
    nt=("n2",), wq=("act",), gm=("n2",), go=("g2",), dq=("wu", 0), dk=("wu", 1), dv=("wd", 0),
    send=("wd", 1), so=("sd", 0), sk=("sd", 1), sv=("sr", 0), sq=("sr", 1), sr1=("sr", 1),
    nt_again=("act",), wq_again=("gp",), sr0=("sr", 0),
)


def layer_kernel(
    x, cot, wq, wk, wv, wo, wup, wdn,
    up_bias, down_bias, gains, shifts, pages, boxes, rel_hbm,
    block_o, grad_o, nt_o, ga_o, down_o, up_o, wo_o, wq_o, hop_o, sums_o, late_o, table_o,
    buffers, wides, rel_table, bias, lse, delta, page_low, page_col, cells,
    cd, cr, yd, yr, zd, zr, hop, hop_in, sums_in, late_in, table_in, table_far,
    in_sem, w_sem, out_sem, csem, crem, ysem, yrem, zsem, zrem, xsem, xrem, hsem, hrem,
    asem, arem, bsem, brem, lsem, lrem, tsem, trem, gxs, gxr, gzs, gzr, gys, gyr, gcs, gcr,
):
    slots, width = x.shape
    heads = lse.shape[0]
    size = width // heads
    third = slots // 3
    thirds = [slice(part * third, (part + 1) * third) for part in range(3)]
    part_rows = width // 16
    st = lax.axis_index("stream")
    me = lax.axis_index("batch")
    c = lax.rem(me, 2)
    y = lax.rem(lax.div(me, 2), 2)
    z = lax.div(me, 4)
    place = lax.rem(me, 4)
    core_peer = (st, me + 1 - 2 * c)
    y_peer = (st, me + 2 - 4 * y)
    z_low = lax.rem(z, 2)
    z_high = lax.div(z, 2)
    one_peer = (st, me + 4 - 8 * z_low)
    two_peer = (st, me + 8 - 16 * z_high)
    z_at = [lax.rem(z + i, 4) for i in range(4)]
    z_peers = [(st, z_at[i] * 4 + place) for i in range(4)]
    place_at = [lax.rem(place + i, 4) for i in range(4)]
    place_peers = [(st, z * 4 + place_at[i]) for i in range(4)]
    x_peer = (1 - st, me)

    def span_of(j):
        return pl.ds(pl.multiple_of(j * third, third), third)

    def unrolled_third(step):
        for j in range(3):
            step(j, pl.ds(j * third, third))

    def each_third(step):
        def body(j, carry):
            step(j, span_of(j))
            return carry

        lax.fori_loop(0, 3, body, 0)

    S = dict(zip(NAMES, buffers))
    for name, (held, *at) in SHARED.items():
        S[name] = S[held].at[at[0]] if at else S[held]
    W = wides

    def slot(name):
        return S[name]

    def remote(source, target, send, recv, peer):
        return pltpu.make_async_remote_copy(
            source, target, send, recv, device_id=peer, device_id_type=MESH
        )

    singles = dict(
        x=(x, W[0]), cot=(cot, W[1]), wo=(wo, slot("wo")), wq=(wq, slot("wq")),
        x_again=(x, W[3]), wq_again=(wq, slot("wq_again")), nt_again=(nt_o, slot("nt_again")),
    )
    load_at = {name: i for i, name in enumerate(singles)}

    def load(name):
        return pltpu.make_async_copy(*singles[name], in_sem.at[load_at[name]])

    def chunk_of(t):
        return lax.rem(z + t + 1, 4)

    def up_load(t):
        at = pl.multiple_of(chunk_of(t) * width, width)
        two = lax.rem(t, 2)
        return pltpu.make_async_copy(
            wup.at[:, pl.ds(at, width)], S["wu"].at[two], w_sem.at[two, 0]
        )

    def down_load(t):
        at = pl.multiple_of(chunk_of(t) * width, width)
        two = lax.rem(t, 2)
        return pltpu.make_async_copy(
            wdn.at[pl.ds(at, width), :], S["wd"].at[two], w_sem.at[two, 1]
        )

    def act_load(t):
        return pltpu.make_async_copy(ga_o.at[t], W[1], w_sem.at[2, 0])

    def act_save(t):
        return pltpu.make_async_copy(W[2 + t % 2], ga_o.at[t], w_sem.at[2, 1 + t % 2])

    load("x").start()
    rel_copy = pltpu.make_async_copy(rel_hbm, rel_table, out_sem.at[1])
    rel_copy.start()
    load("wq").start()
    load("cot").start()
    load("wo").start()
    down_load(0).start()
    down_load(1).start()
    up_load(0).start()

    barrier = pltpu.get_barrier_semaphore()
    peers = place_peers[1:] + z_peers[1:] + [x_peer]
    for peer in peers:
        pl.semaphore_signal(barrier, inc=1, device_id=peer, device_id_type=MESH)
    pl.semaphore_wait(barrier, len(peers))

    def slices(i):
        return S[("wk", "wv")[i]].reshape(4, 2, 2, part_rows, width)

    def gather_x(i):
        source = (wk, wv)[i].at[pl.ds(pl.multiple_of(me * part_rows, 16), part_rows), :]
        return remote(source, slices(i).at[z, y, c], gxs.at[i], gxr.at[i], x_peer)

    def gather_z(i, k):
        own = slices(i).at[z, y, c]
        return remote(own, own, gzs.at[i, k - 1], gzr.at[i, k - 1], z_peers[k])

    def gather_z_here(i, k):
        found = slices(i).at[lax.rem(z + 4 - k, 4), y, c]
        return remote(found, found, gzs.at[i, k - 1], gzr.at[i, k - 1], z_peers[k])

    def gather_y(i, mine=True):
        held = slices(i).at[:, y if mine else 1 - y, c]
        return remote(held, held, gys.at[i], gyr.at[i], y_peer)

    def gather_core(i, mine=True):
        held = slices(i).at[:, :, c if mine else 1 - c]
        return remote(held, held, gcs.at[i], gcr.at[i], core_peer)

    gather_x(0).start()
    gather_x(1).start()

    def far_rows(part):
        return remote(
            slot("nt").at[:, span_of(part)],
            slot("ft").at[:, span_of(part)],
            xsem.at[part],
            xrem.at[part],
            x_peer,
        )

    load("x").wait()

    @unrolled_third
    def _(part, span):
        plain, inverse = plain_norm(W[0][span, :])
        low = (plain * gains[0:1, :] + shifts[0:1, :]).astype(bf16)
        S["nt"][:, span] = low.T
        far_rows(part).start()

    pltpu.make_async_copy(slot("nt"), nt_o, out_sem.at[2]).start()

    page_row = pages[...].astype(f32)
    side = st.astype(f32)
    valid_row = jnp.maximum(side, jnp.where(page_row < PAGES - 0.5, 1.0, 0.0))
    page_rows = [jnp.where(page_row == p, 1.0, 0.0) for p in range(PAGES)]
    for p in range(PAGES):
        page_low[p] = jnp.broadcast_to(page_rows[p], (size, slots)).astype(bf16)
    page_col[...] = jnp.broadcast_to(page_row, (128, slots)).T
    cell = lax.broadcasted_iota(jnp.int32, (GRID, third), 0)
    spot = lax.broadcasted_iota(jnp.int32, (GRID, third), 1)
    spot_first = jnp.where(lax.rem(spot, GRID) == cell, 1.0, 0.0)
    spot_second = jnp.where(lax.div(spot, GRID) == cell, 1.0, 0.0)
    spot_once = stack([spot_first, spot_second]).astype(bf16)
    spot_twice = stack([spot_once, spot_once])
    buckets = rel_table.shape[2] // 2
    radius = (buckets - 1) // 2
    toward = 1 - 2 * st
    cell = lax.broadcasted_iota(jnp.int32, (GRID, slots), 0)
    offsets = [
        jnp.clip(toward * (boxes[axis : axis + 1, :] - cell), -radius, radius) + radius
        for axis in range(2)
    ]

    rel_copy.wait()

    def bias_rows(head, carry):
        exact = []
        for axis in range(2):
            total = jnp.zeros((GRID, slots), f32)
            for bucket in range(buckets):
                total = jnp.where(
                    offsets[axis] == bucket, rel_table[head, 0, axis * buckets + bucket], total
                )
            total = total * LOG2E
            if axis == 0:
                total = jnp.where(page_row > PAGES - 0.5, masked_fill, total)
            exact.append(total)
        exact = stack(exact)
        high = exact.astype(bf16)
        bias[head, : 2 * GRID, :] = high
        bias[head, 2 * GRID :, :] = (exact - high.astype(f32)).astype(bf16)
        return carry

    lax.fori_loop(0, heads, bias_rows, 0)

    load("wq").wait()

    @unrolled_third
    def _(part, span):
        found = dot(S["wq"][:, span], S["nt"][...], "tn")
        S["q_t"][span, :] = (found * (LOG2E * size**-0.5)).astype(bf16)

    sums_o[...] = jnp.zeros_like(sums_o)
    late_o[...] = jnp.zeros_like(late_o)
    for i in range(2):
        gather_x(i).wait()
        for k in (1, 2, 3):
            gather_z(i, k).start()

    load("cot").wait()

    @unrolled_third
    def _(part, span):
        low = W[1][span, :].astype(bf16)
        S["g2"][span, :] = low
        sums_o[4:5, :] += jnp.sum(low.astype(f32), axis=0, keepdims=True)

    for t in range(4):
        down_load(t).wait()
        if t > 1:
            act_save(t - 2).wait()

        @unrolled_third
        def _(part, span):
            W[2 + t % 2][span, :] = dot(S["g2"][span, :], S["wd"][t % 2], "nt")

        act_save(t).start()
        down_load((t + 2) % 4).start()
        if t < 2:
            for k in (1, 2, 3):
                gather_z(t, k).wait_send()
                gather_z_here(t, k).wait_recv()
            gather_y(t).start()

    for i in range(2):
        gather_y(i).wait_send()
        gather_y(i, False).wait_recv()
        gather_core(i).start()

    for i, (weight, result) in enumerate((("wk", "k_t"), ("wv", "v_t"))):
        gather_core(i).wait_send()
        gather_core(i, False).wait_recv()

        @unrolled_third
        def _(part, span):
            if i == 0:
                far_rows(part).wait()
            S[result][:, span] = dot(S[weight][...], S["ft"][:, span], "tn").astype(bf16)

    act_save(2).wait()
    act_save(3).wait()
    act_load(0).start()

    def by_page(name, rows):
        return [S[name][rows, cols] for cols in thirds]

    def masked(name, rows):
        held = S[name][rows, :]
        return [held * page_low[p] for p in range(PAGES)]

    def fold(found):
        total = found[:size] * page_rows[0]
        for p in range(1, PAGES):
            total = total + found[p * size : (p + 1) * size] * page_rows[p]
        return total

    def column(p):
        return page_col[...] == p

    def spread(rows):
        middle, last = [jnp.concatenate([column(p)] * 2, axis=1) for p in (1, 2)]
        return jnp.where(middle, rows[1], jnp.where(last, rows[2], rows[0]))

    def rows_of(head):
        return pl.ds(pl.multiple_of(head * size, size), size)

    def in_pairs(step):
        def several(i, carry):
            for j in range(TOGETHER):
                step(TOGETHER * i + j, carry)
            return carry

        lax.fori_loop(0, heads // TOGETHER, several, 0)

    def text_forward(head, carry):
        rows = rows_of(head)
        scores = dot(
            stack(by_page("k_t", rows) + [spot_twice]),
            stack(masked("q_t", rows) + [bias[head]]),
            "tn",
        )
        top = jnp.max(scores, axis=0, keepdims=True)
        weight = jnp.exp2(scores - top).astype(bf16)
        found = dot(stack(by_page("v_t", rows) + [jnp.ones((16, third), bf16)]), weight)
        total = found[PAGES * size : PAGES * size + 1]
        S["att"][rows, :] = (fold(found) * (valid_row / total)).astype(bf16)
        lse[head] = top + jnp.log2(total)
        return carry

    def vision_forward(head, carry):
        rows = rows_of(head)
        scores = dot(
            stack(masked("k_t", rows) + [bias[head]]),
            stack(by_page("q_t", rows) + [spot_twice]),
            "tn",
        )
        tops = []
        for p in range(PAGES):
            inside = jnp.concatenate([column(p)] * 2, axis=1)
            tops.append(
                jnp.max(jnp.where(inside, scores, 2.0 * masked_fill), axis=0, keepdims=True)
            )
        weight = jnp.exp2(scores - spread(tops)).astype(bf16)
        counts = [page_low[p, :1, :] for p in range(PAGES)]
        counts = stack(counts + [jnp.zeros((16 - PAGES, slots), bf16)])
        found = dot(stack(masked("v_t", rows) + [counts]), weight)
        for p, cols in enumerate(thirds):
            total = found[PAGES * size + p : PAGES * size + p + 1]
            S["att"][rows, cols] = (found[p * size : (p + 1) * size] / total).astype(bf16)
            lse[head, :, cols] = tops[p] + jnp.log2(total)
        return carry

    @pl.when(st == 0)
    def _():
        in_pairs(text_forward)

    @pl.when(st == 1)
    def _():
        in_pairs(vision_forward)

    def down_view(at):
        return at.reshape(2, 2, width // 4, width)

    def rest_view(at):
        return at.reshape(4, 2, 2, part_rows, width)

    def add_low(left, right):
        return left + right

    def core_down(t):
        at = S["sd"].at[lax.rem(t, 2)]
        return remote(down_view(at).at[:, 1 - c], cd.at[t], csem.at[t], crem.at[t], core_peer)

    def core_rest(p, at):
        return remote(
            rest_view(at).at[:, :, 1 - c], cr.at[p], csem.at[4 + p], crem.at[4 + p], core_peer
        )

    def y_down(t):
        return remote(cd.at[t, 1 - y], yd.at[t], ysem.at[t], yrem.at[t], y_peer)

    def y_rest(p):
        return remote(cr.at[p, :, 1 - y], yr.at[p], ysem.at[4 + p], yrem.at[4 + p], y_peer)

    def z_down(t):
        return remote(yd.at[t], zd.at[t], zsem.at[0, t], zrem.at[0, t], z_peers[t + 1])

    def z_rest(p, i):
        q = chunk_of(p) if p < 4 else p
        return remote(
            yr.at[p, z_at[i]], zr.at[q, i - 1], zsem.at[1 + p, i - 1], zrem.at[1 + q, i - 1], z_peers[i]
        )

    def z_here(q, i):
        return remote(
            yr.at[q, z_at[i]], zr.at[q, i - 1], zsem.at[1 + q, i - 1], zrem.at[1 + q, i - 1], z_peers[i]
        )

    def after_core_down(t):
        core_down(t).wait()
        held = down_view(S["sd"].at[lax.rem(t, 2)])

        def part(i, carry):
            rows = pl.ds(pl.multiple_of(lax.rem(i, 2) * (2 * part_rows), 16), 2 * part_rows)
            j = lax.div(i, 2)
            cd[t, j, rows] = add_low(cd[t, j, rows], held[j, c, rows])
            return carry

        lax.fori_loop(0, 4, part, 0)
        y_down(t).start()

    def after_core(p, at):
        core_rest(p, at).wait()
        held = rest_view(at)

        def part(i, carry):
            cr[p, i] = add_low(cr[p, i], held[i, :, c])
            return carry

        lax.fori_loop(0, 4, part, 0)
        y_rest(p).start()

    def after_y_down(t):
        y_down(t).wait()

        def part(i, carry):
            rows = pl.ds(pl.multiple_of(i * (2 * part_rows), 16), 2 * part_rows)
            yd[t, rows] = add_low(yd[t, rows], cd[t, y, rows])
            return carry

        lax.fori_loop(0, 2, part, 0)
        if t < 3:
            z_down(t).start()

    def after_y(p):
        y_rest(p).wait()

        def part(i, carry):
            yr[p, i] = add_low(yr[p, i], cr[p, i, y])
            return carry

        lax.fori_loop(0, 4, part, 0)
        if p < 4:
            for i in (1, 2, 3):
                z_rest(p, i).start()
        else:
            z_near(p).start()

    def z_near(p):
        held = yr.at[p].reshape(2, 2, part_rows, width)
        return remote(
            held.at[:, 1 - z_low], zr.at[p, pl.ds(0, 2)], zsem.at[1 + p, 0], zrem.at[1 + p, 0], one_peer
        )

    def z_far(p):
        return remote(
            zr.at[p, 1 - z_high], zr.at[p, 2], zsem.at[1 + p, 1], zrem.at[1 + p, 1], two_peer
        )

    def after_near(p):
        z_near(p).wait()
        for i in range(2):
            zr[p, i] = add_low(zr[p, i], yr[p, 2 * i + z_low])
        z_far(p).start()

    def end_down():
        total = yd[3].astype(f32)
        for t in range(3):
            z_down(t).wait()
            total = total + zd[t].astype(f32)
        down_o[...] = total

    def end_rest(q):
        if q > 3:
            z_far(q).wait()
            return zr[q, z_high].astype(f32) + zr[q, 2].astype(f32)
        held = lax.rem(q - z + 3, 4) if q < 4 else q
        total = yr[held, z].astype(f32)
        for i in (1, 2, 3):
            z_here(q, i).wait()
            total = total + zr[q, i - 1].astype(f32)
        return total

    def exchange(mine, found, send, recv, peers, at, start):
        for k in (1, 2, 3):
            copy = remote(mine, found.at[at[0]], send.at[k - 1], recv.at[k - 1], peers[k])
            if start:
                copy.start()
            else:
                copy.wait_send()
                there = lax.rem(at[0] + 4 - k, 4)
                remote(mine, found.at[there], send.at[k - 1], recv.at[k - 1], peers[k]).wait_recv()
        if not start:
            found[at[0]] = mine[...]
            mine[...] = ((found[0] + found[1]) + found[2]) + found[3]

    def small_sums(stage, start):
        peers, at = ((place_peers, place_at), (z_peers, z_at))[stage]
        exchange(sums_o, sums_in.at[stage], asem.at[stage], arem.at[stage], peers, at, start)

    def small_table(stage, start):
        peers, at = ((place_peers, place_at), (z_peers, z_at))[stage]
        exchange(table_o, table_in.at[stage], bsem.at[stage], brem.at[stage], peers, at, start)

    pltpu.make_async_copy(slot("nt"), nt_o, out_sem.at[2]).wait()
    load("wo").wait()

    @unrolled_third
    def _(part, span):
        middle = W[0][span, :] + dot(S["att"][:, span], S["wo"][...], "tn")
        W[0][span, :] = middle
        W[2][span, :] = middle + down_bias[...]
        W[3][span, :] = jnp.zeros((third, width), f32)
        plain, inverse = plain_norm(middle)
        S["n2"][span, :] = (plain * gains[1:2, :] + shifts[1:2, :]).astype(bf16)

    def feed(t, carry):
        two = lax.rem(t, 2)
        at = chunk_of(t)
        up_load(t).wait()
        down_load(t).wait()
        act_load(t).wait()

        @pl.when(t < 3)
        def _():
            up_load(t + 1).start()

            @pl.when(t > 0)
            def _():
                down_load(t + 1).start()

        w_u = S["wu"].at[two]
        w_d = S["wd"].at[two]

        @unrolled_third
        def _(part, cols):
            pre = dot(S["n2"][...], w_u[:, cols]) + up_bias[at, :, cols]
            square = pre * pre
            gate = jnp.tanh(pre * (GELU_IN + (GELU_IN * GELU_CUBE) * square))
            gate_half = 0.5 + 0.5 * gate
            act = (pre * gate_half).astype(bf16)
            S["act"][:, cols] = act
            S["sd"][two, cols, :] = dot(act, S["g2"][...], "tn").astype(bf16)
            slope = pre * (GELU_IN + (3.0 * GELU_IN * GELU_CUBE) * square)
            grad_act = W[1][:, cols]
            grad_pre = (grad_act * (gate_half * (1.0 + (1.0 - gate) * slope))).astype(bf16)
            S["gp"][:, cols] = grad_pre
            sums_o[pl.ds(5 + at, 1), cols] = jnp.sum(grad_pre.astype(f32), axis=0, keepdims=True)

        @pl.when(t < 3)
        def _():
            act_load(t + 1).start()

        @pl.when(t == 3)
        def _():
            load("cot").start()

        core_down(t).start()

        @unrolled_third
        def _(part, cols):
            S["sr"][two, :, cols] = dot(S["n2"][...], S["gp"][:, cols], "tn").astype(bf16)

        core_rest(t, S["sr"].at[two]).start()
        after_core_down(t)

        @pl.when(t > 0)
        def _():
            after_core(t - 1, S["sr"].at[1 - two])

        @unrolled_third
        def _(part, span):
            W[2][span, :] = W[2][span, :] + dot(S["act"][span, :], w_d[...])
            W[3][span, :] = W[3][span, :] + dot(S["gp"][span, :], w_u[...], "nt")

        @pl.when(t == 1)
        def _():
            after_y_down(0)

        @pl.when(t == 2)
        def _():
            after_y(0)

        @pl.when(t == 3)
        def _():
            after_y_down(1)

        return carry

    lax.fori_loop(0, 4, feed, 0)
    after_core(3, S["sr1"])
    load("cot").wait()

    pltpu.make_async_copy(W[2], block_o, out_sem.at[0]).start()

    @unrolled_third
    def _(part, span):
        plain, inverse = plain_norm(W[0][span, :])
        grad_two = W[3][span, :]
        sums_o[1:2, :] += jnp.sum(grad_two * plain, axis=0, keepdims=True)
        sums_o[3:4, :] += jnp.sum(grad_two, axis=0, keepdims=True)
        middle = W[1][span, :] + norm_backward(grad_two, plain, inverse, gains[1:2, :])
        W[0][span, :] = middle
        S["gm"][span, :] = middle.astype(bf16)

    load("x_again").start()
    load("wq_again").start()
    load("nt_again").start()

    @unrolled_third
    def _(part, rows):
        grad_att = (dot(S["wo"][rows, :], S["gm"][...], "nt") * valid_row).astype(bf16)
        S["go"][rows, :] = grad_att
        both = S["att"][rows, :].astype(f32) * grad_att.astype(f32)
        delta[pl.ds(4 * part, 4)] = jnp.sum(both.reshape(4, size, slots), axis=1, keepdims=True)

    after_y(1)

    def table_rows(head, found):
        for axis in range(2):
            here = found[axis * GRID : (axis + 1) * GRID]
            for bucket in range(buckets):
                kept = jnp.where(offsets[axis] == bucket, here, 0.0)
                cells[pl.ds(head * 16 + axis * buckets + bucket, 1), :] = jnp.sum(
                    kept, axis=0, keepdims=True
                )

    def text_backward(head, carry):
        rows = rows_of(head)
        keys = by_page("k_t", rows)
        queries = masked("q_t", rows)
        grads = stack(masked("go", rows))
        scores = dot(stack(keys + [spot_twice]), stack(queries + [bias[head]]), "tn")
        prob = jnp.exp2(scores - lse[head])
        grad_prob = dot(stack(by_page("v_t", rows)), grads, "tn")
        grad_score = (prob * (grad_prob - delta[head])).astype(bf16)
        found = dot(grads, prob.astype(bf16), "nt")
        for p, cols in enumerate(thirds):
            S["dv"][rows, cols] = found[p * size : (p + 1) * size].astype(bf16)
        found = dot(stack(queries), grad_score, "nt") * LN2
        for p, cols in enumerate(thirds):
            S["dk"][rows, cols] = found[p * size : (p + 1) * size].astype(bf16)
        found = dot(stack(keys + [spot_once]), grad_score)
        S["dq"][rows, :] = (fold(found) * size**-0.5).astype(bf16)
        table_rows(head, found[PAGES * size :])
        return carry

    def vision_backward(head, carry):
        rows = rows_of(head)
        keys = masked("k_t", rows)
        queries = by_page("q_t", rows)
        grads = stack(by_page("go", rows))
        scores = dot(stack(keys + [bias[head]]), stack(queries + [spot_twice]), "tn")
        prob = jnp.exp2(scores - spread([lse[head, :, cols] for cols in thirds]))
        grad_prob = dot(stack(masked("v_t", rows)), grads, "tn")
        inner = spread([delta[head, :, cols] for cols in thirds])
        grad_score = (prob * (grad_prob - inner)).astype(bf16)
        S["dv"][rows, :] = fold(dot(grads, prob.astype(bf16), "nt")).astype(bf16)
        found = dot(stack(queries + [spot_once]), grad_score, "nt")
        S["dk"][rows, :] = (fold(found) * LN2).astype(bf16)
        table_rows(head, found[PAGES * size :])
        found = dot(stack(keys), grad_score) * size**-0.5
        for p, cols in enumerate(thirds):
            S["dq"][rows, cols] = found[p * size : (p + 1) * size].astype(bf16)
        return carry

    cells[...] = jnp.zeros_like(cells)

    @pl.when(st == 0)
    def _():
        in_pairs(text_backward)

    @pl.when(st == 1)
    def _():
        in_pairs(vision_backward)

    after_y_down(2)

    load("x_again").wait()
    base = heads * 16
    cells[base + 2 : base + 3, :] = valid_row

    @unrolled_third
    def _(part, span):
        block = W[2][span, :]
        own = jnp.maximum(side, jnp.where(page_col[span, 0:1] < PAGES - 0.5, 1.0, 0.0))
        sub = block - W[3][span, :]
        cells[base : base + 1, :] += jnp.sum(own * block * block, axis=0, keepdims=True)
        cells[base + 1 : base + 2, :] += jnp.sum(own * sub * sub, axis=0, keepdims=True)

    table_o[...] = lax.dot_general(
        jnp.ones((8, width), f32),
        cells[...],
        (((1,), (1,)), ((), ())),
        preferred_element_type=f32,
        precision=lax.Precision.HIGHEST,
    )

    small_sums(0, True)
    small_table(0, True)

    def back_rows(part):
        return remote(
            slot("send").at[:, span_of(part)],
            slot("back").at[:, span_of(part)],
            xsem.at[3 + part],
            xrem.at[3 + part],
            x_peer,
        )

    @unrolled_third
    def _(part, cols):
        S["send"][:, cols] = (
            dot(S["wk"][...], S["dk"][:, cols])
            + dot(S["wv"][...], S["dv"][:, cols])
        ).astype(bf16)
        back_rows(part).start()


    @unrolled_third
    def _(part, span):
        S["sk"][span, :] = dot(S["ft"][span, :], S["dk"][...], "nt").astype(bf16)

    core_rest(5, S["sk"]).start()
    after_y(2)

    @unrolled_third
    def _(part, span):
        S["sv"][span, :] = dot(S["ft"][span, :], S["dv"][...], "nt").astype(bf16)

    core_rest(6, S["sv"]).start()
    after_core(5, S["sk"])

    @unrolled_third
    def _(part, span):
        S["so"][span, :] = dot(S["att"][span, :], S["gm"][...]).astype(bf16)

    core_rest(4, S["so"]).start()
    after_core(6, S["sv"])
    load("nt_again").wait()

    @unrolled_third
    def _(part, span):
        S["sq"][span, :] = dot(S["nt_again"][span, :], S["dq"][...], "nt").astype(bf16)

    core_rest(7, S["sq"]).start()
    after_core(4, S["so"])
    load("wq_again").wait()

    @unrolled_third
    def _(part, span):
        W[1][span, :] = dot(S["wq_again"][span, :], S["dq"][...])

    after_core(7, S["sq"])
    after_y_down(3)

    def last_small(stage, start):
        peers, at = ((place_peers, place_at), (z_peers, z_at))[stage]
        exchange(late_o, late_in.at[stage], lsem.at[stage], lrem.at[stage], peers, at, start)

    table_swap = remote(table_o, table_far, tsem, trem, x_peer)

    def hop_copy(i):
        return remote(hop.at[i], hop_in.at[i], hsem.at[i], hrem.at[i], x_peer)

    after_y(3)
    pltpu.make_async_copy(W[2], block_o, out_sem.at[0]).wait()

    @each_third
    def _(part, span):
        back_rows(part).wait()
        grad_one = (W[1][:, span] + S["back"][:, span].astype(f32)).T
        plain, inverse = plain_norm(W[3][span, :])
        late_o[0:1, :] += jnp.sum(grad_one * plain, axis=0, keepdims=True)
        late_o[1:2, :] += jnp.sum(grad_one, axis=0, keepdims=True)
        W[2][span, :] = W[0][span, :] + norm_backward(
            grad_one, plain, inverse, gains[0:1, :]
        )

        @pl.when(part == 0)
        def _():
            small_sums(0, False)
            small_sums(1, True)
            small_table(0, False)
            small_table(1, True)

        @pl.when(part == 1)
        def _():
            after_y(5)

    pltpu.make_async_copy(W[2], grad_o, out_sem.at[1]).start()
    last_small(0, True)
    after_near(5)
    after_y(6)
    end_down()
    for q in range(4):
        up_o[:, q * width : (q + 1) * width] = end_rest(q)
    after_y(4)
    after_near(6)
    small_sums(1, False)
    small_table(1, False)
    table_swap.start()
    hop[0] = end_rest(5).astype(bf16)
    hop_copy(0).start()
    last_small(0, False)
    last_small(1, True)
    after_near(4)
    after_y(7)
    hop[1] = end_rest(6).astype(bf16)
    hop_copy(1).start()
    wo_o[...] = end_rest(4)
    after_near(7)
    last_small(1, False)
    wq_o[...] = end_rest(7)
    table_swap.wait()
    lane = lax.broadcasted_iota(jnp.int32, table_o.shape, 1)
    table_o[...] = table_o[...] + jnp.where(lane >= base, table_far[...], 0.0)
    for i in range(2):
        hop_copy(i).wait()
        hop_o[i] = hop_in[i].astype(f32)
    pltpu.make_async_copy(W[2], grad_o, out_sem.at[1]).wait()


def hand_over(
    block, grad_in, down, up, out, query, hop, sums, late, table,
    block_o, grad_o, gains_o, shifts_o, query_o, key_o, value_o, out_o, up_o, up_bias_o, down_o, down_bias_o, table_o, stats_o,
    held, down_h, up_h, out_h, query_h, hop_h, sums_h, late_h, table_h, in_sem, out_sem, sem,
):
    slots, width = block.shape
    step = slots // 4
    moves = []
    for i, (source, target) in enumerate(((block, block_o), (grad_in, grad_o))):
        for j in range(4):
            span = pl.ds(j * step, step)
            moves.append(
                (
                    pltpu.make_async_copy(
                        source.at[span, :], held.at[i, span, :], in_sem.at[i, j]
                    ),
                    pltpu.make_async_copy(
                        held.at[i, span, :], target.at[span, :], out_sem.at[i, j]
                    ),
                )
            )
    for i, (source, kept, target) in enumerate(((down, down_h, down_o), (up, up_h, up_o))):
        moves.append(
            (
                pltpu.make_async_copy(source, kept, sem.at[i]),
                pltpu.make_async_copy(kept, target, sem.at[i + 8]),
            )
        )
    small = ((out, out_h), (query, query_h), (hop, hop_h), (sums, sums_h), (late, late_h), (table, table_h))
    small = [pltpu.make_async_copy(*pair, sem.at[i + 2]) for i, pair in enumerate(small)]
    for copy in small:
        copy.start()
    for move in moves:
        move[0].start()
    for copy in small:
        copy.wait()
    gains_o[0:1, :] = late_h[0:1, :]
    gains_o[1:2, :] = sums_h[1:2, :]
    shifts_o[0:1, :] = late_h[1:2, :]
    shifts_o[1:2, :] = sums_h[3:4, :]
    down_bias_o[...] = sums_h[4:5, :]
    for q in range(4):
        up_bias_o[:, q * width : (q + 1) * width] = sums_h[5 + q : 6 + q, :]
    query_o[...] = query_h[...]
    key_o[...] = hop_h[0]
    value_o[...] = hop_h[1]
    out_o[...] = out_h[...]
    heads, _, rows = table_o.shape
    for head in range(heads):
        table_o[head] = table_h[0:1, head * 16 : head * 16 + rows]
    total = table_h[0:1, heads * 16 : heads * 16 + 2]
    count = table_h[0:1, heads * 16 + 2 : heads * 16 + 3]
    stats_o[...] = jnp.sqrt(total / (count * width))
    for move in moves:
        move[0].wait()
        move[1].start()
    for move in moves:
        move[1].wait()


def on_device(
    inputs,
    text_pages,
    text_boxes,
    norm_gains,
    norm_shifts,
    w_query,
    w_key,
    w_value,
    w_out,
    w_up,
    up_bias,
    w_down,
    down_bias,
    box_table,
    cotangent,
):
    slots, width = inputs.shape[2:]
    rel_rows, heads = box_table.shape[1:]
    size = width // heads
    part = width // 16
    shape = lambda *dims: jax.ShapeDtypeStruct(dims, f32)
    vmem = pl.BlockSpec(memory_space=pltpu.VMEM)
    hbm = pl.BlockSpec(memory_space=pl.ANY)
    dma = pltpu.SemaphoreType.DMA
    cell_rows = heads * 16 + 16
    low = lambda *dims: pltpu.VMEM(dims, bf16)
    full = lambda *dims: pltpu.VMEM(dims, f32)
    block, grad_in, _, _, down, up, out, query, hop, sums, late, table = pl.pallas_call(
        layer_kernel,
        out_shape=[
            shape(slots, width),
            shape(slots, width),
            jax.ShapeDtypeStruct((width, slots), bf16),
            shape(4, slots, width),
            shape(4 * part, width),
            shape(part, 4 * width),
            shape(part, width),
            shape(part, width),
            shape(2, part, width),
            shape(16, width),
            shape(8, width),
            shape(8, cell_rows),
        ],
        in_specs=[hbm] * 8 + [vmem] * 6 + [hbm],
        out_specs=[hbm] * 4 + [vmem] * 8,
        scratch_shapes=[
            [low(slots, width)] * (len(NAMES) - RINGS) + [low(2, slots, width)] * RINGS,
            [full(slots, width)] * 4,
            pltpu.SMEM((heads, 1, rel_rows), f32),
            low(heads, 4 * GRID, slots),
            full(heads, 1, slots),
            full(heads, 1, slots),
            low(PAGES, size, slots),
            full(slots, 128),
            full(cell_rows, width),
            low(4, 2, 4 * part, width),
            low(8, 4, 2, part, width),
            low(4, 4 * part, width),
            low(8, 4, part, width),
            low(3, 4 * part, width),
            low(8, 3, part, width),
            low(2, part, width),
            low(2, part, width),
            full(2, 4, 16, width),
            full(2, 4, 8, width),
            full(2, 4, 8, cell_rows),
            full(8, cell_rows),
            dma((7,)),
            dma((3, 3)),
            dma((3,)),
            dma((12,)),
            dma((12,)),
            dma((12,)),
            dma((12,)),
            dma((9, 3)),
            dma((9, 3)),
            dma((6,)),
            dma((6,)),
            dma((2,)),
            dma((2,)),
            dma((2, 3)),
            dma((2, 3)),
            dma((2, 3)),
            dma((2, 3)),
            dma((2, 3)),
            dma((2, 3)),
            dma,
            dma,
            dma((2,)),
            dma((2,)),
            dma((2, 3)),
            dma((2, 3)),
            dma((2,)),
            dma((2,)),
            dma((2,)),
            dma((2,)),
        ],
        compiler_params=pltpu.CompilerParams(
            collective_id=0, has_side_effects=True, vmem_limit_bytes=61 * 2**20
        ),
        name="layer",
    )(
        inputs[0, 0],
        cotangent[0, 0],
        w_query[0],
        w_key[0],
        w_value[0],
        w_out[0],
        w_up[0],
        w_down[0],
        up_bias.reshape(4, 1, width),
        down_bias,
        norm_gains[0],
        norm_shifts[0],
        text_pages,
        text_boxes[0],
        box_table.transpose(2, 0, 1),
    )
    outs = pl.pallas_call(
        hand_over,
        out_shape=[
            shape(slots, width),
            shape(slots, width),
            shape(2, width),
            shape(2, width),
            shape(part, width),
            shape(part, width),
            shape(part, width),
            shape(part, width),
            shape(part, 4 * width),
            shape(1, 4 * width),
            shape(4 * part, width),
            shape(1, width),
            shape(heads, 1, rel_rows),
            shape(1, 2),
        ],
        in_specs=[hbm] * 10,
        out_specs=[hbm] * 2 + [vmem] * 6 + [hbm, vmem, hbm] + [vmem] * 3,
        scratch_shapes=[
            full(2, slots, width),
            full(4 * part, width),
            full(part, 4 * width),
            full(part, width),
            full(part, width),
            full(2, part, width),
            full(16, width),
            full(8, width),
            full(8, cell_rows),
            dma((2, 4)),
            dma((2, 4)),
            dma((10,)),
        ],
        compiler_params=pltpu.CompilerParams(vmem_limit_bytes=61 * 2**20),
        name="hand_over",
    )(block, grad_in, down, up, out, query, hop, sums, late, table)
    block, grad_in, gains, shifts, query, key, value, out, up, up_b, down, down_b, table, stats = outs
    return (
        block[None, None],
        grad_in[None, None],
        gains[None],
        shifts[None],
        query[None],
        key[None],
        value[None],
        out[None],
        up[None],
        up_b,
        down[None],
        down_b,
        table.transpose(1, 2, 0),
        stats[0],
    )


def partner(block, axis, bit):
    count = lax.axis_size(axis)
    route = []
    for low in range(count):
        high = low | 1 << bit
        if high != low and high < count:
            route += [(low, high), (high, low)]
    return lax.ppermute(block, axis, route)


def norm_forward(values, gain_row, shift_row):
    center = values - jnp.mean(values, axis=-1, keepdims=True)
    inverse = lax.rsqrt(jnp.mean(center * center, axis=-1, keepdims=True) + 1e-05)
    normal_part = center * inverse
    return (normal_part * gain_row + shift_row, normal_part, inverse)


def general_norm_backward(grad_normed, normal_part, inverse, gain_row):
    scaled = grad_normed * gain_row
    first_mean = jnp.mean(scaled, axis=-1, keepdims=True)
    second_mean = jnp.mean(scaled * normal_part, axis=-1, keepdims=True)
    return inverse * (scaled - first_mean - normal_part * second_mean)


def bucket_offset(own_coord, far_coord, bucket_count):
    radius = (bucket_count - 1) // 2
    return jnp.clip(own_coord[:, None] - far_coord[None, :], -radius, radius) + radius


def bias_from(rel_table, offset):
    result = jnp.zeros((rel_table.shape[1],) + offset.shape, f32)
    for bucket in range(rel_table.shape[0]):
        result = (
            result + rel_table[bucket][:, None, None] * (offset == bucket).astype(f32)[None]
        )
    return result


def bias_grad(grad_wide, offset, bucket_count):
    return jnp.stack(
        [
            jnp.sum(grad_wide * (offset == bucket).astype(f32)[None], axis=(1, 2))
            for bucket in range(bucket_count)
        ]
    )


def project(left, right):
    return jnp.einsum("rsd,de->rse", left, right, preferred_element_type=f32)


def weight_grad(left, right):
    return jnp.einsum("rsd,rse->de", left, right, preferred_element_type=f32)


def back_project(grad_low, weight):
    return jnp.einsum("rse,de->rsd", grad_low, weight, preferred_element_type=f32)


def general_device(
    inputs,
    text_pages,
    text_boxes,
    norm_gains,
    norm_shifts,
    w_query,
    w_key,
    w_value,
    w_out,
    w_up,
    up_bias,
    w_down,
    down_bias,
    box_table,
    cotangent,
):
    slot_count = inputs.shape[2]
    model_width = inputs.shape[3]
    head_count = box_table.shape[2]
    head_size = model_width // head_count
    bucket_count = box_table.shape[1] // 2
    score_scale = head_size ** (-0.5)
    is_text = lax.axis_index("stream") == 0
    positions = jnp.arange(slot_count, dtype=jnp.int32)
    cell_index = positions % (GRID * GRID)
    vision_page = positions // (GRID * GRID)
    vision_first = cell_index % GRID
    vision_second = cell_index // GRID
    own_valid = jnp.where(is_text, text_pages < PAGES, True).astype(f32)
    gain_rows = norm_gains[0]
    shift_rows = norm_shifts[0]
    rel_table = box_table[0]
    block_in = inputs[:, 0]
    normed_one, plain_one, inverse_one = norm_forward(block_in, gain_rows[0], shift_rows[0])
    normed_low = normed_one.astype(bf16)
    query = project(normed_low, w_query[0]).astype(bf16)
    own_keys = project(normed_low, w_key[0]).astype(bf16)
    own_values = project(normed_low, w_value[0]).astype(bf16)
    far_keys, far_values = partner((own_keys, own_values), "stream", 0)

    def geometry(row_index):
        text_page = text_pages[row_index]
        own_page = jnp.where(is_text, text_page, vision_page)
        far_page = jnp.where(is_text, vision_page, text_page)
        own_first = jnp.where(is_text, text_boxes[row_index, 0], vision_first)
        far_first = jnp.where(is_text, vision_first, text_boxes[row_index, 0])
        own_second = jnp.where(is_text, text_boxes[row_index, 1], vision_second)
        far_second = jnp.where(is_text, vision_second, text_boxes[row_index, 1])
        allowed = (own_page[:, None] == far_page[None, :]) | (own_page[:, None] == PAGES)
        return (
            allowed,
            bucket_offset(own_first, far_first, bucket_count),
            bucket_offset(own_second, far_second, bucket_count),
        )

    def heads_of(matrix):
        return matrix.reshape(slot_count, head_count, head_size)

    def score_block(row_index, allowed, offset_first, offset_second):
        raw = (
            jnp.einsum(
                "ihd,jhd->hij",
                heads_of(query[row_index]),
                heads_of(far_keys[row_index]),
                preferred_element_type=f32,
            )
            * score_scale
        )
        raw = (
            raw
            + bias_from(rel_table[:bucket_count], offset_first)
            + bias_from(rel_table[bucket_count:], offset_second)
        )
        return jnp.where(allowed[None], raw, masked_fill)

    row_index = 0
    allowed, offset_first, offset_second = geometry(row_index)
    masked = score_block(row_index, allowed, offset_first, offset_second)
    top_score = jnp.max(masked, axis=-1, keepdims=True)
    exp_scores = jnp.exp(masked - top_score)
    row_total = jnp.sum(exp_scores, axis=-1, keepdims=True)
    prob_low = (exp_scores / row_total).astype(bf16)
    attended = jnp.einsum(
        "hij,jhd->ihd",
        prob_low,
        heads_of(far_values[row_index]),
        preferred_element_type=f32,
    ).reshape(slot_count, model_width)
    attended_rows = [(attended * own_valid[row_index][:, None]).astype(bf16)]
    log_totals = [top_score + jnp.log(row_total)]
    attended_low = jnp.stack(attended_rows)
    branch_one = project(attended_low, w_out[0])
    middle = block_in + branch_one
    normed_two, plain_two, inverse_two = norm_forward(middle, gain_rows[1], shift_rows[1])
    normed_two_low = normed_two.astype(bf16)
    pre_act = project(normed_two_low, w_up[0]) + up_bias[0]
    act_low = jax.nn.gelu(pre_act).astype(bf16)
    branch_two = project(act_low, w_down[0]) + down_bias[0]
    block_out = middle + branch_two
    sublayer = branch_one + branch_two
    totals = lax.psum(
        (
            jnp.sum(own_valid * jnp.sum(block_out * block_out, axis=-1)),
            jnp.sum(own_valid * jnp.sum(sublayer * sublayer, axis=-1)),
            jnp.sum(own_valid),
        ),
        ("stream", "batch"),
    )
    denominator = totals[2] * model_width
    stats = jnp.stack([jnp.sqrt(totals[0] / denominator), jnp.sqrt(totals[1] / denominator)])
    grad_out = cotangent[:, 0]
    grad_out_low = grad_out.astype(bf16)
    grad_w_down = weight_grad(act_low, grad_out_low)
    grad_down_bias = jnp.sum(grad_out_low.astype(f32), axis=(0, 1))
    grad_act = back_project(grad_out_low, w_down[0])
    gelu_back = jax.vjp(jax.nn.gelu, pre_act)[1]
    grad_pre_low = gelu_back(grad_act)[0].astype(bf16)
    grad_w_up = weight_grad(normed_two_low, grad_pre_low)
    grad_up_bias = jnp.sum(grad_pre_low.astype(f32), axis=(0, 1))
    grad_normed_two = back_project(grad_pre_low, w_up[0])
    grad_gain_two = jnp.sum(grad_normed_two * plain_two, axis=(0, 1))
    grad_shift_two = jnp.sum(grad_normed_two, axis=(0, 1))
    grad_middle = grad_out + general_norm_backward(grad_normed_two, plain_two, inverse_two, gain_rows[1])
    grad_middle_low = grad_middle.astype(bf16)
    grad_w_out = weight_grad(attended_low, grad_middle_low)
    grad_attended = back_project(grad_middle_low, w_out[0]).astype(bf16) * own_valid[
        :, :, None
    ].astype(bf16)
    query_grad_rows, key_grad_rows, value_grad_rows = ([], [], [])
    row_index = 0
    allowed, offset_first, offset_second = geometry(row_index)
    masked = score_block(row_index, allowed, offset_first, offset_second)
    prob = jnp.exp(masked - log_totals[row_index])
    grad_heads = heads_of(grad_attended[row_index])
    grad_prob = jnp.einsum(
        "ihd,jhd->hij",
        grad_heads,
        heads_of(far_values[row_index]),
        preferred_element_type=f32,
    )
    inner_sum = jnp.sum(prob * grad_prob, axis=-1, keepdims=True)
    grad_score_low = (prob * (grad_prob - inner_sum)).astype(bf16)
    grad_score_wide = grad_score_low.astype(f32)
    grad_table = jnp.concatenate(
        [
            bias_grad(grad_score_wide, offset_first, bucket_count),
            bias_grad(grad_score_wide, offset_second, bucket_count),
        ],
        axis=0,
    )
    query_grad = (
        jnp.einsum(
            "hij,jhd->ihd",
            grad_score_low,
            heads_of(far_keys[row_index]),
            preferred_element_type=f32,
        )
        * score_scale
    )
    key_grad = (
        jnp.einsum(
            "hij,ihd->jhd",
            grad_score_low,
            heads_of(query[row_index]),
            preferred_element_type=f32,
        )
        * score_scale
    )
    value_grad = jnp.einsum(
        "hij,ihd->jhd", prob.astype(bf16), grad_heads, preferred_element_type=f32
    )
    query_grad_rows.append(query_grad.reshape(slot_count, model_width).astype(bf16))
    key_grad_rows.append(key_grad.reshape(slot_count, model_width).astype(bf16))
    value_grad_rows.append(value_grad.reshape(slot_count, model_width).astype(bf16))
    grad_query_low = jnp.stack(query_grad_rows)
    own_key_grad, own_value_grad = partner(
        (jnp.stack(key_grad_rows), jnp.stack(value_grad_rows)), "stream", 0
    )
    grad_w_query = weight_grad(normed_low, grad_query_low)
    grad_w_key = weight_grad(normed_low, own_key_grad)
    grad_w_value = weight_grad(normed_low, own_value_grad)
    grad_normed_one = (
        back_project(grad_query_low, w_query[0])
        + back_project(own_key_grad, w_key[0])
        + back_project(own_value_grad, w_value[0])
    )
    grad_gain_one = jnp.sum(grad_normed_one * plain_one, axis=(0, 1))
    grad_shift_one = jnp.sum(grad_normed_one, axis=(0, 1))
    grad_inputs = grad_middle + general_norm_backward(grad_normed_one, plain_one, inverse_one, gain_rows[0])
    big_sums = (
        lax.psum_scatter(grad_w_query, "batch", scatter_dimension=0, tiled=True),
        lax.psum_scatter(grad_w_key, "batch", scatter_dimension=0, tiled=True),
        lax.psum_scatter(grad_w_value, "batch", scatter_dimension=0, tiled=True),
        lax.psum_scatter(grad_w_out, "batch", scatter_dimension=0, tiled=True),
        lax.psum_scatter(grad_w_up, "batch", scatter_dimension=0, tiled=True),
        lax.psum_scatter(grad_w_down, "batch", scatter_dimension=0, tiled=True),
    )
    small_sums = lax.psum(
        (
            jnp.stack([grad_gain_one, grad_gain_two]),
            jnp.stack([grad_shift_one, grad_shift_two]),
            grad_up_bias,
            grad_down_bias,
            grad_table,
        ),
        "batch",
    )
    return (
        block_out[:, None],
        grad_inputs[:, None],
        small_sums[0][None],
        small_sums[1][None],
        big_sums[0][None],
        big_sums[1][None],
        big_sums[2][None],
        big_sums[3][None],
        big_sums[4][None],
        small_sums[2][None],
        big_sums[5][None],
        small_sums[3][None],
        small_sums[4][None],
        stats,
    )


def solution(mesh):
    sided = lambda dims: P("stream", *([None] * (dims - 1)))
    rows = P("batch", "stream", None, None)
    shard = P("stream", "batch", None)
    placed = (
        (rows, P("batch", None), P("batch", None, None), sided(3), sided(3))
        + (sided(3),) * 5
        + (sided(2), sided(3), sided(2), sided(3), rows)
    )
    fits = mesh.shape["batch"] == 16 and mesh.shape["stream"] == 2
    return jax.shard_map(
        on_device if fits else general_device,
        mesh=mesh,
        in_specs=placed,
        out_specs=(
            (rows, rows, sided(3), sided(3))
            + (shard,) * 5
            + (sided(2), shard, sided(2), sided(3), P())
        ),
        check_vma=False,
    )
```

```python
import jax
import jax.numpy as jnp
from jax import lax
from jax.experimental import pallas as pl
from jax.experimental.pallas import tpu as pltpu
from jax.sharding import PartitionSpec as P

GRID = 16
PAGES = 3
MESH = pl.DeviceIdType.MESH
LOG2E = 1.4426950408889634
LN2 = 0.6931471805599453
TOGETHER = 4
GELU_IN = 0.7978845608028654
GELU_CUBE = 0.044715
masked_fill = -1e30
f32 = jnp.float32
bf16 = jnp.bfloat16


def dot(left, right, form="nn"):
    dims = {"nn": (1, 0), "nt": (1, 1), "tn": (0, 0)}[form]
    return lax.dot_general(
        left, right, (((dims[0],), (dims[1],)), ((), ())), preferred_element_type=f32
    )


def stack(parts):
    return jnp.concatenate(parts, axis=0)


def plain_norm(values):
    center = values - jnp.mean(values, axis=-1, keepdims=True)
    inverse = lax.rsqrt(jnp.mean(center * center, axis=-1, keepdims=True) + 1e-05)
    return center * inverse, inverse


def norm_backward(grad_normed, plain, inverse, gain_row):
    scaled = grad_normed * gain_row
    first_mean = jnp.mean(scaled, axis=-1, keepdims=True)
    second_mean = jnp.mean(scaled * plain, axis=-1, keepdims=True)
    return inverse * (scaled - first_mean - plain * second_mean)


NAMES = (
    "ft", "wk", "wv", "back", "q_t", "k_t", "v_t", "att", "wo", "n2", "g2", "act", "gp",
    "wu", "wd", "sd", "sr",
)
RINGS = 4
SHARED = dict(
    nt=("n2",), wq=("act",), gm=("n2",), go=("g2",), dq=("wu", 0), dk=("wu", 1), dv=("wd", 0),
    send=("wd", 1), so=("sd", 0), sk=("sd", 1), sv=("sr", 0), sq=("sr", 1), sr1=("sr", 1),
    nt_again=("act",), wq_again=("gp",), sr0=("sr", 0),
)


def layer_kernel(
    x, cot, wq, wk, wv, wo, wup, wdn,
    up_bias, down_bias, gains, shifts, pages, boxes, rel_hbm,
    block_o, grad_o, nt_o, ga_o, down_o, up_o, wo_o, wq_o, hop_o, sums_o, late_o, table_o,
    buffers, wides, rel_table, bias, lse, delta, page_low, page_col, cells,
    cd, cr, yd, yr, zd, zr, hop, hop_in, sums_in, late_in, table_in, table_far,
    in_sem, w_sem, out_sem, csem, crem, ysem, yrem, zsem, zrem, xsem, xrem, hsem, hrem,
    asem, arem, bsem, brem, lsem, lrem, tsem, trem, gxs, gxr, gzs, gzr, gys, gyr, gcs, gcr,
):
    slots, width = x.shape
    heads = lse.shape[0]
    size = width // heads
    third = slots // 3
    thirds = [slice(part * third, (part + 1) * third) for part in range(3)]
    part_rows = width // 16
    st = lax.axis_index("stream")
    me = lax.axis_index("batch")
    c = lax.rem(me, 2)
    y = lax.rem(lax.div(me, 2), 2)
    z = lax.div(me, 4)
    place = lax.rem(me, 4)
    core_peer = (st, me + 1 - 2 * c)
    y_peer = (st, me + 2 - 4 * y)
    z_low = lax.rem(z, 2)
    z_high = lax.div(z, 2)
    one_peer = (st, me + 4 - 8 * z_low)
    two_peer = (st, me + 8 - 16 * z_high)
    z_at = [lax.rem(z + i, 4) for i in range(4)]
    z_peers = [(st, z_at[i] * 4 + place) for i in range(4)]
    place_at = [lax.rem(place + i, 4) for i in range(4)]
    place_peers = [(st, z * 4 + place_at[i]) for i in range(4)]
    x_peer = (1 - st, me)

    def span_of(j):
        return pl.ds(pl.multiple_of(j * third, third), third)

    def unrolled_third(step):
        for j in range(3):
            step(j, pl.ds(j * third, third))

    def each_third(step):
        def body(j, carry):
            step(j, span_of(j))
            return carry

        lax.fori_loop(0, 3, body, 0)

    S = dict(zip(NAMES, buffers))
    for name, (held, *at) in SHARED.items():
        S[name] = S[held].at[at[0]] if at else S[held]
    W = wides

    def slot(name):
        return S[name]

    def remote(source, target, send, recv, peer):
        return pltpu.make_async_remote_copy(
            source, target, send, recv, device_id=peer, device_id_type=MESH
        )

    singles = dict(
        cot=(cot, W[1]), wo=(wo, slot("wo")), wq=(wq, slot("wq")),
        x_again=(x, W[3]), wq_again=(wq, slot("wq_again")), nt_again=(nt_o, slot("nt_again")),
    )
    load_at = {name: i for i, name in enumerate(singles)}

    def load(name):
        return pltpu.make_async_copy(*singles[name], in_sem.at[load_at[name]])

    def chunk_of(t):
        return lax.rem(z + t + 1, 4)

    def up_load(t):
        at = pl.multiple_of(chunk_of(t) * width, width)
        two = lax.rem(t, 2)
        return pltpu.make_async_copy(
            wup.at[:, pl.ds(at, width)], S["wu"].at[two], w_sem.at[two, 0]
        )

    def down_load(t):
        at = pl.multiple_of(chunk_of(t) * width, width)
        two = lax.rem(t, 2)
        return pltpu.make_async_copy(
            wdn.at[pl.ds(at, width), :], S["wd"].at[two], w_sem.at[two, 1]
        )

    def act_load(t):
        return pltpu.make_async_copy(ga_o.at[t], W[1], w_sem.at[2, 0])

    def act_save(t):
        return pltpu.make_async_copy(W[2 + t % 2], ga_o.at[t], w_sem.at[2, 1 + t % 2])

    def first_rows(part):
        span = span_of(part)
        return pltpu.make_async_copy(x.at[span, :], W[0].at[span, :], w_sem.at[3, part])

    for part in range(3):
        first_rows(part).start()
    rel_copy = pltpu.make_async_copy(rel_hbm, rel_table, out_sem.at[1])
    rel_copy.start()
    load("wq").start()
    load("cot").start()
    load("wo").start()
    down_load(0).start()
    down_load(1).start()
    up_load(0).start()

    barrier = pltpu.get_barrier_semaphore()
    peers = place_peers[1:] + z_peers[1:] + [x_peer]
    for peer in peers:
        pl.semaphore_signal(barrier, inc=1, device_id=peer, device_id_type=MESH)
    pl.semaphore_wait(barrier, len(peers))

    def slices(i):
        return S[("wk", "wv")[i]].reshape(4, 2, 2, part_rows, width)

    def gather_x(i):
        source = (wk, wv)[i].at[pl.ds(pl.multiple_of(me * part_rows, 16), part_rows), :]
        return remote(source, slices(i).at[z, y, c], gxs.at[i], gxr.at[i], x_peer)

    def gather_z(i, k):
        own = slices(i).at[z, y, c]
        return remote(own, own, gzs.at[i, k - 1], gzr.at[i, k - 1], z_peers[k])

    def gather_z_here(i, k):
        found = slices(i).at[lax.rem(z + 4 - k, 4), y, c]
        return remote(found, found, gzs.at[i, k - 1], gzr.at[i, k - 1], z_peers[k])

    def gather_y(i, mine=True):
        held = slices(i).at[:, y if mine else 1 - y, c]
        return remote(held, held, gys.at[i], gyr.at[i], y_peer)

    def gather_core(i, mine=True):
        held = slices(i).at[:, :, c if mine else 1 - c]
        return remote(held, held, gcs.at[i], gcr.at[i], core_peer)

    gather_x(0).start()
    gather_x(1).start()

    def far_rows(part):
        return remote(
            slot("nt").at[:, span_of(part)],
            slot("ft").at[:, span_of(part)],
            xsem.at[part],
            xrem.at[part],
            x_peer,
        )


    @unrolled_third
    def _(part, span):
        first_rows(part).wait()
        plain, inverse = plain_norm(W[0][span, :])
        low = (plain * gains[0:1, :] + shifts[0:1, :]).astype(bf16)
        S["nt"][:, span] = low.T
        far_rows(part).start()

    pltpu.make_async_copy(slot("nt"), nt_o, out_sem.at[2]).start()

    page_row = pages[...].astype(f32)
    side = st.astype(f32)
    valid_row = jnp.maximum(side, jnp.where(page_row < PAGES - 0.5, 1.0, 0.0))
    page_rows = [jnp.where(page_row == p, 1.0, 0.0) for p in range(PAGES)]
    for p in range(PAGES):
        page_low[p] = jnp.broadcast_to(page_rows[p], (size, slots)).astype(bf16)
    page_col[...] = jnp.broadcast_to(page_row, (128, slots)).T
    cell = lax.broadcasted_iota(jnp.int32, (GRID, third), 0)
    spot = lax.broadcasted_iota(jnp.int32, (GRID, third), 1)
    spot_first = jnp.where(lax.rem(spot, GRID) == cell, 1.0, 0.0)
    spot_second = jnp.where(lax.div(spot, GRID) == cell, 1.0, 0.0)
    spot_once = stack([spot_first, spot_second]).astype(bf16)
    spot_twice = stack([spot_once, spot_once])
    buckets = rel_table.shape[2] // 2
    radius = (buckets - 1) // 2
    toward = 1 - 2 * st
    cell = lax.broadcasted_iota(jnp.int32, (GRID, slots), 0)
    offsets = [
        jnp.clip(toward * (boxes[axis : axis + 1, :] - cell), -radius, radius) + radius
        for axis in range(2)
    ]

    rel_copy.wait()

    def bias_rows(head, carry):
        exact = []
        for axis in range(2):
            total = jnp.zeros((GRID, slots), f32)
            for bucket in range(buckets):
                total = jnp.where(
                    offsets[axis] == bucket, rel_table[head, 0, axis * buckets + bucket], total
                )
            total = total * LOG2E
            if axis == 0:
                total = jnp.where(page_row > PAGES - 0.5, masked_fill, total)
            exact.append(total)
        exact = stack(exact)
        high = exact.astype(bf16)
        bias[head, : 2 * GRID, :] = high
        bias[head, 2 * GRID :, :] = (exact - high.astype(f32)).astype(bf16)
        return carry

    lax.fori_loop(0, heads, bias_rows, 0)

    load("wq").wait()

    @unrolled_third
    def _(part, span):
        found = dot(S["wq"][:, span], S["nt"][...], "tn")
        S["q_t"][span, :] = (found * (LOG2E * size**-0.5)).astype(bf16)

    sums_o[...] = jnp.zeros_like(sums_o)
    late_o[...] = jnp.zeros_like(late_o)
    for i in range(2):
        gather_x(i).wait()
        for k in (1, 2, 3):
            gather_z(i, k).start()

    load("cot").wait()

    @unrolled_third
    def _(part, span):
        low = W[1][span, :].astype(bf16)
        S["g2"][span, :] = low
        sums_o[4:5, :] += jnp.sum(low.astype(f32), axis=0, keepdims=True)

    for t in range(4):
        down_load(t).wait()
        if t > 1:
            act_save(t - 2).wait()

        @unrolled_third
        def _(part, span):
            W[2 + t % 2][span, :] = dot(S["g2"][span, :], S["wd"][t % 2], "nt")

        act_save(t).start()
        down_load((t + 2) % 4).start()
        if t < 2:
            for k in (1, 2, 3):
                gather_z(t, k).wait_send()
                gather_z_here(t, k).wait_recv()
            gather_y(t).start()

    for i in range(2):
        gather_y(i).wait_send()
        gather_y(i, False).wait_recv()
        gather_core(i).start()

    for i, (weight, result) in enumerate((("wk", "k_t"), ("wv", "v_t"))):
        gather_core(i).wait_send()
        gather_core(i, False).wait_recv()

        @unrolled_third
        def _(part, span):
            if i == 0:
                far_rows(part).wait()
            S[result][:, span] = dot(S[weight][...], S["ft"][:, span], "tn").astype(bf16)

    act_save(2).wait()
    act_save(3).wait()
    act_load(0).start()

    def by_page(name, rows):
        return [S[name][rows, cols] for cols in thirds]

    def masked(name, rows):
        held = S[name][rows, :]
        return [held * page_low[p] for p in range(PAGES)]

    def fold(found):
        total = found[:size] * page_rows[0]
        for p in range(1, PAGES):
            total = total + found[p * size : (p + 1) * size] * page_rows[p]
        return total

    def column(p):
        return page_col[...] == p

    def spread(rows):
        middle, last = [jnp.concatenate([column(p)] * 2, axis=1) for p in (1, 2)]
        return jnp.where(middle, rows[1], jnp.where(last, rows[2], rows[0]))

    def rows_of(head):
        return pl.ds(pl.multiple_of(head * size, size), size)

    def in_pairs(step):
        def several(i, carry):
            for j in range(TOGETHER):
                step(TOGETHER * i + j, carry)
            return carry

        lax.fori_loop(0, heads // TOGETHER, several, 0)

    def text_forward(head, carry):
        rows = rows_of(head)
        scores = dot(
            stack(by_page("k_t", rows) + [spot_twice]),
            stack(masked("q_t", rows) + [bias[head]]),
            "tn",
        )
        top = jnp.max(scores, axis=0, keepdims=True)
        weight = jnp.exp2(scores - top).astype(bf16)
        found = dot(stack(by_page("v_t", rows) + [jnp.ones((16, third), bf16)]), weight)
        total = found[PAGES * size : PAGES * size + 1]
        S["att"][rows, :] = (fold(found) * (valid_row / total)).astype(bf16)
        lse[head] = top + jnp.log2(total)
        return carry

    def vision_forward(head, carry):
        rows = rows_of(head)
        scores = dot(
            stack(masked("k_t", rows) + [bias[head]]),
            stack(by_page("q_t", rows) + [spot_twice]),
            "tn",
        )
        tops = []
        for p in range(PAGES):
            inside = jnp.concatenate([column(p)] * 2, axis=1)
            tops.append(
                jnp.max(jnp.where(inside, scores, 2.0 * masked_fill), axis=0, keepdims=True)
            )
        weight = jnp.exp2(scores - spread(tops)).astype(bf16)
        counts = [page_low[p, :1, :] for p in range(PAGES)]
        counts = stack(counts + [jnp.zeros((16 - PAGES, slots), bf16)])
        found = dot(stack(masked("v_t", rows) + [counts]), weight)
        for p, cols in enumerate(thirds):
            total = found[PAGES * size + p : PAGES * size + p + 1]
            S["att"][rows, cols] = (found[p * size : (p + 1) * size] / total).astype(bf16)
            lse[head, :, cols] = tops[p] + jnp.log2(total)
        return carry

    @pl.when(st == 0)
    def _():
        in_pairs(text_forward)

    @pl.when(st == 1)
    def _():
        in_pairs(vision_forward)

    def down_view(at):
        return at.reshape(2, 2, width // 4, width)

    def rest_view(at):
        return at.reshape(4, 2, 2, part_rows, width)

    def add_low(left, right):
        return left + right

    def core_down(t):
        at = S["sd"].at[lax.rem(t, 2)]
        return remote(down_view(at).at[:, 1 - c], cd.at[t], csem.at[t], crem.at[t], core_peer)

    def core_rest(p, at):
        return remote(
            rest_view(at).at[:, :, 1 - c], cr.at[p], csem.at[4 + p], crem.at[4 + p], core_peer
        )

    def y_down(t):
        return remote(cd.at[t, 1 - y], yd.at[t], ysem.at[t], yrem.at[t], y_peer)

    def y_rest(p):
        return remote(cr.at[p, :, 1 - y], yr.at[p], ysem.at[4 + p], yrem.at[4 + p], y_peer)

    def z_down(t):
        return remote(yd.at[t], zd.at[t], zsem.at[0, t], zrem.at[0, t], z_peers[t + 1])

    def z_rest(p, i):
        q = chunk_of(p) if p < 4 else p
        return remote(
            yr.at[p, z_at[i]], zr.at[q, i - 1], zsem.at[1 + p, i - 1], zrem.at[1 + q, i - 1], z_peers[i]
        )

    def z_here(q, i):
        return remote(
            yr.at[q, z_at[i]], zr.at[q, i - 1], zsem.at[1 + q, i - 1], zrem.at[1 + q, i - 1], z_peers[i]
        )

    def after_core_down(t):
        core_down(t).wait()
        held = down_view(S["sd"].at[lax.rem(t, 2)])

        def part(i, carry):
            rows = pl.ds(pl.multiple_of(lax.rem(i, 2) * (2 * part_rows), 16), 2 * part_rows)
            j = lax.div(i, 2)
            cd[t, j, rows] = add_low(cd[t, j, rows], held[j, c, rows])
            return carry

        lax.fori_loop(0, 4, part, 0)
        y_down(t).start()

    def after_core(p, at):
        core_rest(p, at).wait()
        held = rest_view(at)

        def part(i, carry):
            cr[p, i] = add_low(cr[p, i], held[i, :, c])
            return carry

        lax.fori_loop(0, 4, part, 0)
        y_rest(p).start()

    def after_y_down(t):
        y_down(t).wait()

        def part(i, carry):
            rows = pl.ds(pl.multiple_of(i * (2 * part_rows), 16), 2 * part_rows)
            yd[t, rows] = add_low(yd[t, rows], cd[t, y, rows])
            return carry

        lax.fori_loop(0, 2, part, 0)
        if t < 3:
            z_down(t).start()

    def after_y(p):
        y_rest(p).wait()

        def part(i, carry):
            yr[p, i] = add_low(yr[p, i], cr[p, i, y])
            return carry

        lax.fori_loop(0, 4, part, 0)
        if p < 4:
            for i in (1, 2, 3):
                z_rest(p, i).start()
        else:
            z_near(p).start()

    def z_near(p):
        held = yr.at[p].reshape(2, 2, part_rows, width)
        return remote(
            held.at[:, 1 - z_low], zr.at[p, pl.ds(0, 2)], zsem.at[1 + p, 0], zrem.at[1 + p, 0], one_peer
        )

    def z_far(p):
        return remote(
            zr.at[p, 1 - z_high], zr.at[p, 2], zsem.at[1 + p, 1], zrem.at[1 + p, 1], two_peer
        )

    def after_near(p):
        z_near(p).wait()
        for i in range(2):
            zr[p, i] = add_low(zr[p, i], yr[p, 2 * i + z_low])
        z_far(p).start()

    def end_down():
        total = yd[3].astype(f32)
        for t in range(3):
            z_down(t).wait()
            total = total + zd[t].astype(f32)
        down_o[...] = total

    def end_rest(q):
        if q > 3:
            z_far(q).wait()
            return zr[q, z_high].astype(f32) + zr[q, 2].astype(f32)
        held = lax.rem(q - z + 3, 4) if q < 4 else q
        total = yr[held, z].astype(f32)
        for i in (1, 2, 3):
            z_here(q, i).wait()
            total = total + zr[q, i - 1].astype(f32)
        return total

    def exchange(mine, found, send, recv, peers, at, start):
        for k in (1, 2, 3):
            copy = remote(mine, found.at[at[0]], send.at[k - 1], recv.at[k - 1], peers[k])
            if start:
                copy.start()
            else:
                copy.wait_send()
                there = lax.rem(at[0] + 4 - k, 4)
                remote(mine, found.at[there], send.at[k - 1], recv.at[k - 1], peers[k]).wait_recv()
        if not start:
            found[at[0]] = mine[...]
            mine[...] = ((found[0] + found[1]) + found[2]) + found[3]

    def small_sums(stage, start):
        peers, at = ((place_peers, place_at), (z_peers, z_at))[stage]
        exchange(sums_o, sums_in.at[stage], asem.at[stage], arem.at[stage], peers, at, start)

    def small_table(stage, start):
        peers, at = ((place_peers, place_at), (z_peers, z_at))[stage]
        exchange(table_o, table_in.at[stage], bsem.at[stage], brem.at[stage], peers, at, start)

    pltpu.make_async_copy(slot("nt"), nt_o, out_sem.at[2]).wait()
    load("wo").wait()

    @unrolled_third
    def _(part, span):
        middle = W[0][span, :] + dot(S["att"][:, span], S["wo"][...], "tn")
        W[0][span, :] = middle
        W[2][span, :] = middle + down_bias[...]
        W[3][span, :] = jnp.zeros((third, width), f32)
        plain, inverse = plain_norm(middle)
        S["n2"][span, :] = (plain * gains[1:2, :] + shifts[1:2, :]).astype(bf16)

    def feed(t, carry):
        two = lax.rem(t, 2)
        at = chunk_of(t)
        up_load(t).wait()
        down_load(t).wait()
        act_load(t).wait()

        @pl.when(t < 3)
        def _():
            up_load(t + 1).start()

            @pl.when(t > 0)
            def _():
                down_load(t + 1).start()

        w_u = S["wu"].at[two]
        w_d = S["wd"].at[two]

        @unrolled_third
        def _(part, cols):
            pre = dot(S["n2"][...], w_u[:, cols]) + up_bias[at, :, cols]
            square = pre * pre
            gate = jnp.tanh(pre * (GELU_IN + (GELU_IN * GELU_CUBE) * square))
            gate_half = 0.5 + 0.5 * gate
            act = (pre * gate_half).astype(bf16)
            S["act"][:, cols] = act
            S["sd"][two, cols, :] = dot(act, S["g2"][...], "tn").astype(bf16)
            slope = pre * (GELU_IN + (3.0 * GELU_IN * GELU_CUBE) * square)
            grad_act = W[1][:, cols]
            grad_pre = (grad_act * (gate_half * (1.0 + (1.0 - gate) * slope))).astype(bf16)
            S["gp"][:, cols] = grad_pre
            sums_o[pl.ds(5 + at, 1), cols] = jnp.sum(grad_pre.astype(f32), axis=0, keepdims=True)

        @pl.when(t < 3)
        def _():
            act_load(t + 1).start()

        @pl.when(t == 3)
        def _():
            load("cot").start()

        core_down(t).start()

        @unrolled_third
        def _(part, cols):
            S["sr"][two, :, cols] = dot(S["n2"][...], S["gp"][:, cols], "tn").astype(bf16)

        core_rest(t, S["sr"].at[two]).start()
        after_core_down(t)

        @pl.when(t > 0)
        def _():
            after_core(t - 1, S["sr"].at[1 - two])

        @unrolled_third
        def _(part, span):
            W[2][span, :] = W[2][span, :] + dot(S["act"][span, :], w_d[...])
            W[3][span, :] = W[3][span, :] + dot(S["gp"][span, :], w_u[...], "nt")

        @pl.when(t == 1)
        def _():
            after_y_down(0)

        @pl.when(t == 2)
        def _():
            after_y(0)

        @pl.when(t == 3)
        def _():
            after_y_down(1)

        return carry

    lax.fori_loop(0, 4, feed, 0)
    after_core(3, S["sr1"])
    load("cot").wait()

    pltpu.make_async_copy(W[2], block_o, out_sem.at[0]).start()

    @unrolled_third
    def _(part, span):
        plain, inverse = plain_norm(W[0][span, :])
        grad_two = W[3][span, :]
        sums_o[1:2, :] += jnp.sum(grad_two * plain, axis=0, keepdims=True)
        sums_o[3:4, :] += jnp.sum(grad_two, axis=0, keepdims=True)
        middle = W[1][span, :] + norm_backward(grad_two, plain, inverse, gains[1:2, :])
        W[0][span, :] = middle
        S["gm"][span, :] = middle.astype(bf16)

    load("x_again").start()
    load("wq_again").start()
    load("nt_again").start()

    @unrolled_third
    def _(part, rows):
        grad_att = (dot(S["wo"][rows, :], S["gm"][...], "nt") * valid_row).astype(bf16)
        S["go"][rows, :] = grad_att
        both = S["att"][rows, :].astype(f32) * grad_att.astype(f32)
        delta[pl.ds(4 * part, 4)] = jnp.sum(both.reshape(4, size, slots), axis=1, keepdims=True)

    after_y(1)

    def table_rows(head, found):
        for axis in range(2):
            here = found[axis * GRID : (axis + 1) * GRID]
            for bucket in range(buckets):
                kept = jnp.where(offsets[axis] == bucket, here, 0.0)
                cells[pl.ds(head * 16 + axis * buckets + bucket, 1), :] = jnp.sum(
                    kept, axis=0, keepdims=True
                )

    def text_backward(head, carry):
        rows = rows_of(head)
        keys = by_page("k_t", rows)
        queries = masked("q_t", rows)
        grads = stack(masked("go", rows))
        scores = dot(stack(keys + [spot_twice]), stack(queries + [bias[head]]), "tn")
        prob = jnp.exp2(scores - lse[head])
        grad_prob = dot(stack(by_page("v_t", rows)), grads, "tn")
        grad_score = (prob * (grad_prob - delta[head])).astype(bf16)
        found = dot(grads, prob.astype(bf16), "nt")
        for p, cols in enumerate(thirds):
            S["dv"][rows, cols] = found[p * size : (p + 1) * size].astype(bf16)
        found = dot(stack(queries), grad_score, "nt") * LN2
        for p, cols in enumerate(thirds):
            S["dk"][rows, cols] = found[p * size : (p + 1) * size].astype(bf16)
        found = dot(stack(keys + [spot_once]), grad_score)
        S["dq"][rows, :] = (fold(found) * size**-0.5).astype(bf16)
        table_rows(head, found[PAGES * size :])
        return carry

    def vision_backward(head, carry):
        rows = rows_of(head)
        keys = masked("k_t", rows)
        queries = by_page("q_t", rows)
        grads = stack(by_page("go", rows))
        scores = dot(stack(keys + [bias[head]]), stack(queries + [spot_twice]), "tn")
        prob = jnp.exp2(scores - spread([lse[head, :, cols] for cols in thirds]))
        grad_prob = dot(stack(masked("v_t", rows)), grads, "tn")
        inner = spread([delta[head, :, cols] for cols in thirds])
        grad_score = (prob * (grad_prob - inner)).astype(bf16)
        S["dv"][rows, :] = fold(dot(grads, prob.astype(bf16), "nt")).astype(bf16)
        found = dot(stack(queries + [spot_once]), grad_score, "nt")
        S["dk"][rows, :] = (fold(found) * LN2).astype(bf16)
        table_rows(head, found[PAGES * size :])
        found = dot(stack(keys), grad_score) * size**-0.5
        for p, cols in enumerate(thirds):
            S["dq"][rows, cols] = found[p * size : (p + 1) * size].astype(bf16)
        return carry

    cells[...] = jnp.zeros_like(cells)

    @pl.when(st == 0)
    def _():
        in_pairs(text_backward)

    @pl.when(st == 1)
    def _():
        in_pairs(vision_backward)

    after_y_down(2)

    load("x_again").wait()
    base = heads * 16
    cells[base + 2 : base + 3, :] = valid_row

    @unrolled_third
    def _(part, span):
        block = W[2][span, :]
        own = jnp.maximum(side, jnp.where(page_col[span, 0:1] < PAGES - 0.5, 1.0, 0.0))
        sub = block - W[3][span, :]
        cells[base : base + 1, :] += jnp.sum(own * block * block, axis=0, keepdims=True)
        cells[base + 1 : base + 2, :] += jnp.sum(own * sub * sub, axis=0, keepdims=True)

    table_o[...] = lax.dot_general(
        jnp.ones((8, width), f32),
        cells[...],
        (((1,), (1,)), ((), ())),
        preferred_element_type=f32,
        precision=lax.Precision.HIGHEST,
    )

    small_sums(0, True)
    small_table(0, True)

    def back_rows(part):
        return remote(
            slot("send").at[:, span_of(part)],
            slot("back").at[:, span_of(part)],
            xsem.at[3 + part],
            xrem.at[3 + part],
            x_peer,
        )

    @unrolled_third
    def _(part, cols):
        S["send"][:, cols] = (
            dot(S["wk"][...], S["dk"][:, cols])
            + dot(S["wv"][...], S["dv"][:, cols])
        ).astype(bf16)
        back_rows(part).start()


    @unrolled_third
    def _(part, span):
        S["sk"][span, :] = dot(S["ft"][span, :], S["dk"][...], "nt").astype(bf16)

    core_rest(5, S["sk"]).start()
    after_y(2)

    @unrolled_third
    def _(part, span):
        S["sv"][span, :] = dot(S["ft"][span, :], S["dv"][...], "nt").astype(bf16)

    core_rest(6, S["sv"]).start()
    after_core(5, S["sk"])

    @unrolled_third
    def _(part, span):
        S["so"][span, :] = dot(S["att"][span, :], S["gm"][...]).astype(bf16)

    core_rest(4, S["so"]).start()
    after_core(6, S["sv"])
    load("nt_again").wait()

    @unrolled_third
    def _(part, span):
        S["sq"][span, :] = dot(S["nt_again"][span, :], S["dq"][...], "nt").astype(bf16)

    core_rest(7, S["sq"]).start()
    after_core(4, S["so"])
    load("wq_again").wait()

    @unrolled_third
    def _(part, span):
        W[1][span, :] = dot(S["wq_again"][span, :], S["dq"][...])

    after_core(7, S["sq"])
    after_y_down(3)

    def last_small(stage, start):
        peers, at = ((place_peers, place_at), (z_peers, z_at))[stage]
        exchange(late_o, late_in.at[stage], lsem.at[stage], lrem.at[stage], peers, at, start)

    table_swap = remote(table_o, table_far, tsem, trem, x_peer)

    def hop_copy(i):
        return remote(hop.at[i], hop_in.at[i], hsem.at[i], hrem.at[i], x_peer)

    after_y(3)
    pltpu.make_async_copy(W[2], block_o, out_sem.at[0]).wait()

    @each_third
    def _(part, span):
        back_rows(part).wait()
        grad_one = (W[1][:, span] + S["back"][:, span].astype(f32)).T
        plain, inverse = plain_norm(W[3][span, :])
        late_o[0:1, :] += jnp.sum(grad_one * plain, axis=0, keepdims=True)
        late_o[1:2, :] += jnp.sum(grad_one, axis=0, keepdims=True)
        W[2][span, :] = W[0][span, :] + norm_backward(
            grad_one, plain, inverse, gains[0:1, :]
        )

        @pl.when(part == 0)
        def _():
            small_sums(0, False)
            small_sums(1, True)
            small_table(0, False)
            small_table(1, True)

        @pl.when(part == 1)
        def _():
            after_y(5)

    pltpu.make_async_copy(W[2], grad_o, out_sem.at[1]).start()
    last_small(0, True)
    after_near(5)
    after_y(6)
    end_down()
    for q in range(4):
        up_o[:, q * width : (q + 1) * width] = end_rest(q)
    after_y(4)
    after_near(6)
    small_sums(1, False)
    small_table(1, False)
    table_swap.start()
    hop[0] = end_rest(5).astype(bf16)
    hop_copy(0).start()
    last_small(0, False)
    last_small(1, True)
    after_near(4)
    after_y(7)
    hop[1] = end_rest(6).astype(bf16)
    hop_copy(1).start()
    wo_o[...] = end_rest(4)
    after_near(7)
    last_small(1, False)
    wq_o[...] = end_rest(7)
    table_swap.wait()
    lane = lax.broadcasted_iota(jnp.int32, table_o.shape, 1)
    table_o[...] = table_o[...] + jnp.where(lane >= base, table_far[...], 0.0)
    for i in range(2):
        hop_copy(i).wait()
        hop_o[i] = hop_in[i].astype(f32)
    pltpu.make_async_copy(W[2], grad_o, out_sem.at[1]).wait()


def hand_over(
    block, grad_in, down, up, out, query, hop, sums, late, table,
    block_o, grad_o, gains_o, shifts_o, query_o, key_o, value_o, out_o, up_o, up_bias_o, down_o, down_bias_o, table_o, stats_o,
    held, down_h, up_h, out_h, query_h, hop_h, sums_h, late_h, table_h, in_sem, out_sem, sem,
):
    slots, width = block.shape
    step = slots // 4
    moves = []
    for i, (source, target) in enumerate(((block, block_o), (grad_in, grad_o))):
        for j in range(4):
            span = pl.ds(j * step, step)
            moves.append(
                (
                    pltpu.make_async_copy(
                        source.at[span, :], held.at[i, span, :], in_sem.at[i, j]
                    ),
                    pltpu.make_async_copy(
                        held.at[i, span, :], target.at[span, :], out_sem.at[i, j]
                    ),
                )
            )
    for i, (source, kept, target) in enumerate(((down, down_h, down_o), (up, up_h, up_o))):
        moves.append(
            (
                pltpu.make_async_copy(source, kept, sem.at[i]),
                pltpu.make_async_copy(kept, target, sem.at[i + 8]),
            )
        )
    small = ((out, out_h), (query, query_h), (hop, hop_h), (sums, sums_h), (late, late_h), (table, table_h))
    small = [pltpu.make_async_copy(*pair, sem.at[i + 2]) for i, pair in enumerate(small)]
    for copy in small:
        copy.start()
    for move in moves:
        move[0].start()
    for copy in small:
        copy.wait()
    gains_o[0:1, :] = late_h[0:1, :]
    gains_o[1:2, :] = sums_h[1:2, :]
    shifts_o[0:1, :] = late_h[1:2, :]
    shifts_o[1:2, :] = sums_h[3:4, :]
    down_bias_o[...] = sums_h[4:5, :]
    for q in range(4):
        up_bias_o[:, q * width : (q + 1) * width] = sums_h[5 + q : 6 + q, :]
    query_o[...] = query_h[...]
    key_o[...] = hop_h[0]
    value_o[...] = hop_h[1]
    out_o[...] = out_h[...]
    heads, _, rows = table_o.shape
    for head in range(heads):
        table_o[head] = table_h[0:1, head * 16 : head * 16 + rows]
    total = table_h[0:1, heads * 16 : heads * 16 + 2]
    count = table_h[0:1, heads * 16 + 2 : heads * 16 + 3]
    stats_o[...] = jnp.sqrt(total / (count * width))
    for move in moves:
        move[0].wait()
        move[1].start()
    for move in moves:
        move[1].wait()


def on_device(
    inputs,
    text_pages,
    text_boxes,
    norm_gains,
    norm_shifts,
    w_query,
    w_key,
    w_value,
    w_out,
    w_up,
    up_bias,
    w_down,
    down_bias,
    box_table,
    cotangent,
):
    slots, width = inputs.shape[2:]
    rel_rows, heads = box_table.shape[1:]
    size = width // heads
    part = width // 16
    shape = lambda *dims: jax.ShapeDtypeStruct(dims, f32)
    vmem = pl.BlockSpec(memory_space=pltpu.VMEM)
    hbm = pl.BlockSpec(memory_space=pl.ANY)
    dma = pltpu.SemaphoreType.DMA
    cell_rows = heads * 16 + 16
    low = lambda *dims: pltpu.VMEM(dims, bf16)
    full = lambda *dims: pltpu.VMEM(dims, f32)
    block, grad_in, _, _, down, up, out, query, hop, sums, late, table = pl.pallas_call(
        layer_kernel,
        out_shape=[
            shape(slots, width),
            shape(slots, width),
            jax.ShapeDtypeStruct((width, slots), bf16),
            shape(4, slots, width),
            shape(4 * part, width),
            shape(part, 4 * width),
            shape(part, width),
            shape(part, width),
            shape(2, part, width),
            shape(16, width),
            shape(8, width),
            shape(8, cell_rows),
        ],
        in_specs=[hbm] * 8 + [vmem] * 6 + [hbm],
        out_specs=[hbm] * 4 + [vmem] * 8,
        scratch_shapes=[
            [low(slots, width)] * (len(NAMES) - RINGS) + [low(2, slots, width)] * RINGS,
            [full(slots, width)] * 4,
            pltpu.SMEM((heads, 1, rel_rows), f32),
            low(heads, 4 * GRID, slots),
            full(heads, 1, slots),
            full(heads, 1, slots),
            low(PAGES, size, slots),
            full(slots, 128),
            full(cell_rows, width),
            low(4, 2, 4 * part, width),
            low(8, 4, 2, part, width),
            low(4, 4 * part, width),
            low(8, 4, part, width),
            low(3, 4 * part, width),
            low(8, 3, part, width),
            low(2, part, width),
            low(2, part, width),
            full(2, 4, 16, width),
            full(2, 4, 8, width),
            full(2, 4, 8, cell_rows),
            full(8, cell_rows),
            dma((7,)),
            dma((4, 3)),
            dma((3,)),
            dma((12,)),
            dma((12,)),
            dma((12,)),
            dma((12,)),
            dma((9, 3)),
            dma((9, 3)),
            dma((6,)),
            dma((6,)),
            dma((2,)),
            dma((2,)),
            dma((2, 3)),
            dma((2, 3)),
            dma((2, 3)),
            dma((2, 3)),
            dma((2, 3)),
            dma((2, 3)),
            dma,
            dma,
            dma((2,)),
            dma((2,)),
            dma((2, 3)),
            dma((2, 3)),
            dma((2,)),
            dma((2,)),
            dma((2,)),
            dma((2,)),
        ],
        compiler_params=pltpu.CompilerParams(
            collective_id=0, has_side_effects=True, vmem_limit_bytes=61 * 2**20
        ),
        name="layer",
    )(
        inputs[0, 0],
        cotangent[0, 0],
        w_query[0],
        w_key[0],
        w_value[0],
        w_out[0],
        w_up[0],
        w_down[0],
        up_bias.reshape(4, 1, width),
        down_bias,
        norm_gains[0],
        norm_shifts[0],
        text_pages,
        text_boxes[0],
        box_table.transpose(2, 0, 1),
    )
    outs = pl.pallas_call(
        hand_over,
        out_shape=[
            shape(slots, width),
            shape(slots, width),
            shape(2, width),
            shape(2, width),
            shape(part, width),
            shape(part, width),
            shape(part, width),
            shape(part, width),
            shape(part, 4 * width),
            shape(1, 4 * width),
            shape(4 * part, width),
            shape(1, width),
            shape(heads, 1, rel_rows),
            shape(1, 2),
        ],
        in_specs=[hbm] * 10,
        out_specs=[hbm] * 2 + [vmem] * 6 + [hbm, vmem, hbm] + [vmem] * 3,
        scratch_shapes=[
            full(2, slots, width),
            full(4 * part, width),
            full(part, 4 * width),
            full(part, width),
            full(part, width),
            full(2, part, width),
            full(16, width),
            full(8, width),
            full(8, cell_rows),
            dma((2, 4)),
            dma((2, 4)),
            dma((10,)),
        ],
        compiler_params=pltpu.CompilerParams(vmem_limit_bytes=61 * 2**20),
        name="hand_over",
    )(block, grad_in, down, up, out, query, hop, sums, late, table)
    block, grad_in, gains, shifts, query, key, value, out, up, up_b, down, down_b, table, stats = outs
    return (
        block[None, None],
        grad_in[None, None],
        gains[None],
        shifts[None],
        query[None],
        key[None],
        value[None],
        out[None],
        up[None],
        up_b,
        down[None],
        down_b,
        table.transpose(1, 2, 0),
        stats[0],
    )


def partner(block, axis, bit):
    count = lax.axis_size(axis)
    route = []
    for low in range(count):
        high = low | 1 << bit
        if high != low and high < count:
            route += [(low, high), (high, low)]
    return lax.ppermute(block, axis, route)


def norm_forward(values, gain_row, shift_row):
    center = values - jnp.mean(values, axis=-1, keepdims=True)
    inverse = lax.rsqrt(jnp.mean(center * center, axis=-1, keepdims=True) + 1e-05)
    normal_part = center * inverse
    return (normal_part * gain_row + shift_row, normal_part, inverse)


def general_norm_backward(grad_normed, normal_part, inverse, gain_row):
    scaled = grad_normed * gain_row
    first_mean = jnp.mean(scaled, axis=-1, keepdims=True)
    second_mean = jnp.mean(scaled * normal_part, axis=-1, keepdims=True)
    return inverse * (scaled - first_mean - normal_part * second_mean)


def bucket_offset(own_coord, far_coord, bucket_count):
    radius = (bucket_count - 1) // 2
    return jnp.clip(own_coord[:, None] - far_coord[None, :], -radius, radius) + radius


def bias_from(rel_table, offset):
    result = jnp.zeros((rel_table.shape[1],) + offset.shape, f32)
    for bucket in range(rel_table.shape[0]):
        result = (
            result + rel_table[bucket][:, None, None] * (offset == bucket).astype(f32)[None]
        )
    return result


def bias_grad(grad_wide, offset, bucket_count):
    return jnp.stack(
        [
            jnp.sum(grad_wide * (offset == bucket).astype(f32)[None], axis=(1, 2))
            for bucket in range(bucket_count)
        ]
    )


def project(left, right):
    return jnp.einsum("rsd,de->rse", left, right, preferred_element_type=f32)


def weight_grad(left, right):
    return jnp.einsum("rsd,rse->de", left, right, preferred_element_type=f32)


def back_project(grad_low, weight):
    return jnp.einsum("rse,de->rsd", grad_low, weight, preferred_element_type=f32)


def general_device(
    inputs,
    text_pages,
    text_boxes,
    norm_gains,
    norm_shifts,
    w_query,
    w_key,
    w_value,
    w_out,
    w_up,
    up_bias,
    w_down,
    down_bias,
    box_table,
    cotangent,
):
    slot_count = inputs.shape[2]
    model_width = inputs.shape[3]
    head_count = box_table.shape[2]
    head_size = model_width // head_count
    bucket_count = box_table.shape[1] // 2
    score_scale = head_size ** (-0.5)
    is_text = lax.axis_index("stream") == 0
    positions = jnp.arange(slot_count, dtype=jnp.int32)
    cell_index = positions % (GRID * GRID)
    vision_page = positions // (GRID * GRID)
    vision_first = cell_index % GRID
    vision_second = cell_index // GRID
    own_valid = jnp.where(is_text, text_pages < PAGES, True).astype(f32)
    gain_rows = norm_gains[0]
    shift_rows = norm_shifts[0]
    rel_table = box_table[0]
    block_in = inputs[:, 0]
    normed_one, plain_one, inverse_one = norm_forward(block_in, gain_rows[0], shift_rows[0])
    normed_low = normed_one.astype(bf16)
    query = project(normed_low, w_query[0]).astype(bf16)
    own_keys = project(normed_low, w_key[0]).astype(bf16)
    own_values = project(normed_low, w_value[0]).astype(bf16)
    far_keys, far_values = partner((own_keys, own_values), "stream", 0)

    def geometry(row_index):
        text_page = text_pages[row_index]
        own_page = jnp.where(is_text, text_page, vision_page)
        far_page = jnp.where(is_text, vision_page, text_page)
        own_first = jnp.where(is_text, text_boxes[row_index, 0], vision_first)
        far_first = jnp.where(is_text, vision_first, text_boxes[row_index, 0])
        own_second = jnp.where(is_text, text_boxes[row_index, 1], vision_second)
        far_second = jnp.where(is_text, vision_second, text_boxes[row_index, 1])
        allowed = (own_page[:, None] == far_page[None, :]) | (own_page[:, None] == PAGES)
        return (
            allowed,
            bucket_offset(own_first, far_first, bucket_count),
            bucket_offset(own_second, far_second, bucket_count),
        )

    def heads_of(matrix):
        return matrix.reshape(slot_count, head_count, head_size)

    def score_block(row_index, allowed, offset_first, offset_second):
        raw = (
            jnp.einsum(
                "ihd,jhd->hij",
                heads_of(query[row_index]),
                heads_of(far_keys[row_index]),
                preferred_element_type=f32,
            )
            * score_scale
        )
        raw = (
            raw
            + bias_from(rel_table[:bucket_count], offset_first)
            + bias_from(rel_table[bucket_count:], offset_second)
        )
        return jnp.where(allowed[None], raw, masked_fill)

    row_index = 0
    allowed, offset_first, offset_second = geometry(row_index)
    masked = score_block(row_index, allowed, offset_first, offset_second)
    top_score = jnp.max(masked, axis=-1, keepdims=True)
    exp_scores = jnp.exp(masked - top_score)
    row_total = jnp.sum(exp_scores, axis=-1, keepdims=True)
    prob_low = (exp_scores / row_total).astype(bf16)
    attended = jnp.einsum(
        "hij,jhd->ihd",
        prob_low,
        heads_of(far_values[row_index]),
        preferred_element_type=f32,
    ).reshape(slot_count, model_width)
    attended_rows = [(attended * own_valid[row_index][:, None]).astype(bf16)]
    log_totals = [top_score + jnp.log(row_total)]
    attended_low = jnp.stack(attended_rows)
    branch_one = project(attended_low, w_out[0])
    middle = block_in + branch_one
    normed_two, plain_two, inverse_two = norm_forward(middle, gain_rows[1], shift_rows[1])
    normed_two_low = normed_two.astype(bf16)
    pre_act = project(normed_two_low, w_up[0]) + up_bias[0]
    act_low = jax.nn.gelu(pre_act).astype(bf16)
    branch_two = project(act_low, w_down[0]) + down_bias[0]
    block_out = middle + branch_two
    sublayer = branch_one + branch_two
    totals = lax.psum(
        (
            jnp.sum(own_valid * jnp.sum(block_out * block_out, axis=-1)),
            jnp.sum(own_valid * jnp.sum(sublayer * sublayer, axis=-1)),
            jnp.sum(own_valid),
        ),
        ("stream", "batch"),
    )
    denominator = totals[2] * model_width
    stats = jnp.stack([jnp.sqrt(totals[0] / denominator), jnp.sqrt(totals[1] / denominator)])
    grad_out = cotangent[:, 0]
    grad_out_low = grad_out.astype(bf16)
    grad_w_down = weight_grad(act_low, grad_out_low)
    grad_down_bias = jnp.sum(grad_out_low.astype(f32), axis=(0, 1))
    grad_act = back_project(grad_out_low, w_down[0])
    gelu_back = jax.vjp(jax.nn.gelu, pre_act)[1]
    grad_pre_low = gelu_back(grad_act)[0].astype(bf16)
    grad_w_up = weight_grad(normed_two_low, grad_pre_low)
    grad_up_bias = jnp.sum(grad_pre_low.astype(f32), axis=(0, 1))
    grad_normed_two = back_project(grad_pre_low, w_up[0])
    grad_gain_two = jnp.sum(grad_normed_two * plain_two, axis=(0, 1))
    grad_shift_two = jnp.sum(grad_normed_two, axis=(0, 1))
    grad_middle = grad_out + general_norm_backward(grad_normed_two, plain_two, inverse_two, gain_rows[1])
    grad_middle_low = grad_middle.astype(bf16)
    grad_w_out = weight_grad(attended_low, grad_middle_low)
    grad_attended = back_project(grad_middle_low, w_out[0]).astype(bf16) * own_valid[
        :, :, None
    ].astype(bf16)
    query_grad_rows, key_grad_rows, value_grad_rows = ([], [], [])
    row_index = 0
    allowed, offset_first, offset_second = geometry(row_index)
    masked = score_block(row_index, allowed, offset_first, offset_second)
    prob = jnp.exp(masked - log_totals[row_index])
    grad_heads = heads_of(grad_attended[row_index])
    grad_prob = jnp.einsum(
        "ihd,jhd->hij",
        grad_heads,
        heads_of(far_values[row_index]),
        preferred_element_type=f32,
    )
    inner_sum = jnp.sum(prob * grad_prob, axis=-1, keepdims=True)
    grad_score_low = (prob * (grad_prob - inner_sum)).astype(bf16)
    grad_score_wide = grad_score_low.astype(f32)
    grad_table = jnp.concatenate(
        [
            bias_grad(grad_score_wide, offset_first, bucket_count),
            bias_grad(grad_score_wide, offset_second, bucket_count),
        ],
        axis=0,
    )
    query_grad = (
        jnp.einsum(
            "hij,jhd->ihd",
            grad_score_low,
            heads_of(far_keys[row_index]),
            preferred_element_type=f32,
        )
        * score_scale
    )
    key_grad = (
        jnp.einsum(
            "hij,ihd->jhd",
            grad_score_low,
            heads_of(query[row_index]),
            preferred_element_type=f32,
        )
        * score_scale
    )
    value_grad = jnp.einsum(
        "hij,ihd->jhd", prob.astype(bf16), grad_heads, preferred_element_type=f32
    )
    query_grad_rows.append(query_grad.reshape(slot_count, model_width).astype(bf16))
    key_grad_rows.append(key_grad.reshape(slot_count, model_width).astype(bf16))
    value_grad_rows.append(value_grad.reshape(slot_count, model_width).astype(bf16))
    grad_query_low = jnp.stack(query_grad_rows)
    own_key_grad, own_value_grad = partner(
        (jnp.stack(key_grad_rows), jnp.stack(value_grad_rows)), "stream", 0
    )
    grad_w_query = weight_grad(normed_low, grad_query_low)
    grad_w_key = weight_grad(normed_low, own_key_grad)
    grad_w_value = weight_grad(normed_low, own_value_grad)
    grad_normed_one = (
        back_project(grad_query_low, w_query[0])
        + back_project(own_key_grad, w_key[0])
        + back_project(own_value_grad, w_value[0])
    )
    grad_gain_one = jnp.sum(grad_normed_one * plain_one, axis=(0, 1))
    grad_shift_one = jnp.sum(grad_normed_one, axis=(0, 1))
    grad_inputs = grad_middle + general_norm_backward(grad_normed_one, plain_one, inverse_one, gain_rows[0])
    big_sums = (
        lax.psum_scatter(grad_w_query, "batch", scatter_dimension=0, tiled=True),
        lax.psum_scatter(grad_w_key, "batch", scatter_dimension=0, tiled=True),
        lax.psum_scatter(grad_w_value, "batch", scatter_dimension=0, tiled=True),
        lax.psum_scatter(grad_w_out, "batch", scatter_dimension=0, tiled=True),
        lax.psum_scatter(grad_w_up, "batch", scatter_dimension=0, tiled=True),
        lax.psum_scatter(grad_w_down, "batch", scatter_dimension=0, tiled=True),
    )
    small_sums = lax.psum(
        (
            jnp.stack([grad_gain_one, grad_gain_two]),
            jnp.stack([grad_shift_one, grad_shift_two]),
            grad_up_bias,
            grad_down_bias,
            grad_table,
        ),
        "batch",
    )
    return (
        block_out[:, None],
        grad_inputs[:, None],
        small_sums[0][None],
        small_sums[1][None],
        big_sums[0][None],
        big_sums[1][None],
        big_sums[2][None],
        big_sums[3][None],
        big_sums[4][None],
        small_sums[2][None],
        big_sums[5][None],
        small_sums[3][None],
        small_sums[4][None],
        stats,
    )


def solution(mesh):
    sided = lambda dims: P("stream", *([None] * (dims - 1)))
    rows = P("batch", "stream", None, None)
    shard = P("stream", "batch", None)
    placed = (
        (rows, P("batch", None), P("batch", None, None), sided(3), sided(3))
        + (sided(3),) * 5
        + (sided(2), sided(3), sided(2), sided(3), rows)
    )
    fits = mesh.shape["batch"] == 16 and mesh.shape["stream"] == 2
    return jax.shard_map(
        on_device if fits else general_device,
        mesh=mesh,
        in_specs=placed,
        out_specs=(
            (rows, rows, sided(3), sided(3))
            + (shard,) * 5
            + (sided(2), shard, sided(2), sided(3), P())
        ),
        check_vma=False,
    )
```
